32 devices in a mesh: group: 2 (over x), wide: 8 (over z, y), narrow: 2 (over core).
Axes of the slice: x: 2, y: 2, z: 4, core: 2. Of those that a mesh axis runs over, the one named last changes fastest.
Arguments:
- voxels: bfloat16 [65536, 512], P(('group', 'wide', 'narrow')), parts along dimension 0, may hold values from -6 to 6
- w_qkv: bfloat16 [512, 1536], replicated, may hold values from -0.25 to 0.25
- w_out: bfloat16 [512, 512], replicated, may hold values from -0.25 to 0.25
- w_feature: bfloat16 [512, 256], replicated, may hold values from -0.25 to 0.25
- conv_first: bfloat16 [3, 3, 256, 256], replicated, may hold values from -0.125 to 0.125
- conv_second: bfloat16 [3, 3, 256, 256], replicated, may hold values from -0.125 to 0.125
- row_brick: int32 [512, 1], P(('group', 'wide', 'narrow')), parts along dimension 0, may hold values from 0 to 7; in each aligned block of 16 rows (0 to 15, 16 to 31, ...) at most 4 rows name the same one
- cell_place: int32 [65536], P(('group', 'wide', 'narrow')), parts along dimension 0, may hold values from 0 to 255
Outputs:
- flow_field: float32 [128, 64, 256], P(('group', 'wide'), 'narrow'), parts along dimension 0
The draws below stay inside these ranges and needn't reach their ends.
There are 2 independent parts, one for each index of `group`. The reference program is written for one: setup_inputs(seed, part) draws one part's arguments, and reference() takes and returns one part's arrays. A program takes and returns all parts, laid end to end along the dimension named above; an argument that names none is the same for every part. Nothing has to cross between parts.
Inputs may be any that keep to these rules, and one draw needn't show every extreme that they name: `row_brick`: within the rows of one device (16 rows in a row), no brick row is named more than 4 times, and some brick row exactly 4 times.
All inputs are finite; a program needn't handle non-finite values.
Results may differ from the reference program's by a relative error of at most 0.014.
Values may be sent and summed in bfloat16 or wider, within the bound.
No kernel may reach another device: no remote copies, remote signals or barrier semaphores. Data moves between devices by JAX's collectives and lax.ppermute only.
A program may use at most 128 MiB of HBM per device.

```python
import math
import jax
import jax.numpy as jnp
import numpy as np
from jax import lax

D = 512
HEADS = 4
HEAD = 128
PF = 256
ROW = 128
BLK = 256
TOK_DEV = 2048
BX = 8
BY = 32
MOST = 4
TOKENS = 32768
ROWS = 256
N_WIDE = 8
N_NARROW = 2


def touch_ends(entries, rng, smallest, largest):
    extent = entries.shape
    spot = [jax.random.randint(jax.random.fold_in(rng, axis), (), 0, extent[axis]) for axis in range(len(extent))]
    entries = entries.at[tuple(spot)].set(smallest)
    longest = extent.index(max(extent))
    spot[longest] = (spot[longest] + 1) % extent[longest]
    return entries.at[tuple(spot)].set(largest)


def block_scale(key, dims, split, low, largest):
    factor_of, own = 1.0, jax.random.fold_in(key, 6)
    for position, parts in split:
        draws = jnp.exp(jax.random.uniform(jax.random.fold_in(own, position), (parts,), jnp.float32, low / len(split), largest / len(split)))
        factor_of = factor_of * jnp.repeat(draws, dims[position] // parts).reshape([-1 if axis == position else 1 for axis in range(len(dims))])
    return factor_of


def routed_block(stream_key, own, number, rows, count, top, reach, lean):
    sequence = jax.random.permutation(stream_key, count)
    packed, usual = load_shares(count, rows * top, reach, lean, True), load_shares(count, rows * top, reach, lean, False)
    places = jnp.arange(count)

    def named(sizes, offset_by):
        used = int((sizes > 0).sum())
        fixed = max(1, used // 4)
        passed = fixed + (places - fixed + offset_by * (used - fixed)) % max(1, count - fixed)
        return jnp.zeros((count,), jnp.int32).at[sequence[jnp.where(places < fixed, places, passed)]].set(jnp.asarray(sizes, jnp.int32))

    sizes = jnp.where(number % 4 == 0, named(packed, number // 4), named(usual, number - number // 4 - 1))
    mixed = jax.random.permutation(jax.random.fold_in(own, 3), count)
    donor, sink = mixed[0:count // 2 * 2:2], mixed[1:count // 2 * 2:2]
    margin = jnp.minimum(sizes[donor] - 1, reach - sizes[sink]) // 2
    margin = jnp.where((donor == sequence[0]) | (sink == sequence[0]) | (sizes[sink] == 0), 0, jnp.maximum(margin, 0))
    passed = jax.random.randint(jax.random.fold_in(own, 4), (count // 2,), 0, 1 << 20) % (margin + 1)
    sizes = sizes.at[donor].add(-passed).at[sink].add(passed)
    members = jnp.searchsorted(jnp.cumsum(sizes), jnp.arange(rows * top), side="right").astype(jnp.int32)
    grid = members.reshape(top, rows).T
    grid = grid[jax.random.permutation(jax.random.fold_in(own, 1), rows)]
    offset_by = jax.random.randint(jax.random.fold_in(own, 2), (rows, 1), 0, top)
    return jnp.take_along_axis(grid, (jnp.arange(top)[None, :] + offset_by) % top, axis=1)


def load_shares(count, total, limit, lean, full):
    weights = [(1 << 20) // math.isqrt(rank ** lean) + 1 for rank in range(1, count + 1)]
    largest = limit if full else min(limit, max(-(-total // count), total * weights[0] // sum(weights)))
    least = 1 if total - largest >= count - 1 else 0
    holding, spare = [largest] + [least] * (count - 1), total - largest - least * (count - 1)
    while spare > 0:
        free = [i for i in range(1, count) if holding[i] < largest] or [i for i in range(1, count) if holding[i] < limit]
        mass, left = sum([weights[i] for i in free]), spare
        for i in free:
            more = min(limit - holding[i], max(1, left * weights[i] // mass), spare)
            holding[i] = holding[i] + more
            spare = spare - more
    return np.array(holding)


def bell_draw(own_key, extent, scale, reach, split=(), held_as=jnp.bfloat16):
    result = jax.random.normal(own_key, extent, jnp.float32) * scale
    if len(split) > 0:
        result = block_scale(own_key, extent, split, -0.22, 0.18) * result
    return jnp.clip(result, min=-reach, max=reach).astype(held_as)


def setup_inputs(seed: int = 0, part: int = 0) -> dict:
    splits = jax.random.split(jax.random.key(seed), 9)
    part_splits = jax.random.split(jax.random.fold_in(splits[8], part), 9)
    voxels = bell_draw(part_splits[0], (TOKENS, D), 1.0, 6.0, ((0, 16),))
    w_qkv = bell_draw(splits[1], (D, 3 * D), D ** -0.5, 0.25)
    w_out = bell_draw(splits[2], (D, D), D ** -0.5, 0.25)
    w_feature = bell_draw(splits[3], (D, PF), D ** -0.5, 0.25)
    conv_first = bell_draw(splits[4], (3, 3, PF, PF), (9 * PF) ** -0.5, 0.125)
    conv_second = bell_draw(splits[5], (3, 3, PF, PF), (9 * PF) ** -0.5, 0.125)
    row_brick_keys = jax.random.split(jax.random.fold_in(part_splits[6], 1), ROWS // (TOK_DEV // ROW))
    row_brick_turns = jax.random.permutation(jax.random.fold_in(part_splits[6], 3), ROWS // (TOK_DEV // ROW))
    row_brick = jax.vmap(lambda own, number: routed_block(jax.random.fold_in(part_splits[6], 2), own, number, TOK_DEV // ROW, N_WIDE, 1, MOST, 2))(row_brick_keys, row_brick_turns).reshape((ROWS, 1))
    cell_place = touch_ends(jax.random.randint(part_splits[7], (TOKENS,), 0, BX * BY), jax.random.fold_in(part_splits[7], 1), 0, (BX * BY) - 1).astype(jnp.int32)
    return {"voxels": voxels, "w_qkv": w_qkv, "w_out": w_out, "w_feature": w_feature, "conv_first": conv_first, "conv_second": conv_second, "row_brick": row_brick, "cell_place": cell_place}


epsilon = 1e-06
layout_names = ('NHWC', 'HWIO', 'NHWC')

def convolve_same(field, weight):
    return lax.conv_general_dilated(field[None], weight, (1, 1), 'SAME', dimension_numbers=layout_names, preferred_element_type=jnp.float32)[0]

def reference(voxels, w_qkv, w_out, w_feature, conv_first, conv_second, row_brick, cell_place):
    projected = jnp.dot(voxels, w_qkv, preferred_element_type=jnp.float32).astype(jnp.bfloat16)
    block_count = TOKENS // BLK
    split_rows = projected.reshape(block_count, BLK, 3, HEADS, HEAD)
    query_rows = split_rows[:, :, 0]
    key_rows = split_rows[:, :, 1]
    value_rows = split_rows[:, :, 2]
    causal_mask = jnp.arange(BLK)[:, None] >= jnp.arange(BLK)[None, :]

    def advance(carry_state, block):
        query_block, key_block, value_block = block
        query_wide = query_block.astype(jnp.float32)
        key_wide = key_block.astype(jnp.float32)
        value_wide = value_block.astype(jnp.float32)
        carried = jnp.einsum('thd,hde->the', query_wide, carry_state, precision=lax.Precision.HIGHEST)
        scores = jnp.einsum('thd,shd->hts', query_wide, key_wide)
        scores = jnp.where(causal_mask[None], scores, 0.0).astype(jnp.bfloat16)
        local_part = jnp.einsum('hts,she->the', scores.astype(jnp.float32), value_wide)
        carry_state = carry_state + jnp.einsum('shd,she->hde', key_wide, value_wide)
        return (carry_state, carried + local_part)
    start_state = jnp.zeros((HEADS, HEAD, HEAD), jnp.float32)
    final_state, attended = lax.scan(advance, start_state, (query_rows, key_rows, value_rows))
    attended = attended.reshape(TOKENS, HEADS, HEAD)
    mean_square = lax.optimization_barrier(jnp.mean(attended * attended, axis=-1, keepdims=True))
    normed = (attended * lax.rsqrt(mean_square + epsilon)).astype(jnp.bfloat16).reshape(TOKENS, D)
    hidden = (voxels.astype(jnp.float32) + jnp.dot(normed, w_out, preferred_element_type=jnp.float32)).astype(jnp.bfloat16)
    features = jnp.dot(hidden, w_feature, preferred_element_type=jnp.float32).astype(jnp.bfloat16)
    row_index = jnp.arange(TOKENS, dtype=jnp.int32) // ROW
    column_brick = row_index // (TOK_DEV // ROW) % N_NARROW
    brick_index = row_brick[:, 0][row_index]
    grid_row = brick_index * BX + cell_place // BY
    grid_column = column_brick * BY + cell_place % BY
    flat_cell = (grid_row * (BY * N_NARROW) + grid_column).astype(jnp.int32)
    pooled = jax.ops.segment_sum(features.astype(jnp.float32), flat_cell, num_segments=BX * N_WIDE * BY * N_NARROW)
    pooled = pooled.astype(jnp.bfloat16).reshape(BX * N_WIDE, BY * N_NARROW, PF)
    inner_field = jax.nn.gelu(convolve_same(pooled, conv_first), approximate=True).astype(jnp.bfloat16)
    return convolve_same(inner_field, conv_second)
```

```python
import functools

import jax
import jax.numpy as jnp
from jax import lax
from jax.experimental import pallas as pl
from jax.experimental.pallas import tpu as pltpu
from jax.sharding import PartitionSpec as P

HEADS = 4
HEAD = 128
ROW = 128
BLK = 256
BX = 8
BY = 32
EPS = 1e-06
LINE = BY + 16

F32 = jnp.float32
BF16 = jnp.bfloat16


def dot(a, b):
    return jnp.dot(a, b, preferred_element_type=F32)


def dot_t(a, b):
    return lax.dot_general(a, b, (((0,), (0,)), ((), ())), preferred_element_type=F32)


def dot_nt(a, b):
    return lax.dot_general(a, b, (((1,), (1,)), ((), ())), preferred_element_type=F32)


def params(mib=48):
    return pltpu.CompilerParams(vmem_limit_bytes=mib << 20)


def head_cols(h):
    return slice(h * HEAD, (h + 1) * HEAD)


def key_value_kernel(x_ref, wk_ref, wv_ref, k_ref, v_ref, total_ref, acc):
    step = pl.program_id(0)

    @pl.when(step == 0)
    def _():
        acc[...] = jnp.zeros_like(acc)

    x = x_ref[...]
    k = dot(x, wk_ref[...]).astype(BF16)
    v = dot(x, wv_ref[...]).astype(BF16)
    k_ref[...] = k
    v_ref[...] = v
    for pair in range(HEADS // 2):
        cols = slice(pair * 2 * HEAD, (pair + 1) * 2 * HEAD)
        outer = dot_t(k[:, cols], v[:, cols])
        acc[2 * pair] += outer[:HEAD, :HEAD]
        acc[2 * pair + 1] += outer[HEAD:, HEAD:]

    @pl.when(step == pl.num_programs(0) - 1)
    def _():
        total_ref[...] = acc[...].astype(BF16)


def key_value(voxels, w_qkv, block):
    tokens, width = voxels.shape
    inner = HEADS * HEAD
    tile = pl.BlockSpec((block, inner), lambda i: (i, 0))
    return pl.pallas_call(
        key_value_kernel,
        grid=(tokens // block,),
        in_specs=[
            pl.BlockSpec((block, width), lambda i: (i, 0)),
            pl.BlockSpec((width, inner), lambda i: (0, 1)),
            pl.BlockSpec((width, inner), lambda i: (0, 2)),
        ],
        out_specs=[tile, tile, pl.BlockSpec((HEADS, HEAD, HEAD), lambda i: (0, 0, 0))],
        out_shape=[
            jax.ShapeDtypeStruct((tokens, inner), BF16),
            jax.ShapeDtypeStruct((tokens, inner), BF16),
            jax.ShapeDtypeStruct((HEADS, HEAD, HEAD), BF16),
        ],
        scratch_shapes=[pltpu.VMEM((HEADS, HEAD, HEAD), F32)],
        compiler_params=params(),
        name="key_value",
    )(voxels, w_qkv, w_qkv)


def local_kernel(x_ref, wq_ref, k_ref, v_ref, q_ref, part_ref, state):
    step = pl.program_id(0)

    @pl.when(step == 0)
    def _():
        state[...] = jnp.zeros_like(state)

    q = dot(x_ref[...], wq_ref[...]).astype(BF16)
    q_ref[...] = q
    causal = lax.broadcasted_iota(jnp.int32, (BLK, BLK), 0) >= lax.broadcasted_iota(
        jnp.int32, (BLK, BLK), 1
    )
    for h in range(HEADS):
        cols = head_cols(h)
        qh, kh, vh = q[:, cols], k_ref[:, cols], v_ref[:, cols]
        scores = jnp.where(causal, dot_nt(qh, kh), 0.0).astype(BF16)
        part_ref[:, cols] = dot(scores, vh) + dot(qh, state[h].astype(BF16))
        state[h] += dot_t(kh, vh)


def local_attention(voxels, w_qkv, k, v):
    tokens, width = voxels.shape
    inner = HEADS * HEAD
    tile = pl.BlockSpec((BLK, inner), lambda i: (i, 0))
    return pl.pallas_call(
        local_kernel,
        grid=(tokens // BLK,),
        in_specs=[
            pl.BlockSpec((BLK, width), lambda i: (i, 0)),
            pl.BlockSpec((width, inner), lambda i: (0, 0)),
            tile,
            tile,
        ],
        out_specs=[tile, tile],
        out_shape=[
            jax.ShapeDtypeStruct((tokens, inner), BF16),
            jax.ShapeDtypeStruct((tokens, inner), F32),
        ],
        scratch_shapes=[pltpu.VMEM((HEADS, HEAD, HEAD), F32)],
        compiler_params=params(),
        cost_estimate=pl.CostEstimate(
            flops=2 * tokens * inner * (width + 2 * BLK + 2 * HEAD),
            bytes_accessed=tokens * inner * 12,
            transcendentals=0,
        ),
        name="local_attention",
    )(voxels, w_qkv, k, v)


def finish_kernel(
    orders, brick_ref, q_ref, part_ref, x_ref, state_ref, wo_ref, wf_ref, place_ref, *refs
):
    outs, acc, normed = refs[:-2], refs[-2], refs[-1]
    step = pl.program_id(0)

    @pl.when(step == 0)
    def _():
        acc[...] = jnp.zeros_like(acc)

    for h in range(HEADS):
        cols = head_cols(h)
        attended = part_ref[:, cols] + dot(q_ref[:, cols], state_ref[h])
        mean_square = jnp.mean(attended * attended, axis=-1, keepdims=True)
        normed[:, cols] = (attended * lax.rsqrt(mean_square + EPS)).astype(BF16)
    hidden = (x_ref[...].astype(F32) + dot(normed[...], wo_ref[...])).astype(BF16)
    features = dot(hidden, wf_ref[...]).astype(BF16)
    cells = BX * BY
    rows = place_ref.shape[0]
    for r in range(rows):
        here = lax.broadcasted_iota(jnp.int32, (cells, ROW), 0) == place_ref[r]
        onehot = jnp.where(here, 1.0, 0.0).astype(BF16)
        acc[brick_ref[step * rows + r]] += dot(onehot, features[r * ROW : (r + 1) * ROW])

    @pl.when(step == pl.num_programs(0) - 1)
    def _():
        bricks = acc.shape[0]
        half_cells = cells // 2
        for part, order in enumerate(orders):
            for i in range(bricks):
                place = 0
                for bit in order:
                    place = 2 * place + ((i >> bit) & 1)
                which, slot = divmod(place, bricks // 2)
                outs[2 * part + which][slot] = acc[
                    i, part * half_cells : (part + 1) * half_cells
                ].astype(BF16)


def finish(q, part, voxels, state, w_out, w_feature, places, bricks, count, orders, block):
    tokens, width = voxels.shape
    inner = HEADS * HEAD
    channels = w_feature.shape[1]
    cells = BX * BY
    rows = block // ROW
    tile = lambda cols: pl.BlockSpec((block, cols), lambda i, *_: (i, 0))
    whole = lambda array: pl.BlockSpec(array.shape, lambda i, *_: (0,) * array.ndim)
    out = jax.ShapeDtypeStruct((count // 2, cells // 2, channels), BF16)
    return pl.pallas_call(
        functools.partial(finish_kernel, orders),
        grid_spec=pltpu.PrefetchScalarGridSpec(
            num_scalar_prefetch=1,
            grid=(tokens // block,),
            in_specs=[
                tile(inner),
                tile(inner),
                tile(width),
                whole(state),
                whole(w_out),
                whole(w_feature),
                pl.BlockSpec((rows, 1, ROW), lambda i, *_: (i, 0, 0)),
            ],
            out_specs=[whole(out)] * 4,
            scratch_shapes=[
                pltpu.VMEM((count, cells, channels), F32),
                pltpu.VMEM((block, inner), BF16),
            ],
        ),
        out_shape=[out] * 4,
        compiler_params=params(),
        name="finish",
    )(bricks, q, part, voxels, state, w_out, w_feature, places)


def field_kernel(
    edge_ref, own_ref, above_ref, below_ref, left_ref, right_ref, w1_ref, w2_ref, out_ref, field, wide
):
    lines = BX + 4
    shown = wide.shape[0]
    field[...] = jnp.zeros_like(field)
    for r in range(lines):
        at = 16 + r * LINE
        if r < 2:
            line = above_ref[r]
        elif r < BX + 2:
            line = own_ref[r - 2]
        else:
            line = below_ref[r - BX - 2]
        field[at : at + BY] = line.astype(F32)
        field[at - 2 : at] = left_ref[r].astype(F32)
        field[at + BY : at + BY + 2] = right_ref[r].astype(F32)

    channels = field.shape[1]

    def widen():
        for shift in range(3):
            wide[:, shift * channels : (shift + 1) * channels] = field[
                7 + shift : 7 + shift + shown
            ].astype(BF16)

    def convolve(w_ref, first, count):
        return sum(
            dot(wide[(first + dy - 1) * LINE : (first + dy - 1 + count) * LINE], w_ref[dy])
            for dy in range(3)
        )

    widen()
    inner = jax.nn.gelu(convolve(w1_ref, 1, BX + 2), approximate=True)
    column = lax.broadcasted_iota(jnp.int32, (LINE, 1), 0) - 8
    inside = (column >= edge_ref[2]) & (column < edge_ref[3])
    for r in range(1, BX + 3):
        keep = inside
        if r == 1:
            keep = keep & (edge_ref[0] == 0)
        if r == BX + 2:
            keep = keep & (edge_ref[1] == 0)
        field[8 + r * LINE : 8 + (r + 1) * LINE] = jnp.where(
            keep, inner[(r - 1) * LINE : r * LINE], 0.0
        )
    widen()
    flow = convolve(w2_ref, 2, BX)
    for r in range(BX):
        out_ref[r] = flow[r * LINE + 8 : r * LINE + 8 + BY]


def field_flow(edges, own, above, below, left, right, conv_first, conv_second):
    channels = own.shape[-1]
    vmem = pl.BlockSpec(memory_space=pltpu.VMEM)
    lines = BX + 4
    return pl.pallas_call(
        field_kernel,
        in_specs=[pl.BlockSpec(memory_space=pltpu.SMEM)] + [vmem] * 7,
        out_specs=vmem,
        out_shape=jax.ShapeDtypeStruct((BX, BY, channels), F32),
        scratch_shapes=[
            pltpu.VMEM((16 + lines * LINE, channels), F32),
            pltpu.VMEM((lines * LINE, 3 * channels), BF16),
        ],
        compiler_params=params(),
        name="field_flow",
    )(
        edges,
        own,
        above,
        below,
        left,
        right,
        conv_first.reshape(3, 3 * channels, channels),
        conv_second.reshape(3, 3 * channels, channels),
    )


def swap(array, axis, bit):
    count = lax.axis_size(axis)
    return lax.ppermute(array, axis, [(i, i ^ (1 << bit)) for i in range(count)])


def shift(array, axis, by):
    count = lax.axis_size(axis)
    return lax.ppermute(
        array, axis, [(i, i + by) for i in range(count) if 0 <= i + by < count]
    )


def exclusive_state(total):
    count, place = lax.axis_size("narrow"), lax.axis_index("narrow")
    shares = total.reshape(count, -1, HEAD, HEAD)
    pieces = []
    for k in range(count):
        if k == 0:
            pieces.append(lax.dynamic_index_in_dim(shares, place, 0, keepdims=False))
            continue
        target = lax.rem(place + k, count)
        out = lax.dynamic_index_in_dim(shares, target, 0, keepdims=False)
        pieces.append(lax.ppermute(out, "narrow", [(i, (i + k) % count) for i in range(count)]))
    pieces = [piece.astype(F32) for piece in pieces]
    running = sum(pieces)
    before = jnp.zeros_like(running)
    devices, position = lax.axis_size("wide"), lax.axis_index("wide")
    for bit in range(devices.bit_length() - 1):
        other = swap(running.astype(BF16), "wide", bit).astype(F32)
        before = before + jnp.where((position >> bit) & 1 == 1, other, 0.0)
        running = running + other
    result = []
    for k in range(count):
        receiver = lax.rem(place + k, count)
        value = before
        for j in range(count):
            source = lax.rem(place - j + count, count)
            value = value + jnp.where(source < receiver, pieces[j], 0.0)
        value = value.astype(BF16)
        if k > 0:
            value = lax.ppermute(value, "narrow", [(i, (i + k) % count) for i in range(count)])
        result.append(value)
    stacked = jnp.stack(result)
    order = jnp.array([(p - h) % count for p in range(count) for h in range(count)]).reshape(
        count, count
    )
    whole = stacked[order[place]] if count > 2 else jnp.where(
        place == 0, stacked, stacked[::-1]
    )
    return whole.reshape(HEADS, HEAD, HEAD)


def reduce_bricks(parts, orders):
    parts = [list(pair) for pair in parts]
    for level in range(len(orders[0])):
        arrived = [
            swap(gone, "wide", order[level]) for (_, gone), order in zip(parts, orders)
        ]
        for pair, more in zip(parts, arrived):
            total = (pair[0].astype(F32) + more.astype(F32)).astype(BF16)
            half = total.shape[0] // 2
            pair[0], pair[1] = total[:half] if half else total, total[half:]
    return [pair[0] if pair[0].shape[0] else pair[1] for pair in parts]


def per_device(voxels, w_qkv, w_out, w_feature, conv_first, conv_second, row_brick, cell_place):
    tokens = voxels.shape[0]
    channels = w_feature.shape[1]
    wide_count, wide_place = lax.axis_size("wide"), lax.axis_index("wide")
    narrow_count, narrow_place = lax.axis_size("narrow"), lax.axis_index("narrow")
    block = min(512, tokens)

    k, v, total = key_value(voxels, w_qkv, block)
    state = exclusive_state(total)
    q, part = local_attention(voxels, w_qkv, k, v)

    bits = list(range(wide_count.bit_length() - 1))
    orders = [bits, bits[1::-1] + bits[2:]]
    bricks = row_brick[:, 0] ^ wide_place
    places = cell_place.reshape(-1, 1, ROW)
    kept_a, sent_a, kept_b, sent_b = finish(
        q, part, voxels, state, w_out, w_feature, places, bricks, wide_count, orders, block
    )
    top, bottom = reduce_bricks([(kept_a, sent_a), (kept_b, sent_b)], orders)
    own = jnp.concatenate([top[0], bottom[0]], axis=0).reshape(BX, BY, channels)

    if narrow_count == 2:
        edge = jnp.where(narrow_place == 0, own[:, BY - 2 :], own[:, :2])
        other = swap(edge, "narrow", 0)
        left = jnp.where(narrow_place == 1, other, jnp.zeros_like(other))
        right = jnp.where(narrow_place == 0, other, jnp.zeros_like(other))
    else:
        left = shift(own[:, BY - 2 :], "narrow", 1)
        right = shift(own[:, :2], "narrow", -1)
    strip = jnp.concatenate([own, left, right], axis=1)
    above = shift(strip[BX - 2 :], "wide", 1)
    below = shift(strip[:2], "wide", -1)
    left = jnp.concatenate([above[:, BY : BY + 2], left, below[:, BY : BY + 2]], axis=0)
    right = jnp.concatenate([above[:, BY + 2 :], right, below[:, BY + 2 :]], axis=0)
    edges = jnp.stack(
        [
            (wide_place == 0).astype(jnp.int32),
            (wide_place == wide_count - 1).astype(jnp.int32),
            jnp.where(narrow_place == 0, 0, -1),
            jnp.where(narrow_place == narrow_count - 1, BY, BY + 1),
        ]
    ).astype(jnp.int32)
    return field_flow(
        edges, own, above[:, :BY], below[:, :BY], left, right, conv_first, conv_second
    )


def solution(mesh):
    placed = (
        P(("group", "wide", "narrow"), None),
        P(),
        P(),
        P(),
        P(),
        P(),
        P(("group", "wide", "narrow"), None),
        P(("group", "wide", "narrow")),
    )
    return jax.shard_map(
        per_device,
        mesh=mesh,
        in_specs=placed,
        out_specs=P(("group", "wide"), "narrow", None),
        check_vma=False,
    )
```

```python
import functools

import jax
import jax.numpy as jnp
from jax import lax
from jax.experimental import pallas as pl
from jax.experimental.pallas import tpu as pltpu
from jax.sharding import PartitionSpec as P

HEADS = 4
HEAD = 128
ROW = 128
BLK = 256
BX = 8
BY = 32
EPS = 1e-06
LINE = BY + 16

F32 = jnp.float32
BF16 = jnp.bfloat16


def dot(a, b):
    return jnp.dot(a, b, preferred_element_type=F32)


def dot_t(a, b):
    return lax.dot_general(a, b, (((0,), (0,)), ((), ())), preferred_element_type=F32)


def dot_nt(a, b):
    return lax.dot_general(a, b, (((1,), (1,)), ((), ())), preferred_element_type=F32)


KEY_VALUE_KIB = 44 * 1024


def params(kib=24 * 1024):
    return pltpu.CompilerParams(vmem_limit_bytes=kib << 10)


def head_cols(h):
    return slice(h * HEAD, (h + 1) * HEAD)


def key_value_kernel(
    chunks, x_ref, w_ref, x, k_ref, v_ref, before_ref, *refs
):
    totals, sems = refs[:-1], refs[-1]
    tokens = x.shape[0]
    inner = HEADS * HEAD
    rows = tokens // chunks
    blocks = rows // BLK
    loads = [
        pltpu.make_async_copy(
            x_ref.at[pl.ds(c * rows, rows)], x.at[pl.ds(c * rows, rows)], sems.at[c]
        )
        for c in range(chunks)
    ]
    for load in loads:
        load.start()
    running = [jnp.zeros((HEAD, HEAD), F32) for _ in range(HEADS)]
    for c in range(chunks):
        loads[c].wait()
        here = slice(c * rows, (c + 1) * rows)
        k = dot(x[here], w_ref[:, inner : 2 * inner]).astype(BF16)
        k_ref[here] = k
        v = dot(x[here], w_ref[:, 2 * inner :]).astype(BF16)
        v_ref[here] = v
        for b in range(blocks):
            block = slice(b * BLK, (b + 1) * BLK)
            for h in range(HEADS):
                before_ref[c * blocks + b, h] = running[h].astype(BF16)
            for pair in range(HEADS // 2):
                cols = slice(pair * 2 * HEAD, (pair + 1) * 2 * HEAD)
                outer = dot_t(k[block, cols], v[block, cols])
                running[2 * pair] += outer[:HEAD, :HEAD]
                running[2 * pair + 1] += outer[HEAD:, HEAD:]
    share = HEADS // len(totals)
    for h in range(HEADS):
        for k, total_ref in enumerate(totals):

            @pl.when((lax.axis_index("narrow") + k) % len(totals) == h // share)
            def _(total_ref=total_ref, h=h):
                total_ref[h % share] = running[h].astype(BF16)


def key_value(voxels, w_qkv, chunks, cores):
    tokens, width = voxels.shape
    inner = HEADS * HEAD
    hbm = pl.BlockSpec(memory_space=pl.ANY)
    vmem = pl.BlockSpec(memory_space=pltpu.VMEM)
    flat = jax.ShapeDtypeStruct((tokens, inner), BF16)
    states = jax.ShapeDtypeStruct((tokens // BLK, HEADS, HEAD, HEAD), BF16)
    share = jax.ShapeDtypeStruct((HEADS // cores, HEAD, HEAD), BF16)
    return pl.pallas_call(
        functools.partial(key_value_kernel, chunks),
        in_specs=[hbm, vmem],
        out_specs=[vmem] * (4 + cores),
        out_shape=[jax.ShapeDtypeStruct(voxels.shape, BF16), flat, flat, states] + [share] * cores,
        scratch_shapes=[pltpu.SemaphoreType.DMA((chunks,))],
        compiler_params=params(KEY_VALUE_KIB),
        name="key_value",
    )(voxels, w_qkv)


def local_kernel(first, count, x_ref, w_ref, k_ref, v_ref, before_ref, q_ref, part_ref):
    causal = lax.broadcasted_iota(jnp.int32, (BLK, BLK), 0) >= lax.broadcasted_iota(
        jnp.int32, (BLK, BLK), 1
    )
    here = slice(first * BLK, (first + count) * BLK)
    q = dot(x_ref[here], w_ref[:, : HEADS * HEAD]).astype(BF16)
    q_ref[...] = q
    for b in range(count):
        rows = slice((first + b) * BLK, (first + b + 1) * BLK)
        own = slice(b * BLK, (b + 1) * BLK)
        for h in range(HEADS):
            cols = head_cols(h)
            scores = dot_nt(q[own, cols], k_ref[rows, cols])
            scores = jnp.where(causal, scores, 0.0).astype(BF16)
            part_ref[own, cols] = dot(scores, v_ref[rows, cols]) + dot(
                q[own, cols], before_ref[first + b, h]
            )


def local_attention(x, w_qkv, k, v, before, first, count):
    width = x.shape[1]
    inner = HEADS * HEAD
    vmem = pl.BlockSpec(memory_space=pltpu.VMEM)
    rows = count * BLK
    return pl.pallas_call(
        functools.partial(local_kernel, first, count),
        in_specs=[vmem] * 5,
        out_specs=[vmem, vmem],
        out_shape=[
            jax.ShapeDtypeStruct((rows, inner), BF16),
            jax.ShapeDtypeStruct((rows, inner), F32),
        ],
        compiler_params=params(),
        cost_estimate=pl.CostEstimate(
            flops=2 * rows * inner * (width + 2 * BLK + HEAD),
            bytes_accessed=rows * inner * 12,
            transcendentals=0,
        ),
        name="local_attention",
    )(x, w_qkv, k, v, before)


def gather_kernel(*refs):
    ins, (running_ref, packed_ref) = refs[:-2], refs[-2:]
    running = sum(ref[...].astype(F32) for ref in ins)
    running_ref[...] = running
    packed_ref[...] = running.astype(BF16)


def scan_kernel(bit, running_ref, before_ref, other_ref, new_running, new_before, packed):
    other = other_ref[...].astype(F32)
    running = running_ref[...] + other
    new_running[...] = running
    packed[...] = running.astype(BF16)
    later = ((lax.axis_index("wide") >> bit) & 1).astype(F32)
    new_before[...] = before_ref[...] + later * other


def spread_kernel(cores, bit, before_ref, other_ref, *refs):
    pieces, outs = refs[:cores], refs[cores:]
    place = lax.axis_index("narrow")
    later = ((lax.axis_index("wide") >> bit) & 1).astype(F32)
    before = before_ref[...] + later * other_ref[...].astype(F32)
    for k, out in enumerate(outs):
        receiver = (place + k) % cores
        value = before
        for j, piece in enumerate(pieces):
            source = (place - j + cores) % cores
            value = value + jnp.where(source < receiver, 1.0, 0.0) * piece[...].astype(F32)
        out[...] = value.astype(BF16)


def small_call(kernel, name, inputs, dtypes, shape):
    vmem = pl.BlockSpec(memory_space=pltpu.VMEM)
    smem = pl.BlockSpec(memory_space=pltpu.SMEM)
    return pl.pallas_call(
        kernel,
        in_specs=[smem if array.dtype == jnp.int32 else vmem for array in inputs],
        out_specs=[vmem] * len(dtypes),
        out_shape=[jax.ShapeDtypeStruct(shape, dtype) for dtype in dtypes],
        compiler_params=params(4 * 1024),
        name=name,
    )(*inputs)


def finish_kernel(orders, spans, cores, brick_ref, *refs):
    pieces = len(spans)
    refs = list(refs)
    take = lambda n: [refs.pop(0) for _ in range(n)]
    q_refs, part_refs, state_refs = take(pieces), take(pieces), take(cores)
    x_ref, wo_ref, wf_ref, cell_ref = take(4)
    outs = take(4)
    acc, normed, state = refs
    share = HEADS // cores
    for k, ref in enumerate(state_refs):
        owner = (lax.axis_index("narrow") - k + cores) % cores
        for j in range(share):
            state[owner * share + j] = ref[j]
    acc[...] = jnp.zeros_like(acc)
    cells = BX * BY
    for (first, count), q_ref, part_ref in zip(spans, q_refs, part_refs):
        here = slice(first * BLK, (first + count) * BLK)
        for h in range(HEADS):
            cols = head_cols(h)
            attended = part_ref[:, cols] + dot(q_ref[:, cols], state[h])
            mean_square = jnp.mean(attended * attended, axis=-1, keepdims=True)
            normed[here, cols] = (attended * lax.rsqrt(mean_square + EPS)).astype(BF16)
        hidden = (x_ref[here].astype(F32) + dot(normed[here], wo_ref[...])).astype(BF16)
        features = dot(hidden, wf_ref[...]).astype(BF16)
        for r in range(count * BLK // ROW):
            row = first * BLK // ROW + r
            match = lax.broadcasted_iota(jnp.int32, (cells, ROW), 0) == cell_ref[row : row + 1]
            onehot = jnp.where(match, 1.0, 0.0).astype(BF16)
            brick = brick_ref[row] ^ lax.axis_index("wide")
            acc[brick] += dot(onehot, features[r * ROW : (r + 1) * ROW])
    bricks = acc.shape[0]
    half_cells = cells // 2
    for part, order in enumerate(orders):
        for i in range(bricks):
            place = 0
            for bit in order:
                place = 2 * place + ((i >> bit) & 1)
            which, slot = divmod(place, bricks // 2)
            outs[2 * part + which][slot] = acc[
                i, part * half_cells : (part + 1) * half_cells
            ].astype(BF16)


def finish(spans, bricks, qs, parts, states, x, w_out, w_feature, cell_rows, count, orders):
    tokens = x.shape[0]
    channels = w_feature.shape[1]
    cells = BX * BY
    vmem = pl.BlockSpec(memory_space=pltpu.VMEM)
    smem = pl.BlockSpec(memory_space=pltpu.SMEM)
    out = jax.ShapeDtypeStruct((count // 2, cells // 2, channels), BF16)
    return pl.pallas_call(
        functools.partial(finish_kernel, orders, spans, len(states)),
        in_specs=[smem] + [vmem] * (2 * len(spans) + len(states) + 4),
        out_specs=[vmem] * 4,
        out_shape=[out] * 4,
        scratch_shapes=[
            pltpu.VMEM((count, cells, channels), F32),
            pltpu.VMEM((tokens, HEADS * HEAD), BF16),
            pltpu.VMEM((HEADS, HEAD, HEAD), BF16),
        ],
        compiler_params=params(),
        name="finish",
    )(bricks, *qs, *parts, *states, x, w_out, w_feature, cell_rows)


def field_kernel(
    edge_ref, own_ref, above_ref, below_ref, left_ref, right_ref, w1_ref, w2_ref, out_ref, field, wide
):
    lines = BX + 4
    shown = wide.shape[0]
    field[...] = jnp.zeros_like(field)
    for r in range(lines):
        at = 16 + r * LINE
        if r < 2:
            line = above_ref[r]
        elif r < BX + 2:
            line = own_ref[r - 2]
        else:
            line = below_ref[r - BX - 2]
        field[at : at + BY] = line.astype(F32)
        field[at - 2 : at] = left_ref[r].astype(F32)
        field[at + BY : at + BY + 2] = right_ref[r].astype(F32)

    channels = field.shape[1]

    def widen():
        for shift in range(3):
            wide[:, shift * channels : (shift + 1) * channels] = field[
                7 + shift : 7 + shift + shown
            ].astype(BF16)

    def convolve(w_ref, first, count):
        return sum(
            dot(wide[(first + dy - 1) * LINE : (first + dy - 1 + count) * LINE], w_ref[dy])
            for dy in range(3)
        )

    widen()
    inner = jax.nn.gelu(convolve(w1_ref, 1, BX + 2), approximate=True)
    column = lax.broadcasted_iota(jnp.int32, (LINE, 1), 0) - 8
    inside = (column >= edge_ref[2]) & (column < edge_ref[3])
    for r in range(1, BX + 3):
        keep = inside
        if r == 1:
            keep = keep & (edge_ref[0] == 0)
        if r == BX + 2:
            keep = keep & (edge_ref[1] == 0)
        field[8 + r * LINE : 8 + (r + 1) * LINE] = jnp.where(
            keep, inner[(r - 1) * LINE : r * LINE], 0.0
        )
    widen()
    flow = convolve(w2_ref, 2, BX)
    for r in range(BX):
        out_ref[r] = flow[r * LINE + 8 : r * LINE + 8 + BY]


def field_flow(edges, own, above, below, left, right, conv_first, conv_second):
    channels = own.shape[-1]
    vmem = pl.BlockSpec(memory_space=pltpu.VMEM)
    lines = BX + 4
    return pl.pallas_call(
        field_kernel,
        in_specs=[pl.BlockSpec(memory_space=pltpu.SMEM)] + [vmem] * 7,
        out_specs=vmem,
        out_shape=jax.ShapeDtypeStruct((BX, BY, channels), F32),
        scratch_shapes=[
            pltpu.VMEM((16 + lines * LINE, channels), F32),
            pltpu.VMEM((lines * LINE, 3 * channels), BF16),
        ],
        compiler_params=params(16 * 1024),
        name="field_flow",
    )(
        edges,
        own,
        above,
        below,
        left,
        right,
        conv_first.reshape(3, 3 * channels, channels),
        conv_second.reshape(3, 3 * channels, channels),
    )


def swap(array, axis, bit):
    count = lax.axis_size(axis)
    return lax.ppermute(array, axis, [(i, i ^ (1 << bit)) for i in range(count)])


def shift(array, axis, by):
    count = lax.axis_size(axis)
    return lax.ppermute(
        array, axis, [(i, i + by) for i in range(count) if 0 <= i + by < count]
    )


def rotate(array, axis, by):
    count = lax.axis_size(axis)
    return lax.ppermute(array, axis, [(i, (i + by) % count) for i in range(count)])


def exchange_lines(strip):
    groups, count, cores = (lax.axis_size(axis) for axis in ("group", "wide", "narrow"))
    place = lax.axis_index("wide")
    got = []
    for start in range(2):
        pairs = []
        for g in range(groups):
            for w in range(count):
                other = w + 1 if w % 2 == start else w - 1
                far = g
                if not 0 <= other < count:
                    other, far = w, g ^ 1 if groups % 2 == 0 else g
                for c in range(cores):
                    pairs.append(((g * count + w) * cores + c, (far * count + other) * cores + c))
        upper = place % 2 == start
        out = jnp.where(upper, strip[BX - 2 :], strip[:2])
        got.append(lax.ppermute(out, ("group", "wide", "narrow"), pairs))
    above = jnp.where(place % 2 == 1, got[0], got[1])
    below = jnp.where(place % 2 == 1, got[1], got[0])
    above = jnp.where(place > 0, above, jnp.zeros_like(above))
    below = jnp.where(place < count - 1, below, jnp.zeros_like(below))
    return above, below


def earlier_state(totals, works):
    cores, shape = len(totals), totals[0].shape
    works, done = list(works), []
    pieces = [totals[0]] + [rotate(totals[k], "narrow", k) for k in range(1, cores)]
    running, packed = small_call(gather_kernel, "gather", pieces, [F32, BF16], shape)
    before = jnp.zeros(shape, F32)
    bits = lax.axis_size("wide").bit_length() - 1
    for bit in range(bits):
        held = None
        if works:
            held, packed = works.pop(0)(packed)
        other = swap(packed, "wide", bit)
        if held is not None:
            held, other = lax.optimization_barrier((held, other))
            done.append(held)
        if bit == bits - 1:
            break
        running, before, packed = small_call(
            functools.partial(scan_kernel, bit),
            "scan",
            [running, before, other],
            [F32, F32, BF16],
            shape,
        )
    outs = small_call(
        functools.partial(spread_kernel, cores, bits - 1),
        "spread",
        [before, other] + pieces,
        [BF16] * cores,
        shape,
    )
    states = [outs[0]] + [rotate(outs[k], "narrow", k) for k in range(1, cores)]
    while works:
        done.append(works.pop(0)(packed)[0])
    return states, done


def reduce_bricks(parts, orders):
    parts = [list(pair) for pair in parts]
    for level in range(len(orders[0])):
        arrived = [
            swap(gone, "wide", order[level]) for (_, gone), order in zip(parts, orders)
        ]
        for pair, more in zip(parts, arrived):
            total = (pair[0].astype(F32) + more.astype(F32)).astype(BF16)
            half = total.shape[0] // 2
            pair[0], pair[1] = total[:half] if half else total, total[half:]
    return [pair[0] if pair[0].shape[0] else pair[1] for pair in parts]


def per_device(voxels, w_qkv, w_out, w_feature, conv_first, conv_second, row_brick, cell_place):
    tokens = voxels.shape[0]
    channels = w_feature.shape[1]
    wide_count, wide_place = lax.axis_size("wide"), lax.axis_index("wide")
    narrow_count, narrow_place = lax.axis_size("narrow"), lax.axis_index("narrow")

    blocks = tokens // BLK
    x, k, v, before, *totals = key_value(voxels, w_qkv, max(1, blocks // 2), narrow_count)
    cuts = sorted({blocks * i // 3 for i in range(4)})
    spans = [(first, last - first) for first, last in zip(cuts, cuts[1:])]

    def work(span):
        def run(array):
            array, k_now = lax.optimization_barrier((array, k))
            return local_attention(x, w_qkv, k_now, v, before, *span), array

        return run

    states, pieces = earlier_state(totals, [work(span) for span in spans])

    bits = list(range(wide_count.bit_length() - 1))
    orders = [bits, bits[1::-1] + bits[2:]]
    kept_a, sent_a, kept_b, sent_b = finish(
        spans,
        row_brick[:, 0],
        [q for q, _ in pieces],
        [part for _, part in pieces],
        states,
        x,
        w_out,
        w_feature,
        cell_place.reshape(-1, ROW),
        wide_count,
        orders,
    )
    top, bottom = reduce_bricks([(kept_a, sent_a), (kept_b, sent_b)], orders)
    own = jnp.concatenate([top[0], bottom[0]], axis=0).reshape(BX, BY, channels)

    if narrow_count == 2:
        edge = jnp.where(narrow_place == 0, own[:, BY - 2 :], own[:, :2])
        other = swap(edge, "narrow", 0)
        left = jnp.where(narrow_place == 1, other, jnp.zeros_like(other))
        right = jnp.where(narrow_place == 0, other, jnp.zeros_like(other))
    else:
        left = shift(own[:, BY - 2 :], "narrow", 1)
        right = shift(own[:, :2], "narrow", -1)
    strip = jnp.concatenate([own, left, right], axis=1)
    above, below = exchange_lines(strip)
    left = jnp.concatenate([above[:, BY : BY + 2], left, below[:, BY : BY + 2]], axis=0)
    right = jnp.concatenate([above[:, BY + 2 :], right, below[:, BY + 2 :]], axis=0)
    edges = jnp.stack(
        [
            (wide_place == 0).astype(jnp.int32),
            (wide_place == wide_count - 1).astype(jnp.int32),
            jnp.where(narrow_place == 0, 0, -1),
            jnp.where(narrow_place == narrow_count - 1, BY, BY + 1),
        ]
    ).astype(jnp.int32)
    return field_flow(
        edges, own, above[:, :BY], below[:, :BY], left, right, conv_first, conv_second
    )


def solution(mesh):
    placed = (
        P(("group", "wide", "narrow"), None),
        P(),
        P(),
        P(),
        P(),
        P(),
        P(("group", "wide", "narrow"), None),
        P(("group", "wide", "narrow")),
    )
    return jax.shard_map(
        per_device,
        mesh=mesh,
        in_specs=placed,
        out_specs=P(("group", "wide"), "narrow", None),
        check_vma=False,
    )
```

```python
import functools

import jax
import jax.numpy as jnp
from jax import lax
from jax.experimental import pallas as pl
from jax.experimental.pallas import tpu as pltpu
from jax.sharding import PartitionSpec as P

HEADS = 4
HEAD = 128
ROW = 128
BLK = 256
BX = 8
BY = 32
EPS = 1e-06
GAP = 16
LINE = GAP + BY

F32 = jnp.float32
BF16 = jnp.bfloat16


def dot(a, b):
    return jnp.dot(a, b, preferred_element_type=F32)


def dot_t(a, b):
    return lax.dot_general(a, b, (((0,), (0,)), ((), ())), preferred_element_type=F32)


def dot_nt(a, b):
    return lax.dot_general(a, b, (((1,), (1,)), ((), ())), preferred_element_type=F32)


KEY_VALUE_KIB = 46592


def params(kib=24 * 1024):
    return pltpu.CompilerParams(vmem_limit_bytes=kib << 10)


def head_cols(h):
    return slice(h * HEAD, (h + 1) * HEAD)


def key_value_kernel(spans, x_ref, w_ref, *refs):
    refs = list(refs)
    take = lambda n: [refs.pop(0) for _ in range(n)]
    xs, ks, vs = take(len(spans)), take(len(spans)), take(len(spans))
    wq, before_ref = take(2)
    totals, (w, sems) = refs[:-2], refs[-2:]
    inner = HEADS * HEAD

    def columns(part, target):
        return pltpu.make_async_copy(
            w_ref.at[:, pl.ds(part * inner, inner)], target, sems.at[len(spans) + part]
        )

    loads = [
        pltpu.make_async_copy(x_ref.at[pl.ds(first * BLK, count * BLK)], x, sems.at[n])
        for n, ((first, count), x) in enumerate(zip(spans, xs))
    ]
    w_loads = [columns(0, wq), columns(1, w.at[0]), columns(2, w.at[1])]
    w_loads[1].start()
    loads[0].start()
    w_loads[2].start()
    for load in loads[1:]:
        load.start()
    w_loads[0].start()
    running = [jnp.zeros((HEAD, HEAD), F32) for _ in range(HEADS)]
    for n, ((first, count), x, k_ref, v_ref) in enumerate(zip(spans, xs, ks, vs)):
        if n == 0:
            w_loads[1].wait()
        loads[n].wait()
        k = dot(x[...], w[0]).astype(BF16)
        k_ref[...] = k
        if n == 0:
            w_loads[2].wait()
        v = dot(x[...], w[1]).astype(BF16)
        v_ref[...] = v
        for b in range(count):
            block = slice(b * BLK, (b + 1) * BLK)
            for h in range(HEADS):
                before_ref[first + b, h] = running[h].astype(BF16)
            for pair in range(HEADS // 2):
                cols = slice(pair * 2 * HEAD, (pair + 1) * 2 * HEAD)
                outer = dot_t(k[block, cols], v[block, cols])
                running[2 * pair] += outer[:HEAD, :HEAD]
                running[2 * pair + 1] += outer[HEAD:, HEAD:]
    share = HEADS // len(totals)
    for h in range(HEADS):
        for k, total_ref in enumerate(totals):

            @pl.when((lax.axis_index("narrow") + k) % len(totals) == h // share)
            def _(total_ref=total_ref, h=h):
                total_ref[h % share] = running[h].astype(BF16)

    w_loads[0].wait()


def key_value(spans, voxels, w_qkv, cores):
    tokens, width = voxels.shape
    inner = HEADS * HEAD
    hbm = pl.BlockSpec(memory_space=pl.ANY)
    vmem = pl.BlockSpec(memory_space=pltpu.VMEM)
    rows = [count * BLK for _, count in spans]
    out_shape = [jax.ShapeDtypeStruct((n, cols), BF16) for cols in (width, inner, inner) for n in rows]
    out_shape.append(jax.ShapeDtypeStruct((width, inner), BF16))
    out_shape.append(jax.ShapeDtypeStruct((tokens // BLK, HEADS, HEAD, HEAD), BF16))
    out_shape += [jax.ShapeDtypeStruct((HEADS // cores, HEAD, HEAD), BF16)] * cores
    outs = list(
        pl.pallas_call(
            functools.partial(key_value_kernel, spans),
            in_specs=[hbm, hbm],
            out_specs=[vmem] * len(out_shape),
            out_shape=out_shape,
            scratch_shapes=[
                pltpu.VMEM((2, width, inner), BF16),
                pltpu.SemaphoreType.DMA((len(spans) + 3,)),
            ],
            compiler_params=params(KEY_VALUE_KIB),
            name="key_value",
        )(voxels, w_qkv)
    )
    n = len(spans)
    return outs[:n], outs[n : 2 * n], outs[2 * n : 3 * n], outs[3 * n], outs[3 * n + 1], outs[3 * n + 2 :]


def local_kernel(first, count, weights, x_ref, wq_ref, k_ref, v_ref, before_ref, *refs):
    wf_ref, q_ref, part_ref, own_ref = refs[weights : weights + 4]
    causal = lax.broadcasted_iota(jnp.int32, (BLK, BLK), 0) >= lax.broadcasted_iota(
        jnp.int32, (BLK, BLK), 1
    )
    q = dot(x_ref[...], wq_ref[...]).astype(BF16)
    q_ref[...] = q
    own_ref[...] = dot(x_ref[...], wf_ref[...])
    for b in range(count):
        rows = slice(b * BLK, (b + 1) * BLK)
        for h in range(HEADS):
            cols = head_cols(h)
            scores = dot_nt(q[rows, cols], k_ref[rows, cols])
            scores = jnp.where(causal, scores, 0.0).astype(BF16)
            part_ref[rows, cols] = dot(scores, v_ref[rows, cols]) + dot(
                q[rows, cols], before_ref[first + b, h]
            )
    if weights:
        refs[-1][...] = dot(refs[0][...], wf_ref[...]).astype(BF16)


def local_attention(x, w_q, k, v, before, w_out, w_feature, first, count):
    rows, width = x.shape
    inner = HEADS * HEAD
    channels = w_feature.shape[1]
    vmem = pl.BlockSpec(memory_space=pltpu.VMEM)
    inputs = [x, w_q, k, v, before] + [w_out] * (w_out is not None) + [w_feature]
    out_shape = [
        jax.ShapeDtypeStruct((rows, inner), BF16),
        jax.ShapeDtypeStruct((rows, inner), F32),
        jax.ShapeDtypeStruct((rows, channels), F32),
    ]
    if w_out is not None:
        out_shape.append(jax.ShapeDtypeStruct(w_feature.shape, BF16))
    return pl.pallas_call(
        functools.partial(local_kernel, first, count, int(w_out is not None)),
        in_specs=[vmem] * len(inputs),
        out_specs=[vmem] * len(out_shape),
        out_shape=out_shape,
        compiler_params=params(),
        cost_estimate=pl.CostEstimate(
            flops=2 * rows * inner * (width + 2 * BLK + HEAD),
            bytes_accessed=rows * inner * 12,
            transcendentals=0,
        ),
        name="local_attention",
    )(*inputs)


def gather_kernel(*refs):
    ins, (running_ref, packed_ref) = refs[:-2], refs[-2:]
    running = sum(ref[...].astype(F32) for ref in ins)
    running_ref[...] = running
    packed_ref[...] = running.astype(BF16)


def scan_kernel(bit, running_ref, before_ref, other_ref, new_before, packed, *new_running):
    other = other_ref[...].astype(F32)
    running = running_ref[...] + other
    packed[...] = running.astype(BF16)
    for ref in new_running:
        ref[...] = running
    later = ((lax.axis_index("wide") >> bit) & 1).astype(F32)
    new_before[...] = before_ref[...] + later * other


def spread_kernel(cores, bit, before_ref, other_ref, *refs):
    pieces, outs = refs[:cores], refs[cores:]
    place = lax.axis_index("narrow")
    later = ((lax.axis_index("wide") >> bit) & 1).astype(F32)
    before = before_ref[...] + later * other_ref[...].astype(F32)
    for k, out in enumerate(outs):
        receiver = (place + k) % cores
        value = before
        for j, piece in enumerate(pieces):
            source = (place - j + cores) % cores
            value = value + jnp.where(source < receiver, 1.0, 0.0) * piece[...].astype(F32)
        out[...] = value.astype(BF16)


def small_call(kernel, name, inputs, dtypes, shape):
    vmem = pl.BlockSpec(memory_space=pltpu.VMEM)
    smem = pl.BlockSpec(memory_space=pltpu.SMEM)
    return pl.pallas_call(
        kernel,
        in_specs=[smem if array.dtype == jnp.int32 else vmem for array in inputs],
        out_specs=[vmem] * len(dtypes),
        out_shape=[jax.ShapeDtypeStruct(shape, dtype) for dtype in dtypes],
        compiler_params=params(4 * 1024),
        name=name,
    )(*inputs)


def ones_blocks(width):
    rows, cols = (lax.broadcasted_iota(jnp.int32, (width, width), axis) for axis in range(2))
    return jnp.where(rows // HEAD == cols // HEAD, 1.0, 0.0).astype(BF16)


def block_state(state_ref, scratch):
    scratch[...] = jnp.zeros_like(scratch)
    for j in range(state_ref.shape[0]):
        scratch[head_cols(j), head_cols(j)] = state_ref[j]
    return scratch[...]


def norm_share(q, part, state, ones):
    attended = part + dot(q, state)
    squares = dot((attended * attended).astype(BF16), ones)
    return (attended * lax.rsqrt(squares * (1 / HEAD) + EPS)).astype(BF16)


def share_columns(cores, before):
    width = HEADS // cores * HEAD
    owner = (lax.axis_index("narrow") - before + cores) % cores
    return pl.ds(pl.multiple_of(owner * width, width), width)


def own_share_kernel(cores, state_ref, *refs):
    pieces = len(refs) // 3
    qs, parts, outs, scratch = refs[:pieces], refs[pieces : 2 * pieces], refs[2 * pieces : -1], refs[-1]
    cols = share_columns(cores, 0)
    state, ones = block_state(state_ref, scratch), ones_blocks(scratch.shape[0])
    for q, part, out in zip(qs, parts, outs):
        out[...] = norm_share(q[:, cols], part[:, cols], state, ones)


def own_share(cores, state, qs, parts):
    width = HEADS // cores * HEAD
    vmem = pl.BlockSpec(memory_space=pltpu.VMEM)
    rows = sum(q.shape[0] for q in qs)
    return pl.pallas_call(
        functools.partial(own_share_kernel, cores),
        in_specs=[vmem] * (1 + 2 * len(qs)),
        out_specs=[vmem] * len(qs),
        out_shape=[jax.ShapeDtypeStruct((q.shape[0], width), BF16) for q in qs],
        scratch_shapes=[pltpu.VMEM((width, width), BF16)],
        compiler_params=params(),
        cost_estimate=pl.CostEstimate(
            flops=4 * rows * width * width, bytes_accessed=rows * width * 8, transcendentals=0
        ),
        name="own_share",
    )(state, *qs, *parts)


def finish_kernel(orders, spans, cores, brick_ref, *refs):
    pieces = len(spans)
    refs = list(refs)
    take = lambda n: [refs.pop(0) for _ in range(n)]
    q_refs, part_refs, normed_refs, own_refs = (take(pieces) for _ in range(4))
    state_refs = take(cores - 1)
    w_ref, cell_ref = take(2)
    outs = take(4)
    acc, scratch = refs
    shares = [share_columns(cores, k) for k in range(cores)]
    ones = ones_blocks(scratch.shape[1])
    states = [block_state(ref, scratch.at[k]) for k, ref in enumerate(state_refs)]
    acc[...] = jnp.zeros_like(acc)
    cells = BX * BY
    for n, (first, count) in enumerate(spans):
        features = own_refs[n][...] + dot(normed_refs[n][...], w_ref[shares[0], :])
        for state, cols in zip(states, shares[1:]):
            normed = norm_share(q_refs[n][:, cols], part_refs[n][:, cols], state, ones)
            features += dot(normed, w_ref[cols, :])
        features = features.astype(BF16)
        for r in range(count * BLK // ROW):
            row = first * BLK // ROW + r
            match = lax.broadcasted_iota(jnp.int32, (cells, ROW), 0) == cell_ref[row : row + 1]
            onehot = jnp.where(match, 1.0, 0.0).astype(BF16)
            brick = brick_ref[row] ^ lax.axis_index("wide")
            acc[brick] += dot(onehot, features[r * ROW : (r + 1) * ROW])
    ranges = [[(0, 2 * BY), (cells - 2 * BY, cells)], [(2 * BY, cells - 2 * BY)]]
    bricks = acc.shape[0]
    for part, order in enumerate(orders):
        for i in range(bricks):
            place = 0
            for bit in order:
                place = 2 * place + ((i >> bit) & 1)
            which, slot = divmod(place, bricks // 2)
            to = 0
            for first, last in ranges[part]:
                outs[2 * part + which][slot, to : to + last - first] = acc[i, first:last].astype(BF16)
                to += last - first


def finish(spans, bricks, qs, parts, normed, own, states, weights, cell_rows, count, orders):
    channels = weights.shape[1]
    cores = len(states) + 1
    width = HEADS // cores * HEAD
    cells = BX * BY
    vmem = pl.BlockSpec(memory_space=pltpu.VMEM)
    smem = pl.BlockSpec(memory_space=pltpu.SMEM)
    out = jax.ShapeDtypeStruct((count // 2, cells // 2, channels), BF16)
    return pl.pallas_call(
        functools.partial(finish_kernel, orders, spans, cores),
        in_specs=[smem] + [vmem] * (4 * len(spans) + cores + 1),
        out_specs=[vmem] * 4,
        out_shape=[out] * 4,
        scratch_shapes=[
            pltpu.VMEM((count, cells, channels), F32),
            pltpu.VMEM((max(1, cores - 1), width, width), BF16),
        ],
        compiler_params=params(),
        name="finish",
    )(bricks, *qs, *parts, *normed, *own, *states, weights, cell_rows)


def field_kernel(lines_ref, sides_ref, w1_ref, w2_ref, out_ref, field):
    lines = BX + 4
    wide, narrow = lax.axis_index("wide"), lax.axis_index("narrow")
    first_line, last_line = wide == 0, wide == lax.axis_size("wide") - 1
    first_column, last_column = narrow == 0, narrow == lax.axis_size("narrow") - 1
    for r in range(lines):
        field[r * LINE : r * LINE + GAP] = sides_ref[r]
        field[r * LINE + GAP : (r + 1) * LINE] = lines_ref[r]
    field[lines * LINE :] = sides_ref[lines]

    def convolve(w_ref, start, count):
        lhs = jnp.concatenate(
            [field[start + dy * LINE : start + dy * LINE + count] for dy in (-1, 0, 1)], axis=1
        )
        left, middle, right = [
            dot(lhs, jnp.concatenate([w_ref[dy, dx] for dy in range(3)], axis=0))
            for dx in range(3)
        ]
        return pltpu.roll(left, 1, 0) + middle + pltpu.roll(right, count - 1, 0)

    count = (BX + 2) * LINE + GAP
    inner = jax.nn.gelu(convolve(w1_ref, LINE, count), approximate=True)
    at = lax.broadcasted_iota(jnp.int32, (count, 1), 0)
    outside = first_line & (at <= LINE) | last_line & (at > (BX + 1) * LINE)
    for r in range(BX + 2):
        outside |= first_column & (at == r * LINE + GAP - 1)
        outside |= last_column & (at == (r + 1) * LINE)
    field[LINE : LINE + count] = jnp.where(outside, 0.0, inner).astype(BF16)
    flow = convolve(w2_ref, 2 * LINE, BX * LINE + GAP)
    for r in range(BX):
        out_ref[r] = flow[r * LINE + GAP : (r + 1) * LINE]


def field_flow(lines, left, right, conv_first, conv_second):
    count, _, channels = lines.shape
    vmem = pl.BlockSpec(memory_space=pltpu.VMEM)
    sides = jnp.pad(right, ((1, 0), (0, GAP - 2), (0, 0))) + jnp.pad(
        left, ((0, 1), (GAP - 2, 0), (0, 0))
    )
    return pl.pallas_call(
        field_kernel,
        in_specs=[vmem] * 4,
        out_specs=vmem,
        out_shape=jax.ShapeDtypeStruct((BX, BY, channels), F32),
        scratch_shapes=[pltpu.VMEM((count * LINE + GAP, channels), BF16)],
        compiler_params=params(16 * 1024),
        name="field_flow",
    )(lines, sides, conv_first, conv_second)


def swap(array, axis, bit):
    count = lax.axis_size(axis)
    return lax.ppermute(array, axis, [(i, i ^ (1 << bit)) for i in range(count)])


def shift(array, axis, by):
    count = lax.axis_size(axis)
    return lax.ppermute(
        array, axis, [(i, i + by) for i in range(count) if 0 <= i + by < count]
    )


def rotate(array, axis, by):
    count = lax.axis_size(axis)
    return lax.ppermute(array, axis, [(i, (i + by) % count) for i in range(count)])


def side_columns(lines):
    if lax.axis_size("narrow") != 2:
        return shift(lines[:, BY - 2 :], "narrow", 1), shift(lines[:, :2], "narrow", -1)
    first = lax.axis_index("narrow") == 0
    other = swap(jnp.where(first, lines[:, BY - 2 :], lines[:, :2]), "narrow", 0)
    nothing = jnp.zeros_like(other)
    return jnp.where(first, nothing, other), jnp.where(first, other, nothing)


def exchange_lines(strip):
    groups, count, cores = (lax.axis_size(axis) for axis in ("group", "wide", "narrow"))
    place = lax.axis_index("wide")
    got = []
    for start in range(2):
        pairs = []
        for g in range(groups):
            for w in range(count):
                other = w + 1 if w % 2 == start else w - 1
                far = g
                if not 0 <= other < count:
                    other, far = w, g ^ 1 if groups % 2 == 0 else g
                for c in range(cores):
                    pairs.append(((g * count + w) * cores + c, (far * count + other) * cores + c))
        upper = place % 2 == start
        out = jnp.where(upper, strip[2:], strip[:2])
        got.append(lax.ppermute(out, ("group", "wide", "narrow"), pairs))
    above = jnp.where(place % 2 == 1, got[0], got[1])
    below = jnp.where(place % 2 == 1, got[1], got[0])
    above = jnp.where(place > 0, above, jnp.zeros_like(above))
    below = jnp.where(place < count - 1, below, jnp.zeros_like(below))
    return above, below


def earlier_state(totals, works):
    cores, shape = len(totals), totals[0].shape
    works, done = list(works), []
    pieces = [totals[0]] + [rotate(totals[k], "narrow", k) for k in range(1, cores)]
    running, packed = small_call(gather_kernel, "gather", pieces, [F32, BF16], shape)
    before = jnp.zeros(shape, F32)
    bits = lax.axis_size("wide").bit_length() - 1
    for bit in range(bits):
        held = None
        if works:
            held, packed = works.pop(0)(packed)
        other = swap(packed, "wide", bit)
        if held is not None:
            held, other = lax.optimization_barrier((held, other))
            done.append(held)
        if bit == bits - 1:
            break
        before, packed, *more = small_call(
            functools.partial(scan_kernel, bit),
            "scan",
            [running, before, other],
            [F32, BF16] + [F32] * (bit < bits - 2),
            shape,
        )
        running = more[0] if more else None
    outs = small_call(
        functools.partial(spread_kernel, cores, bits - 1),
        "spread",
        [before, other] + pieces,
        [BF16] * cores,
        shape,
    )
    states = [outs[0]] + [rotate(outs[k], "narrow", k) for k in range(1, cores)]
    while works:
        done.append(works.pop(0)(packed)[0])
    return states, done


def reduce_bricks(parts, orders):
    parts = [list(pair) for pair in parts]
    for level in range(len(orders[0])):
        arrived = [
            swap(gone, "wide", order[level]) for (_, gone), order in zip(parts, orders)
        ]
        for pair, more in zip(parts, arrived):
            total = (pair[0].astype(F32) + more.astype(F32)).astype(BF16)
            half = total.shape[0] // 2
            pair[0], pair[1] = total[:half] if half else total, total[half:]
    return [pair[0] if pair[0].shape[0] else pair[1] for pair in parts]


def per_device(voxels, w_qkv, w_out, w_feature, conv_first, conv_second, row_brick, cell_place):
    tokens = voxels.shape[0]
    channels = w_feature.shape[1]
    wide_count, wide_place = lax.axis_size("wide"), lax.axis_index("wide")
    narrow_count, narrow_place = lax.axis_size("narrow"), lax.axis_index("narrow")

    blocks = tokens // BLK
    cuts = sorted({blocks * i // 3 for i in range(4)})
    spans = [(first, last - first) for first, last in zip(cuts, cuts[1:])]
    xs, ks, vs, w_q, before, totals = key_value(spans, voxels, w_qkv, narrow_count)

    def work(n):
        def run(array):
            array, k = lax.optimization_barrier((array, ks[n]))
            weight = w_out if n == 0 else None
            return local_attention(
                xs[n], w_q, k, vs[n], before, weight, w_feature, *spans[n]
            ), array

        return run

    states, pieces = earlier_state(totals, [work(n) for n in range(len(spans))])
    weights = pieces[0][3]
    qs, parts, own = ([piece[i] for piece in pieces] for i in range(3))
    normed = own_share(narrow_count, states[0], qs, parts)

    bits = list(range(wide_count.bit_length() - 1))
    orders = [bits, bits[1::-1] + bits[2:]]
    kept_a, sent_a, kept_b, sent_b = finish(
        spans,
        row_brick[:, 0],
        qs,
        parts,
        normed,
        own,
        states[1:],
        weights,
        cell_place.reshape(-1, ROW),
        wide_count,
        orders,
    )
    outer, middle = reduce_bricks([(kept_a, sent_a), (kept_b, sent_b)], orders)
    outer, middle = (part.reshape(-1, BY, channels) for part in (outer, middle))
    above, below = exchange_lines(outer)
    lines = jnp.concatenate([above, outer[:2], middle, outer[2:], below], axis=0)
    left, right = side_columns(lines)
    return field_flow(lines, left, right, conv_first, conv_second)


def solution(mesh):
    placed = (
        P(("group", "wide", "narrow"), None),
        P(),
        P(),
        P(),
        P(),
        P(),
        P(("group", "wide", "narrow"), None),
        P(("group", "wide", "narrow")),
    )
    return jax.shard_map(
        per_device,
        mesh=mesh,
        in_specs=placed,
        out_specs=P(("group", "wide"), "narrow", None),
        check_vma=False,
    )
```

```python
import functools

import jax
import jax.numpy as jnp
from jax import lax
from jax.experimental import pallas as pl
from jax.experimental.pallas import tpu as pltpu
from jax.sharding import PartitionSpec as P

HEADS = 4
HEAD = 128
ROW = 128
BLK = 256
BX = 8
BY = 32
EPS = 1e-06
GAP = 16
LINE = GAP + BY

F32 = jnp.float32
BF16 = jnp.bfloat16


def dot(a, b):
    return jnp.dot(a, b, preferred_element_type=F32)


def dot_t(a, b):
    return lax.dot_general(a, b, (((0,), (0,)), ((), ())), preferred_element_type=F32)


def dot_nt(a, b):
    return lax.dot_general(a, b, (((1,), (1,)), ((), ())), preferred_element_type=F32)


KEY_VALUE_KIB = 46592


def params(kib=24 * 1024):
    return pltpu.CompilerParams(vmem_limit_bytes=kib << 10)


def head_cols(h):
    return slice(h * HEAD, (h + 1) * HEAD)


def key_value_kernel(spans, x_ref, w_ref, *refs):
    refs = list(refs)
    take = lambda n: [refs.pop(0) for _ in range(n)]
    xs, ks, vs = take(len(spans)), take(len(spans)), take(len(spans))
    wq, before_ref = take(2)
    totals, (w, sems) = refs[:-2], refs[-2:]
    inner = HEADS * HEAD

    def columns(part, target):
        return pltpu.make_async_copy(
            w_ref.at[:, pl.ds(part * inner, inner)], target, sems.at[len(spans) + part]
        )

    loads = [
        pltpu.make_async_copy(x_ref.at[pl.ds(first * BLK, count * BLK)], x, sems.at[n])
        for n, ((first, count), x) in enumerate(zip(spans, xs))
    ]
    w_loads = [columns(0, wq), columns(1, w.at[0]), columns(2, w.at[1])]
    w_loads[1].start()
    loads[0].start()
    w_loads[2].start()
    for load in loads[1:]:
        load.start()
    w_loads[0].start()
    running = [jnp.zeros((HEAD, HEAD), F32) for _ in range(HEADS)]
    for n, ((first, count), x, k_ref, v_ref) in enumerate(zip(spans, xs, ks, vs)):
        if n == 0:
            w_loads[1].wait()
        loads[n].wait()
        k = dot(x[...], w[0]).astype(BF16)
        k_ref[...] = k
        if n == 0:
            w_loads[2].wait()
        v = dot(x[...], w[1]).astype(BF16)
        v_ref[...] = v
        for b in range(count):
            block = slice(b * BLK, (b + 1) * BLK)
            for h in range(HEADS):
                before_ref[first + b, h] = running[h].astype(BF16)
            for pair in range(HEADS // 2):
                cols = slice(pair * 2 * HEAD, (pair + 1) * 2 * HEAD)
                outer = dot_t(k[block, cols], v[block, cols])
                running[2 * pair] += outer[:HEAD, :HEAD]
                running[2 * pair + 1] += outer[HEAD:, HEAD:]
    share = HEADS // len(totals)
    for h in range(HEADS):
        for k, total_ref in enumerate(totals):

            @pl.when((lax.axis_index("narrow") + k) % len(totals) == h // share)
            def _(total_ref=total_ref, h=h):
                total_ref[h % share] = running[h].astype(BF16)

    w_loads[0].wait()


def key_value(spans, voxels, w_qkv, cores):
    tokens, width = voxels.shape
    inner = HEADS * HEAD
    hbm = pl.BlockSpec(memory_space=pl.ANY)
    vmem = pl.BlockSpec(memory_space=pltpu.VMEM)
    rows = [count * BLK for _, count in spans]
    out_shape = [jax.ShapeDtypeStruct((n, cols), BF16) for cols in (width, inner, inner) for n in rows]
    out_shape.append(jax.ShapeDtypeStruct((width, inner), BF16))
    out_shape.append(jax.ShapeDtypeStruct((tokens // BLK, HEADS, HEAD, HEAD), BF16))
    out_shape += [jax.ShapeDtypeStruct((HEADS // cores, HEAD, HEAD), BF16)] * cores
    outs = list(
        pl.pallas_call(
            functools.partial(key_value_kernel, spans),
            in_specs=[hbm, hbm],
            out_specs=[vmem] * len(out_shape),
            out_shape=out_shape,
            scratch_shapes=[
                pltpu.VMEM((2, width, inner), BF16),
                pltpu.SemaphoreType.DMA((len(spans) + 3,)),
            ],
            compiler_params=params(KEY_VALUE_KIB),
            name="key_value",
        )(voxels, w_qkv)
    )
    n = len(spans)
    return outs[:n], outs[n : 2 * n], outs[2 * n : 3 * n], outs[3 * n], outs[3 * n + 1], outs[3 * n + 2 :]


def local_kernel(first, count, x_ref, wq_ref, k_ref, v_ref, before_ref, q_ref, part_ref):
    causal = lax.broadcasted_iota(jnp.int32, (BLK, BLK), 0) >= lax.broadcasted_iota(
        jnp.int32, (BLK, BLK), 1
    )
    q = dot(x_ref[...], wq_ref[...]).astype(BF16)
    q_ref[...] = q
    for b in range(count):
        rows = slice(b * BLK, (b + 1) * BLK)
        for h in range(HEADS):
            cols = head_cols(h)
            scores = dot_nt(q[rows, cols], k_ref[rows, cols])
            scores = jnp.where(causal, scores, 0.0).astype(BF16)
            part_ref[rows, cols] = dot(scores, v_ref[rows, cols]) + dot(
                q[rows, cols], before_ref[first + b, h]
            )


def local_attention(x, w_q, k, v, before, first, count):
    rows, width = x.shape
    inner = HEADS * HEAD
    vmem = pl.BlockSpec(memory_space=pltpu.VMEM)
    return pl.pallas_call(
        functools.partial(local_kernel, first, count),
        in_specs=[vmem] * 5,
        out_specs=[vmem] * 2,
        out_shape=[
            jax.ShapeDtypeStruct((rows, inner), BF16),
            jax.ShapeDtypeStruct((rows, inner), F32),
        ],
        compiler_params=params(),
        cost_estimate=pl.CostEstimate(
            flops=2 * rows * inner * (width + 2 * BLK + HEAD),
            bytes_accessed=rows * inner * 12,
            transcendentals=0,
        ),
        name="local_attention",
    )(x, w_q, k, v, before)


def direct_kernel(*refs):
    count = len(refs) // 2 - 1
    xs, (wo_ref, wf_ref), outs = refs[:count], refs[count : count + 2], refs[count + 2 :]
    for x, out in zip(xs, outs):
        out[...] = dot(x[...], wf_ref[...])
    outs[-1][...] = dot(wo_ref[...], wf_ref[...]).astype(BF16)


def direct_features(xs, w_out, w_feature):
    channels = w_feature.shape[1]
    vmem = pl.BlockSpec(memory_space=pltpu.VMEM)
    rows = sum(x.shape[0] for x in xs)
    return pl.pallas_call(
        direct_kernel,
        in_specs=[vmem] * (len(xs) + 2),
        out_specs=[vmem] * (len(xs) + 1),
        out_shape=[jax.ShapeDtypeStruct((x.shape[0], channels), F32) for x in xs]
        + [jax.ShapeDtypeStruct(w_feature.shape, BF16)],
        compiler_params=params(),
        cost_estimate=pl.CostEstimate(
            flops=2 * (rows + w_out.shape[0]) * w_out.shape[1] * channels,
            bytes_accessed=rows * channels * 8,
            transcendentals=0,
        ),
        name="direct_features",
    )(*xs, w_out, w_feature)


def gather_kernel(*refs):
    ins, (running_ref, packed_ref) = refs[:-2], refs[-2:]
    running = sum(ref[...].astype(F32) for ref in ins)
    running_ref[...] = running
    packed_ref[...] = running.astype(BF16)


def earlier_sum(bits, others):
    digit = (lax.axis_index("wide") >> bits[0]) & ((1 << len(bits)) - 1)
    return sum(
        ((digit ^ (k + 1)) < digit).astype(F32) * other for k, other in enumerate(others)
    )


def scan_kernel(bits, count, running_ref, before_ref, *refs):
    others = [ref[...].astype(F32) for ref in refs[:count]]
    new_before, packed, *new_running = refs[count:]
    running = running_ref[...] + sum(others)
    packed[...] = running.astype(BF16)
    for ref in new_running:
        ref[...] = running
    new_before[...] = before_ref[...] + earlier_sum(bits, others)


def spread_kernel(cores, bits, count, before_ref, *refs):
    others = [ref[...].astype(F32) for ref in refs[:count]]
    pieces, outs = refs[count : count + cores], refs[count + cores :]
    place = lax.axis_index("narrow")
    before = before_ref[...] + earlier_sum(bits, others)
    for k, out in enumerate(outs):
        receiver = (place + k) % cores
        value = before
        for j, piece in enumerate(pieces):
            source = (place - j + cores) % cores
            value = value + jnp.where(source < receiver, 1.0, 0.0) * piece[...].astype(F32)
        out[...] = value.astype(BF16)


def small_call(kernel, name, inputs, dtypes, shape):
    vmem = pl.BlockSpec(memory_space=pltpu.VMEM)
    smem = pl.BlockSpec(memory_space=pltpu.SMEM)
    return pl.pallas_call(
        kernel,
        in_specs=[smem if array.dtype == jnp.int32 else vmem for array in inputs],
        out_specs=[vmem] * len(dtypes),
        out_shape=[jax.ShapeDtypeStruct(shape, dtype) for dtype in dtypes],
        compiler_params=params(4 * 1024),
        name=name,
    )(*inputs)


def ones_blocks(width):
    rows, cols = (lax.broadcasted_iota(jnp.int32, (width, width), axis) for axis in range(2))
    return jnp.where(rows // HEAD == cols // HEAD, 1.0, 0.0).astype(BF16)


def block_state(state_ref, scratch):
    scratch[...] = jnp.zeros_like(scratch)
    for j in range(state_ref.shape[0]):
        scratch[head_cols(j), head_cols(j)] = state_ref[j]
    return scratch[...]


def norm_share(q, part, state, ones):
    attended = part + dot(q, state)
    squares = dot((attended * attended).astype(BF16), ones)
    return (attended * lax.rsqrt(squares * (1 / HEAD) + EPS)).astype(BF16)


def share_columns(cores, before):
    width = HEADS // cores * HEAD
    owner = (lax.axis_index("narrow") - before + cores) % cores
    return pl.ds(pl.multiple_of(owner * width, width), width)


def own_share_kernel(cores, state_ref, *refs):
    pieces = len(refs) // 3
    qs, parts, outs, scratch = refs[:pieces], refs[pieces : 2 * pieces], refs[2 * pieces : -1], refs[-1]
    cols = share_columns(cores, 0)
    state, ones = block_state(state_ref, scratch), ones_blocks(scratch.shape[0])
    for q, part, out in zip(qs, parts, outs):
        out[...] = norm_share(q[:, cols], part[:, cols], state, ones)


def own_share(cores, state, qs, parts):
    width = HEADS // cores * HEAD
    vmem = pl.BlockSpec(memory_space=pltpu.VMEM)
    rows = sum(q.shape[0] for q in qs)
    return pl.pallas_call(
        functools.partial(own_share_kernel, cores),
        in_specs=[vmem] * (1 + 2 * len(qs)),
        out_specs=[vmem] * len(qs),
        out_shape=[jax.ShapeDtypeStruct((q.shape[0], width), BF16) for q in qs],
        scratch_shapes=[pltpu.VMEM((width, width), BF16)],
        compiler_params=params(),
        cost_estimate=pl.CostEstimate(
            flops=4 * rows * width * width, bytes_accessed=rows * width * 8, transcendentals=0
        ),
        name="own_share",
    )(state, *qs, *parts)


def list_rows(brick_ref, most, slots, fill):
    for i in range(slots.shape[0]):
        slots[i] = -1
    for b in range(fill.shape[0]):
        fill[b] = 0
    for r in range(brick_ref.shape[0]):
        brick = brick_ref[r] ^ lax.axis_index("wide")
        used = fill[brick]
        slots[brick * most + used] = r
        fill[brick] = used + 1


def cell_numbers(middle):
    number = lax.broadcasted_iota(jnp.int32, (BX * BY // 2, 1), 0)
    if middle:
        return number + 2 * BY
    return number + jnp.where(number < 2 * BY, 0, BX * BY // 2)


def cell_sums(brick, numbers, most, slots, cell_ref, features_ref):
    onehots, rows = [], []
    for j in range(most):
        row = slots[brick * most + j]
        at = jnp.maximum(row, 0)
        match = (numbers == cell_ref[at]) & (row >= 0)
        onehots.append(jnp.where(match, 1.0, 0.0).astype(BF16))
        rows.append(features_ref[pl.ds(pl.multiple_of(at * ROW, ROW), ROW), :])
    return dot(jnp.concatenate(onehots, axis=1), jnp.concatenate(rows, axis=0)).astype(BF16)


def pool_into(outs, brick_ref, cell_ref, features_ref, slots, fill):
    most = slots.shape[0] // fill.shape[0]
    list_rows(brick_ref, most, slots, fill)
    for bricks, middle, out in outs:
        numbers = cell_numbers(middle)
        for n, brick in enumerate(bricks):
            out[n] = cell_sums(brick, numbers, most, slots, cell_ref, features_ref)


def features_kernel(bricks, spans, cores, brick_ref, *refs):
    pieces = len(spans)
    refs = list(refs)
    take = lambda n: [refs.pop(0) for _ in range(n)]
    q_refs, part_refs, normed_refs, own_refs = (take(pieces) for _ in range(4))
    state_refs = take(cores - 1)
    w_ref, cell_ref, features_ref, out = take(4)
    scratch, slots, fill = refs
    shares = [share_columns(cores, k) for k in range(cores)]
    ones = ones_blocks(scratch.shape[1])
    states = [block_state(ref, scratch.at[k]) for k, ref in enumerate(state_refs)]
    for n, (first, count) in enumerate(spans):
        features = own_refs[n][...] + dot(normed_refs[n][...], w_ref[shares[0], :])
        for state, cols in zip(states, shares[1:]):
            normed = norm_share(q_refs[n][:, cols], part_refs[n][:, cols], state, ones)
            features += dot(normed, w_ref[cols, :])
        features_ref[first * BLK : (first + count) * BLK] = features.astype(BF16)
    pool_into([(bricks, False, out)], brick_ref, cell_ref, features_ref, slots, fill)


def list_scratch(count, most):
    return [pltpu.SMEM((count * most,), jnp.int32), pltpu.SMEM((count,), jnp.int32)]


def sums_shape(count, channels):
    return jax.ShapeDtypeStruct((count, BX * BY // 2, channels), BF16)


def voxel_features(
    spans, bricks, qs, parts, normed, own, states, weights, cell_rows, chosen, count, most
):
    tokens, channels = sum(q.shape[0] for q in qs), weights.shape[1]
    cores = len(states) + 1
    width = HEADS // cores * HEAD
    vmem = pl.BlockSpec(memory_space=pltpu.VMEM)
    smem = pl.BlockSpec(memory_space=pltpu.SMEM)
    return pl.pallas_call(
        functools.partial(features_kernel, chosen, spans, cores),
        in_specs=[smem] + [vmem] * (4 * len(spans) + cores + 1),
        out_specs=[vmem] * 2,
        out_shape=[
            jax.ShapeDtypeStruct((tokens, channels), BF16),
            sums_shape(len(chosen), channels),
        ],
        scratch_shapes=[pltpu.VMEM((max(1, cores - 1), width, width), BF16)]
        + list_scratch(count, most),
        compiler_params=params(),
        name="voxel_features",
    )(bricks, *qs, *parts, *normed, *own, *states, weights, cell_rows)


def pool_kernel(chosen, brick_ref, cell_ref, features_ref, *refs):
    outs, (slots, fill) = refs[:-2], refs[-2:]
    pool_into(
        [(bricks, middle, out) for (bricks, middle), out in zip(chosen, outs)],
        brick_ref,
        cell_ref,
        features_ref,
        slots,
        fill,
    )


def pool(bricks, cell_rows, features, chosen, count, most):
    tokens, channels = features.shape
    vmem = pl.BlockSpec(memory_space=pltpu.VMEM)
    smem = pl.BlockSpec(memory_space=pltpu.SMEM)
    return pl.pallas_call(
        functools.partial(pool_kernel, chosen),
        in_specs=[smem, vmem, vmem],
        out_specs=[vmem] * len(chosen),
        out_shape=[sums_shape(len(which), channels) for which, _ in chosen],
        scratch_shapes=list_scratch(count, most),
        compiler_params=params(),
        cost_estimate=pl.CostEstimate(
            flops=sum(len(which) for which, _ in chosen) * most * ROW * BX * BY * channels,
            bytes_accessed=tokens * channels * 2,
            transcendentals=0,
        ),
        name="pool",
    )(bricks, cell_rows, features)


def field_kernel(lines_ref, sides_ref, w1_ref, w2_ref, out_ref, field):
    lines = BX + 4
    wide, narrow = lax.axis_index("wide"), lax.axis_index("narrow")
    first_line, last_line = wide == 0, wide == lax.axis_size("wide") - 1
    first_column, last_column = narrow == 0, narrow == lax.axis_size("narrow") - 1
    for r in range(lines):
        field[r * LINE : r * LINE + GAP] = sides_ref[r]
        field[r * LINE + GAP : (r + 1) * LINE] = lines_ref[r]
    field[lines * LINE :] = sides_ref[lines]

    def convolve(w_ref, start, count):
        lhs = jnp.concatenate(
            [field[start + dy * LINE : start + dy * LINE + count] for dy in (-1, 0, 1)], axis=1
        )
        left, middle, right = [
            dot(lhs, jnp.concatenate([w_ref[dy, dx] for dy in range(3)], axis=0))
            for dx in range(3)
        ]
        return pltpu.roll(left, 1, 0) + middle + pltpu.roll(right, count - 1, 0)

    count = (BX + 2) * LINE + GAP
    inner = jax.nn.gelu(convolve(w1_ref, LINE, count), approximate=True)
    at = lax.broadcasted_iota(jnp.int32, (count, 1), 0)
    outside = first_line & (at <= LINE) | last_line & (at > (BX + 1) * LINE)
    for r in range(BX + 2):
        outside |= first_column & (at == r * LINE + GAP - 1)
        outside |= last_column & (at == (r + 1) * LINE)
    field[LINE : LINE + count] = jnp.where(outside, 0.0, inner).astype(BF16)
    flow = convolve(w2_ref, 2 * LINE, BX * LINE + GAP)
    for r in range(BX):
        out_ref[r] = flow[r * LINE + GAP : (r + 1) * LINE]


def field_flow(lines, left, right, conv_first, conv_second):
    count, _, channels = lines.shape
    vmem = pl.BlockSpec(memory_space=pltpu.VMEM)
    sides = jnp.pad(right, ((1, 0), (0, GAP - 2), (0, 0))) + jnp.pad(
        left, ((0, 1), (GAP - 2, 0), (0, 0))
    )
    return pl.pallas_call(
        field_kernel,
        in_specs=[vmem] * 4,
        out_specs=vmem,
        out_shape=jax.ShapeDtypeStruct((BX, BY, channels), F32),
        scratch_shapes=[pltpu.VMEM((count * LINE + GAP, channels), BF16)],
        compiler_params=params(16 * 1024),
        name="field_flow",
    )(lines, sides, conv_first, conv_second)


def swap(array, axis, bit):
    count = lax.axis_size(axis)
    return lax.ppermute(array, axis, [(i, i ^ (1 << bit)) for i in range(count)])


def swap_digit(array, axis, bit, by):
    count = lax.axis_size(axis)
    return lax.ppermute(array, axis, [(i, i ^ (by << bit)) for i in range(count)])


def shift(array, axis, by):
    count = lax.axis_size(axis)
    return lax.ppermute(
        array, axis, [(i, i + by) for i in range(count) if 0 <= i + by < count]
    )


def rotate(array, axis, by):
    count = lax.axis_size(axis)
    return lax.ppermute(array, axis, [(i, (i + by) % count) for i in range(count)])


def side_columns(lines):
    if lax.axis_size("narrow") != 2:
        return shift(lines[:, BY - 2 :], "narrow", 1), shift(lines[:, :2], "narrow", -1)
    first = lax.axis_index("narrow") == 0
    other = swap(jnp.where(first, lines[:, BY - 2 :], lines[:, :2]), "narrow", 0)
    nothing = jnp.zeros_like(other)
    return jnp.where(first, nothing, other), jnp.where(first, other, nothing)


def exchange_lines(strip):
    groups, count, cores = (lax.axis_size(axis) for axis in ("group", "wide", "narrow"))
    place = lax.axis_index("wide")
    got = []
    for start in range(2):
        pairs = []
        for g in range(groups):
            for w in range(count):
                other = w + 1 if w % 2 == start else w - 1
                far = g
                if not 0 <= other < count:
                    other, far = w, g ^ 1 if groups % 2 == 0 else g
                for c in range(cores):
                    pairs.append(((g * count + w) * cores + c, (far * count + other) * cores + c))
        upper = place % 2 == start
        out = jnp.where(upper, strip[2:], strip[:2])
        got.append(lax.ppermute(out, ("group", "wide", "narrow"), pairs))
    above = jnp.where(place % 2 == 1, got[0], got[1])
    below = jnp.where(place % 2 == 1, got[1], got[0])
    above = jnp.where(place > 0, above, jnp.zeros_like(above))
    below = jnp.where(place < count - 1, below, jnp.zeros_like(below))
    return above, below


def earlier_state(totals, first_work, works):
    cores, shape = len(totals), totals[0].shape
    works, done = list(works), []

    def beside(work, arrays, exchange):
        held, arrays = work(arrays)
        done.append(held)
        held, arrived = lax.optimization_barrier((held, exchange(arrays)))
        done[-1] = held
        return arrived

    others = beside(
        first_work,
        totals[1:],
        lambda arrays: [rotate(array, "narrow", k + 1) for k, array in enumerate(arrays)],
    )
    pieces = [totals[0]] + others
    running, packed = small_call(gather_kernel, "gather", pieces, [F32, BF16], shape)
    before = jnp.zeros(shape, F32)
    count = lax.axis_size("wide").bit_length() - 1
    levels = [list(range(bit, min(bit + 2, count))) for bit in range(0, count, 2)]
    for level, bits in enumerate(levels):
        exchange = lambda packed: [
            swap_digit(packed, "wide", bits[0], k) for k in range(1, 1 << len(bits))
        ]
        others = beside(works.pop(0), packed, exchange) if works else exchange(packed)
        if level == len(levels) - 1:
            break
        before, packed, *more = small_call(
            functools.partial(scan_kernel, bits, len(others)),
            "scan",
            [running, before] + others,
            [F32, BF16] + [F32] * (level < len(levels) - 2),
            shape,
        )
        running = more[0] if more else None
    outs = small_call(
        functools.partial(spread_kernel, cores, bits, len(others)),
        "spread",
        [before] + others + pieces,
        [BF16] * cores,
        shape,
    )
    states = [outs[0]] + [rotate(outs[k], "narrow", k) for k in range(1, cores)]
    while works:
        done.append(works.pop(0)(outs[0])[0])
    return states, done


def split_order(order):
    half = 1 << (len(order) - 1)
    place = lambda slot: sum(
        ((slot >> (len(order) - 1 - i)) & 1) << bit for i, bit in enumerate(order)
    )
    return [place(slot) for slot in range(half)], [place(slot) for slot in range(half, 2 * half)]


def reduce_bricks(parts, orders):
    parts = [list(pair) for pair in parts]
    for level in range(len(orders[0])):
        arrived = [
            swap(gone, "wide", order[level]) for (_, gone), order in zip(parts, orders)
        ]
        for pair, more in zip(parts, arrived):
            total = (pair[0].astype(F32) + more.astype(F32)).astype(BF16)
            half = total.shape[0] // 2
            pair[0], pair[1] = total[:half] if half else total, total[half:]
    return [pair[0] if pair[0].shape[0] else pair[1] for pair in parts]


def per_device(voxels, w_qkv, w_out, w_feature, conv_first, conv_second, row_brick, cell_place):
    tokens = voxels.shape[0]
    channels = w_feature.shape[1]
    wide_count, wide_place = lax.axis_size("wide"), lax.axis_index("wide")
    narrow_count, narrow_place = lax.axis_size("narrow"), lax.axis_index("narrow")

    blocks = tokens // BLK
    cuts = sorted({blocks * i // 2 for i in range(3)})
    spans = [(first, last - first) for first, last in zip(cuts, cuts[1:])]
    xs, ks, vs, w_q, before, totals = key_value(spans, voxels, w_qkv, narrow_count)

    def direct(arrays):
        arrays, x = lax.optimization_barrier((arrays, xs[0]))
        return direct_features([x] + xs[1:], w_out, w_feature), arrays

    def work(n):
        def run(array):
            array, k = lax.optimization_barrier((array, ks[n]))
            return local_attention(xs[n], w_q, k, vs[n], before, *spans[n]), array

        return run

    states, done = earlier_state(totals, direct, [work(n) for n in range(len(spans))])
    own, weights = done[0][:-1], done[0][-1]
    qs, parts = ([piece[i] for piece in done[1:]] for i in range(2))
    normed = own_share(narrow_count, states[0], qs, parts)

    bits = list(range(wide_count.bit_length() - 1))
    orders = [bits, bits[1::-1] + bits[2:]]
    sides = [split_order(order) for order in orders]
    cell_rows = cell_place.reshape(-1, 1, ROW)
    most = max(2, 2 * (tokens // ROW) // wide_count)
    bricks = row_brick[:, 0]
    features, outer_goes = voxel_features(
        spans, bricks, qs, parts, normed, own, states[1:], weights, cell_rows, sides[0][1], wide_count, most
    )
    (middle_goes,) = pool(bricks, cell_rows, features, [(sides[1][1], True)], wide_count, most)
    outer_stays, middle_stays = pool(
        bricks, cell_rows, features, [(sides[0][0], False), (sides[1][0], True)], wide_count, most
    )
    outer, middle = reduce_bricks(
        [(outer_stays, outer_goes), (middle_stays, middle_goes)], orders
    )
    outer, middle = (part.reshape(-1, BY, channels) for part in (outer, middle))
    above, below = exchange_lines(outer)
    lines = jnp.concatenate([above, outer[:2], middle, outer[2:], below], axis=0)
    left, right = side_columns(lines)
    return field_flow(lines, left, right, conv_first, conv_second)


def solution(mesh):
    placed = (
        P(("group", "wide", "narrow"), None),
        P(),
        P(),
        P(),
        P(),
        P(),
        P(("group", "wide", "narrow"), None),
        P(("group", "wide", "narrow")),
    )
    return jax.shard_map(
        per_device,
        mesh=mesh,
        in_specs=placed,
        out_specs=P(("group", "wide"), "narrow", None),
        check_vma=False,
    )
```

```python
import functools

import jax
import jax.numpy as jnp
from jax import lax
from jax.experimental import pallas as pl
from jax.experimental.pallas import tpu as pltpu
from jax.sharding import PartitionSpec as P

HEADS = 4
HEAD = 128
ROW = 128
BLK = 256
BX = 8
BY = 32
EPS = 1e-06
GAP = 16
LINE = GAP + BY

F32 = jnp.float32
BF16 = jnp.bfloat16


def dot(a, b):
    return jnp.dot(a, b, preferred_element_type=F32)


def dot_t(a, b):
    return lax.dot_general(a, b, (((0,), (0,)), ((), ())), preferred_element_type=F32)


def dot_nt(a, b):
    return lax.dot_general(a, b, (((1,), (1,)), ((), ())), preferred_element_type=F32)


KEY_VALUE_KIB = 46592


def params(kib=24 * 1024):
    return pltpu.CompilerParams(vmem_limit_bytes=kib << 10)


def head_cols(h):
    return slice(h * HEAD, (h + 1) * HEAD)


def key_value_kernel(spans, x_ref, w_ref, *refs):
    refs = list(refs)
    take = lambda n: [refs.pop(0) for _ in range(n)]
    xs, ks, vs = take(len(spans)), take(len(spans)), take(len(spans))
    wq, before_ref = take(2)
    totals, (w, sems) = refs[:-2], refs[-2:]
    inner = HEADS * HEAD

    def columns(part, target):
        return pltpu.make_async_copy(
            w_ref.at[:, pl.ds(part * inner, inner)], target, sems.at[len(spans) + part]
        )

    loads = [
        pltpu.make_async_copy(x_ref.at[pl.ds(first * BLK, count * BLK)], x, sems.at[n])
        for n, ((first, count), x) in enumerate(zip(spans, xs))
    ]
    w_loads = [columns(0, wq), columns(1, w.at[0]), columns(2, w.at[1])]
    w_loads[1].start()
    loads[0].start()
    w_loads[2].start()
    for load in loads[1:]:
        load.start()
    w_loads[0].start()
    running = [jnp.zeros((HEAD, HEAD), F32) for _ in range(HEADS)]
    for n, ((first, count), x, k_ref, v_ref) in enumerate(zip(spans, xs, ks, vs)):
        if n == 0:
            w_loads[1].wait()
        loads[n].wait()
        k = dot(x[...], w[0]).astype(BF16)
        k_ref[...] = k
        if n == 0:
            w_loads[2].wait()
        v = dot(x[...], w[1]).astype(BF16)
        v_ref[...] = v
        for b in range(count):
            block = slice(b * BLK, (b + 1) * BLK)
            for h in range(HEADS):
                before_ref[first + b, h] = running[h].astype(BF16)
            for pair in range(HEADS // 2):
                cols = slice(pair * 2 * HEAD, (pair + 1) * 2 * HEAD)
                outer = dot_t(k[block, cols], v[block, cols])
                running[2 * pair] += outer[:HEAD, :HEAD]
                running[2 * pair + 1] += outer[HEAD:, HEAD:]
    share = HEADS // len(totals)
    for h in range(HEADS):
        for k, total_ref in enumerate(totals):

            @pl.when((lax.axis_index("narrow") + k) % len(totals) == h // share)
            def _(total_ref=total_ref, h=h):
                total_ref[h % share] = running[h].astype(BF16)

    w_loads[0].wait()


def key_value(spans, voxels, w_qkv, cores):
    tokens, width = voxels.shape
    inner = HEADS * HEAD
    hbm = pl.BlockSpec(memory_space=pl.ANY)
    vmem = pl.BlockSpec(memory_space=pltpu.VMEM)
    rows = [count * BLK for _, count in spans]
    out_shape = [jax.ShapeDtypeStruct((n, cols), BF16) for cols in (width, inner, inner) for n in rows]
    out_shape.append(jax.ShapeDtypeStruct((width, inner), BF16))
    out_shape.append(jax.ShapeDtypeStruct((tokens // BLK, HEADS, HEAD, HEAD), BF16))
    out_shape += [jax.ShapeDtypeStruct((HEADS // cores, HEAD, HEAD), BF16)] * cores
    outs = list(
        pl.pallas_call(
            functools.partial(key_value_kernel, spans),
            in_specs=[hbm, hbm],
            out_specs=[vmem] * len(out_shape),
            out_shape=out_shape,
            scratch_shapes=[
                pltpu.VMEM((2, width, inner), BF16),
                pltpu.SemaphoreType.DMA((len(spans) + 3,)),
            ],
            compiler_params=params(KEY_VALUE_KIB),
            name="key_value",
        )(voxels, w_qkv)
    )
    n = len(spans)
    return outs[:n], outs[n : 2 * n], outs[2 * n : 3 * n], outs[3 * n], outs[3 * n + 1], outs[3 * n + 2 :]


def local_kernel(first, count, x_ref, wq_ref, k_ref, v_ref, before_ref, q_ref, part_ref):
    causal = lax.broadcasted_iota(jnp.int32, (BLK, BLK), 0) >= lax.broadcasted_iota(
        jnp.int32, (BLK, BLK), 1
    )
    q = dot(x_ref[...], wq_ref[...]).astype(BF16)
    q_ref[...] = q
    for b in range(count):
        rows = slice(b * BLK, (b + 1) * BLK)
        for h in range(HEADS):
            cols = head_cols(h)
            scores = dot_nt(q[rows, cols], k_ref[rows, cols])
            scores = jnp.where(causal, scores, 0.0).astype(BF16)
            part_ref[rows, cols] = dot(scores, v_ref[rows, cols]) + dot(
                q[rows, cols], before_ref[first + b, h]
            )


def local_attention(x, w_q, k, v, before, first, count):
    rows, width = x.shape
    inner = HEADS * HEAD
    vmem = pl.BlockSpec(memory_space=pltpu.VMEM)
    return pl.pallas_call(
        functools.partial(local_kernel, first, count),
        in_specs=[vmem] * 5,
        out_specs=[vmem] * 2,
        out_shape=[
            jax.ShapeDtypeStruct((rows, inner), BF16),
            jax.ShapeDtypeStruct((rows, inner), F32),
        ],
        compiler_params=params(),
        cost_estimate=pl.CostEstimate(
            flops=2 * rows * inner * (width + 2 * BLK + HEAD),
            bytes_accessed=rows * inner * 12,
            transcendentals=0,
        ),
        name="local_attention",
    )(x, w_q, k, v, before)


def direct_kernel(*refs):
    count = len(refs) // 2 - 1
    xs, (wo_ref, wf_ref), outs = refs[:count], refs[count : count + 2], refs[count + 2 :]
    for x, out in zip(xs, outs):
        out[...] = dot(x[...], wf_ref[...])
    outs[-1][...] = dot(wo_ref[...], wf_ref[...]).astype(BF16)


def direct_features(xs, w_out, w_feature):
    channels = w_feature.shape[1]
    vmem = pl.BlockSpec(memory_space=pltpu.VMEM)
    rows = sum(x.shape[0] for x in xs)
    return pl.pallas_call(
        direct_kernel,
        in_specs=[vmem] * (len(xs) + 2),
        out_specs=[vmem] * (len(xs) + 1),
        out_shape=[jax.ShapeDtypeStruct((x.shape[0], channels), F32) for x in xs]
        + [jax.ShapeDtypeStruct(w_feature.shape, BF16)],
        compiler_params=params(),
        cost_estimate=pl.CostEstimate(
            flops=2 * (rows + w_out.shape[0]) * w_out.shape[1] * channels,
            bytes_accessed=rows * channels * 8,
            transcendentals=0,
        ),
        name="direct_features",
    )(*xs, w_out, w_feature)


def gather_kernel(*refs):
    ins, (running_ref, packed_ref) = refs[:-2], refs[-2:]
    running = sum(ref[...].astype(F32) for ref in ins)
    running_ref[...] = running
    packed_ref[...] = running.astype(BF16)


def earlier_sum(bits, others):
    digit = (lax.axis_index("wide") >> bits[0]) & ((1 << len(bits)) - 1)
    return sum(
        ((digit ^ (k + 1)) < digit).astype(F32) * other for k, other in enumerate(others)
    )


def scan_kernel(bits, count, running_ref, before_ref, *refs):
    others = [ref[...].astype(F32) for ref in refs[:count]]
    new_before, packed, *new_running = refs[count:]
    running = running_ref[...] + sum(others)
    packed[...] = running.astype(BF16)
    for ref in new_running:
        ref[...] = running
    new_before[...] = before_ref[...] + earlier_sum(bits, others)


def spread_kernel(cores, bits, count, before_ref, *refs):
    others = [ref[...].astype(F32) for ref in refs[:count]]
    pieces, outs = refs[count : count + cores], refs[count + cores :]
    place = lax.axis_index("narrow")
    before = before_ref[...] + earlier_sum(bits, others)
    for k, out in enumerate(outs):
        receiver = (place + k) % cores
        value = before
        for j, piece in enumerate(pieces):
            source = (place - j + cores) % cores
            value = value + jnp.where(source < receiver, 1.0, 0.0) * piece[...].astype(F32)
        out[...] = value.astype(BF16)


def small_call(kernel, name, inputs, dtypes, shape):
    vmem = pl.BlockSpec(memory_space=pltpu.VMEM)
    smem = pl.BlockSpec(memory_space=pltpu.SMEM)
    return pl.pallas_call(
        kernel,
        in_specs=[smem if array.dtype == jnp.int32 else vmem for array in inputs],
        out_specs=[vmem] * len(dtypes),
        out_shape=[jax.ShapeDtypeStruct(shape, dtype) for dtype in dtypes],
        compiler_params=params(4 * 1024),
        name=name,
    )(*inputs)


def ones_blocks(width):
    rows, cols = (lax.broadcasted_iota(jnp.int32, (width, width), axis) for axis in range(2))
    return jnp.where(rows // HEAD == cols // HEAD, 1.0, 0.0).astype(BF16)


def block_state(state_ref, scratch):
    scratch[...] = jnp.zeros_like(scratch)
    for j in range(state_ref.shape[0]):
        scratch[head_cols(j), head_cols(j)] = state_ref[j]
    return scratch[...]


def norm_share(q, part, state, ones):
    attended = part + dot(q, state)
    squares = dot((attended * attended).astype(BF16), ones)
    return (attended * lax.rsqrt(squares * (1 / HEAD) + EPS)).astype(BF16)


def share_columns(cores, before):
    width = HEADS // cores * HEAD
    owner = (lax.axis_index("narrow") - before + cores) % cores
    return pl.ds(pl.multiple_of(owner * width, width), width)


def own_share_kernel(cores, state_ref, w_ref, *refs):
    pieces = len(refs) // 4
    qs, parts, direct, outs = (refs[i * pieces : (i + 1) * pieces] for i in range(4))
    scratch = refs[-1]
    cols = share_columns(cores, 0)
    state, ones = block_state(state_ref, scratch), ones_blocks(scratch.shape[0])
    for q, part, start, out in zip(qs, parts, direct, outs):
        normed = norm_share(q[:, cols], part[:, cols], state, ones)
        out[...] = start[...] + dot(normed, w_ref[cols, :])


def own_share(cores, state, weights, qs, parts, direct):
    width = HEADS // cores * HEAD
    vmem = pl.BlockSpec(memory_space=pltpu.VMEM)
    rows = sum(q.shape[0] for q in qs)
    return pl.pallas_call(
        functools.partial(own_share_kernel, cores),
        in_specs=[vmem] * (2 + 3 * len(qs)),
        out_specs=[vmem] * len(qs),
        out_shape=[jax.ShapeDtypeStruct(start.shape, F32) for start in direct],
        scratch_shapes=[pltpu.VMEM((width, width), BF16)],
        compiler_params=params(),
        cost_estimate=pl.CostEstimate(
            flops=6 * rows * width * width, bytes_accessed=rows * width * 8, transcendentals=0
        ),
        name="own_share",
    )(state, weights, *qs, *parts, *direct)


def list_rows(brick_ref, most, slots, fill):
    for i in range(slots.shape[0]):
        slots[i] = -1
    for b in range(fill.shape[0]):
        fill[b] = 0
    for r in range(brick_ref.shape[0]):
        brick = brick_ref[r] ^ lax.axis_index("wide")
        used = fill[brick]
        slots[brick * most + used] = r
        fill[brick] = used + 1


def cell_numbers(middle):
    number = lax.broadcasted_iota(jnp.int32, (BX * BY // 2, 1), 0)
    if middle:
        return number + 2 * BY
    return number + jnp.where(number < 2 * BY, 0, BX * BY // 2)


def cell_sums(brick, numbers, most, slots, cell_ref, features_ref):
    onehots, rows = [], []
    for j in range(most):
        row = slots[brick * most + j]
        at = jnp.maximum(row, 0)
        match = (numbers == cell_ref[at]) & (row >= 0)
        onehots.append(jnp.where(match, 1.0, 0.0).astype(BF16))
        rows.append(features_ref[pl.ds(pl.multiple_of(at * ROW, ROW), ROW), :])
    return dot(jnp.concatenate(onehots, axis=1), jnp.concatenate(rows, axis=0)).astype(BF16)


def pool_into(outs, brick_ref, cell_ref, features_ref, slots, fill):
    most = slots.shape[0] // fill.shape[0]
    list_rows(brick_ref, most, slots, fill)
    for bricks, middle, out in outs:
        numbers = cell_numbers(middle)
        for n, brick in enumerate(bricks):
            out[n] = cell_sums(brick, numbers, most, slots, cell_ref, features_ref)


def features_kernel(bricks, spans, cores, brick_ref, *refs):
    pieces = len(spans)
    refs = list(refs)
    take = lambda n: [refs.pop(0) for _ in range(n)]
    q_refs, part_refs, own_refs = (take(pieces) for _ in range(3))
    state_refs = take(cores - 1)
    w_ref, cell_ref, features_ref, out = take(4)
    scratch, slots, fill = refs
    shares = [share_columns(cores, k) for k in range(cores)]
    ones = ones_blocks(scratch.shape[1])
    states = [block_state(ref, scratch.at[k]) for k, ref in enumerate(state_refs)]
    for n, (first, count) in enumerate(spans):
        features = own_refs[n][...]
        for state, cols in zip(states, shares[1:]):
            normed = norm_share(q_refs[n][:, cols], part_refs[n][:, cols], state, ones)
            features += dot(normed, w_ref[cols, :])
        features_ref[first * BLK : (first + count) * BLK] = features.astype(BF16)
    pool_into([(bricks, False, out)], brick_ref, cell_ref, features_ref, slots, fill)


def list_scratch(count, most):
    return [pltpu.SMEM((count * most,), jnp.int32), pltpu.SMEM((count,), jnp.int32)]


def sums_shape(count, channels):
    return jax.ShapeDtypeStruct((count, BX * BY // 2, channels), BF16)


def voxel_features(
    spans, bricks, qs, parts, own, states, weights, cell_rows, chosen, count, most
):
    tokens, channels = sum(q.shape[0] for q in qs), weights.shape[1]
    cores = len(states) + 1
    width = HEADS // cores * HEAD
    vmem = pl.BlockSpec(memory_space=pltpu.VMEM)
    smem = pl.BlockSpec(memory_space=pltpu.SMEM)
    return pl.pallas_call(
        functools.partial(features_kernel, chosen, spans, cores),
        in_specs=[smem] + [vmem] * (3 * len(spans) + cores + 1),
        out_specs=[vmem] * 2,
        out_shape=[
            jax.ShapeDtypeStruct((tokens, channels), BF16),
            sums_shape(len(chosen), channels),
        ],
        scratch_shapes=[pltpu.VMEM((max(1, cores - 1), width, width), BF16)]
        + list_scratch(count, most),
        compiler_params=params(),
        name="voxel_features",
    )(bricks, *qs, *parts, *own, *states, weights, cell_rows)


def pool_kernel(chosen, brick_ref, cell_ref, features_ref, *refs):
    outs, (slots, fill) = refs[:-2], refs[-2:]
    pool_into(
        [(bricks, middle, out) for (bricks, middle), out in zip(chosen, outs)],
        brick_ref,
        cell_ref,
        features_ref,
        slots,
        fill,
    )


def pool(bricks, cell_rows, features, chosen, count, most):
    tokens, channels = features.shape
    vmem = pl.BlockSpec(memory_space=pltpu.VMEM)
    smem = pl.BlockSpec(memory_space=pltpu.SMEM)
    return pl.pallas_call(
        functools.partial(pool_kernel, chosen),
        in_specs=[smem, vmem, vmem],
        out_specs=[vmem] * len(chosen),
        out_shape=[sums_shape(len(which), channels) for which, _ in chosen],
        scratch_shapes=list_scratch(count, most),
        compiler_params=params(),
        cost_estimate=pl.CostEstimate(
            flops=sum(len(which) for which, _ in chosen) * most * ROW * BX * BY * channels,
            bytes_accessed=tokens * channels * 2,
            transcendentals=0,
        ),
        name="pool",
    )(bricks, cell_rows, features)


def field_kernel(lines_ref, sides_ref, w1_ref, w2_ref, out_ref, field):
    lines = BX + 4
    wide, narrow = lax.axis_index("wide"), lax.axis_index("narrow")
    first_line, last_line = wide == 0, wide == lax.axis_size("wide") - 1
    first_column, last_column = narrow == 0, narrow == lax.axis_size("narrow") - 1
    for r in range(lines):
        field[r * LINE : r * LINE + GAP] = sides_ref[r]
        field[r * LINE + GAP : (r + 1) * LINE] = lines_ref[r]
    field[lines * LINE :] = sides_ref[lines]

    def convolve(w_ref, start, count):
        lhs = jnp.concatenate(
            [field[start + dy * LINE : start + dy * LINE + count] for dy in (-1, 0, 1)], axis=1
        )
        left, middle, right = [
            dot(lhs, jnp.concatenate([w_ref[dy, dx] for dy in range(3)], axis=0))
            for dx in range(3)
        ]
        return pltpu.roll(left, 1, 0) + middle + pltpu.roll(right, count - 1, 0)

    count = (BX + 2) * LINE + GAP
    inner = jax.nn.gelu(convolve(w1_ref, LINE, count), approximate=True)
    at = lax.broadcasted_iota(jnp.int32, (count, 1), 0)
    outside = first_line & (at <= LINE) | last_line & (at > (BX + 1) * LINE)
    for r in range(BX + 2):
        outside |= first_column & (at == r * LINE + GAP - 1)
        outside |= last_column & (at == (r + 1) * LINE)
    field[LINE : LINE + count] = jnp.where(outside, 0.0, inner).astype(BF16)
    flow = convolve(w2_ref, 2 * LINE, BX * LINE + GAP)
    for r in range(BX):
        out_ref[r] = flow[r * LINE + GAP : (r + 1) * LINE]


def field_flow(lines, left, right, conv_first, conv_second):
    count, _, channels = lines.shape
    vmem = pl.BlockSpec(memory_space=pltpu.VMEM)
    sides = jnp.pad(right, ((1, 0), (0, GAP - 2), (0, 0))) + jnp.pad(
        left, ((0, 1), (GAP - 2, 0), (0, 0))
    )
    return pl.pallas_call(
        field_kernel,
        in_specs=[vmem] * 4,
        out_specs=vmem,
        out_shape=jax.ShapeDtypeStruct((BX, BY, channels), F32),
        scratch_shapes=[pltpu.VMEM((count * LINE + GAP, channels), BF16)],
        compiler_params=params(16 * 1024),
        name="field_flow",
    )(lines, sides, conv_first, conv_second)


def swap(array, axis, bit):
    count = lax.axis_size(axis)
    return lax.ppermute(array, axis, [(i, i ^ (1 << bit)) for i in range(count)])


def swap_digit(array, axis, bit, by):
    count = lax.axis_size(axis)
    return lax.ppermute(array, axis, [(i, i ^ (by << bit)) for i in range(count)])


def shift(array, axis, by):
    count = lax.axis_size(axis)
    return lax.ppermute(
        array, axis, [(i, i + by) for i in range(count) if 0 <= i + by < count]
    )


def rotate(array, axis, by):
    count = lax.axis_size(axis)
    return lax.ppermute(array, axis, [(i, (i + by) % count) for i in range(count)])


def side_columns(lines):
    if lax.axis_size("narrow") != 2:
        return shift(lines[:, BY - 2 :], "narrow", 1), shift(lines[:, :2], "narrow", -1)
    first = lax.axis_index("narrow") == 0
    other = swap(jnp.where(first, lines[:, BY - 2 :], lines[:, :2]), "narrow", 0)
    nothing = jnp.zeros_like(other)
    return jnp.where(first, nothing, other), jnp.where(first, other, nothing)


def exchange_lines(strip, with_it):
    groups, count, cores = (lax.axis_size(axis) for axis in ("group", "wide", "narrow"))
    place = lax.axis_index("wide")
    got = []
    for start in range(2):
        pairs = []
        for g in range(groups):
            for w in range(count):
                other = w + 1 if w % 2 == start else w - 1
                far = g
                if not 0 <= other < count:
                    other, far = w, g ^ 1 if groups % 2 == 0 else g
                for c in range(cores):
                    pairs.append(((g * count + w) * cores + c, (far * count + other) * cores + c))
        upper = place % 2 == start
        out = jnp.where(upper, strip[2:], strip[:2])
        got.append(lax.ppermute(out, ("group", "wide", "narrow"), pairs))
    got, with_it = lax.optimization_barrier((got, with_it))
    above = jnp.where(place % 2 == 1, got[0], got[1])
    below = jnp.where(place % 2 == 1, got[1], got[0])
    above = jnp.where(place > 0, above, jnp.zeros_like(above))
    below = jnp.where(place < count - 1, below, jnp.zeros_like(below))
    return above, below, with_it


def earlier_state(totals, first_work, works):
    cores, shape = len(totals), totals[0].shape
    works, done = list(works), []

    def beside(work, arrays, exchange):
        held, arrays = work(arrays)
        done.append(held)
        held, arrived = lax.optimization_barrier((held, exchange(arrays)))
        done[-1] = held
        return arrived

    others = beside(
        first_work,
        totals[1:],
        lambda arrays: [rotate(array, "narrow", k + 1) for k, array in enumerate(arrays)],
    )
    pieces = [totals[0]] + others
    running, packed = small_call(gather_kernel, "gather", pieces, [F32, BF16], shape)
    before = jnp.zeros(shape, F32)
    count = lax.axis_size("wide").bit_length() - 1
    levels = [list(range(bit, min(bit + 2, count))) for bit in range(0, count, 2)]
    for level, bits in enumerate(levels):
        exchange = lambda packed: [
            swap_digit(packed, "wide", bits[0], k) for k in range(1, 1 << len(bits))
        ]
        others = beside(works.pop(0), packed, exchange) if works else exchange(packed)
        if level == len(levels) - 1:
            break
        before, packed, *more = small_call(
            functools.partial(scan_kernel, bits, len(others)),
            "scan",
            [running, before] + others,
            [F32, BF16] + [F32] * (level < len(levels) - 2),
            shape,
        )
        running = more[0] if more else None
    outs = small_call(
        functools.partial(spread_kernel, cores, bits, len(others)),
        "spread",
        [before] + others + pieces,
        [BF16] * cores,
        shape,
    )
    states = [outs[0]] + [rotate(outs[k], "narrow", k) for k in range(1, cores)]
    while works:
        done.append(works.pop(0)(outs[0])[0])
    return states, done


def split_order(order):
    half = 1 << (len(order) - 1)
    place = lambda slot: sum(
        ((slot >> (len(order) - 1 - i)) & 1) << bit for i, bit in enumerate(order)
    )
    return [place(slot) for slot in range(half)], [place(slot) for slot in range(half, 2 * half)]


def reduce_level(stays, goes, bit, with_it=None):
    arrived = [swap(array, "wide", bit) for array in reversed(goes)][::-1]
    if with_it is not None:
        arrived, with_it = lax.optimization_barrier((arrived, with_it))
    sums = [
        (here.astype(F32) + more.astype(F32)).astype(BF16) for here, more in zip(stays, arrived)
    ]
    return sums, with_it


def next_level(sums):
    if len(sums) == 1:
        half = sums[0].shape[0] // 2
        return [sums[0][:half]], [sums[0][half:]]
    return sums[:1], sums[1:]


def reduce_both(outer, middle, orders):
    levels = len(orders[0])
    for level in range(levels):
        if level > 0:
            middle_sums, _ = reduce_level(*middle, orders[1][level - 1])
            middle = next_level(middle_sums)
        if level > 1:
            outer_sums, middle = reduce_level(*outer, orders[0][level], middle)
        else:
            outer_sums, _ = reduce_level(*outer, orders[0][level])
        outer = next_level(outer_sums)
    return outer_sums[0][0], reduce_level(*middle, orders[1][-1])[0][0][0]


def per_device(voxels, w_qkv, w_out, w_feature, conv_first, conv_second, row_brick, cell_place):
    tokens = voxels.shape[0]
    channels = w_feature.shape[1]
    wide_count, wide_place = lax.axis_size("wide"), lax.axis_index("wide")
    narrow_count, narrow_place = lax.axis_size("narrow"), lax.axis_index("narrow")

    blocks = tokens // BLK
    cuts = sorted({blocks * i // 2 for i in range(3)})
    spans = [(first, last - first) for first, last in zip(cuts, cuts[1:])]
    xs, ks, vs, w_q, before, totals = key_value(spans, voxels, w_qkv, narrow_count)

    def direct(arrays):
        arrays, x = lax.optimization_barrier((arrays, xs[0]))
        return direct_features([x] + xs[1:], w_out, w_feature), arrays

    def work(n):
        def run(array):
            array, k = lax.optimization_barrier((array, ks[n]))
            return local_attention(xs[n], w_q, k, vs[n], before, *spans[n]), array

        return run

    states, done = earlier_state(totals, direct, [work(n) for n in range(len(spans))])
    own, weights = done[0][:-1], done[0][-1]
    qs, parts = ([piece[i] for piece in done[1:]] for i in range(2))
    own = own_share(narrow_count, states[0], weights, qs, parts, own)

    bits = list(range(wide_count.bit_length() - 1))
    orders = [bits, bits[1::-1] + bits[2:]]
    halves = lambda places: (places[: len(places) // 2], places[len(places) // 2 :])
    stay, go = zip(*(map(halves, split_order(order)) for order in orders))
    cell_rows = cell_place.reshape(-1, 1, ROW)
    most = max(2, 2 * (tokens // ROW) // wide_count)
    bricks = row_brick[:, 0]
    features, outer_first = voxel_features(
        spans, bricks, qs, parts, own, states[1:], weights, cell_rows, go[0][1], wide_count, most
    )
    pooled = lambda *chosen: pool(bricks, cell_rows, features, chosen, wide_count, most)
    (middle_first,) = pooled((go[1][1], True))
    outer_later, middle_later = pooled((go[0][0], False), (go[1][0], True))
    sums = pooled(*((stay[middle][n], middle == 1) for middle in range(2) for n in range(2)))
    outer, middle = reduce_both(
        (sums[:2], [outer_later, outer_first]), (sums[2:], [middle_later, middle_first]), orders
    )
    outer, middle = (part.reshape(-1, BY, channels) for part in (outer, middle))
    above, below, middle = exchange_lines(outer, middle)
    lines = jnp.concatenate([above, outer[:2], middle, outer[2:], below], axis=0)
    left, right = side_columns(lines)
    return field_flow(lines, left, right, conv_first, conv_second)


def solution(mesh):
    placed = (
        P(("group", "wide", "narrow"), None),
        P(),
        P(),
        P(),
        P(),
        P(),
        P(("group", "wide", "narrow"), None),
        P(("group", "wide", "narrow")),
    )
    return jax.shard_map(
        per_device,
        mesh=mesh,
        in_specs=placed,
        out_specs=P(("group", "wide"), "narrow", None),
        check_vma=False,
    )
```

```python
import functools

import jax
import jax.numpy as jnp
from jax import lax
from jax.experimental import pallas as pl
from jax.experimental.pallas import tpu as pltpu
from jax.sharding import PartitionSpec as P

HEADS = 4
HEAD = 128
ROW = 128
BLK = 256
BX = 8
BY = 32
EPS = 1e-06
GAP = 16
LINE = GAP + BY

F32 = jnp.float32
BF16 = jnp.bfloat16


def dot(a, b):
    return jnp.dot(a, b, preferred_element_type=F32)


def dot_t(a, b):
    return lax.dot_general(a, b, (((0,), (0,)), ((), ())), preferred_element_type=F32)


def dot_nt(a, b):
    return lax.dot_general(a, b, (((1,), (1,)), ((), ())), preferred_element_type=F32)


KEY_VALUE_KIB = 46592


def params(kib=24 * 1024):
    return pltpu.CompilerParams(vmem_limit_bytes=kib << 10)


def head_cols(h):
    return slice(h * HEAD, (h + 1) * HEAD)


def key_value_kernel(spans, x_ref, w_ref, *refs):
    refs = list(refs)
    take = lambda n: [refs.pop(0) for _ in range(n)]
    xs, ks, vs = take(len(spans)), take(len(spans)), take(len(spans))
    wq, before_ref = take(2)
    totals, (w, sems) = refs[:-2], refs[-2:]
    inner = HEADS * HEAD

    def columns(part, target):
        return pltpu.make_async_copy(
            w_ref.at[:, pl.ds(part * inner, inner)], target, sems.at[len(spans) + part]
        )

    loads = [
        pltpu.make_async_copy(x_ref.at[pl.ds(first * BLK, count * BLK)], x, sems.at[n])
        for n, ((first, count), x) in enumerate(zip(spans, xs))
    ]
    w_loads = [columns(0, wq), columns(1, w.at[0]), columns(2, w.at[1])]
    w_loads[1].start()
    loads[0].start()
    w_loads[2].start()
    for load in loads[1:]:
        load.start()
    w_loads[0].start()
    running = [jnp.zeros((HEAD, HEAD), F32) for _ in range(HEADS)]
    for n, ((first, count), x, k_ref, v_ref) in enumerate(zip(spans, xs, ks, vs)):
        if n == 0:
            w_loads[1].wait()
        loads[n].wait()
        k = dot(x[...], w[0]).astype(BF16)
        k_ref[...] = k
        if n == 0:
            w_loads[2].wait()
        v = dot(x[...], w[1]).astype(BF16)
        v_ref[...] = v
        for b in range(count):
            block = slice(b * BLK, (b + 1) * BLK)
            for h in range(HEADS):
                before_ref[first + b, h] = running[h].astype(BF16)
            for pair in range(HEADS // 2):
                cols = slice(pair * 2 * HEAD, (pair + 1) * 2 * HEAD)
                outer = dot_t(k[block, cols], v[block, cols])
                running[2 * pair] += outer[:HEAD, :HEAD]
                running[2 * pair + 1] += outer[HEAD:, HEAD:]
    share = HEADS // len(totals)
    for h in range(HEADS):
        for k, total_ref in enumerate(totals):

            @pl.when((lax.axis_index("narrow") + k) % len(totals) == h // share)
            def _(total_ref=total_ref, h=h):
                total_ref[h % share] = running[h].astype(BF16)

    w_loads[0].wait()


def key_value(spans, voxels, w_qkv, cores):
    tokens, width = voxels.shape
    inner = HEADS * HEAD
    hbm = pl.BlockSpec(memory_space=pl.ANY)
    vmem = pl.BlockSpec(memory_space=pltpu.VMEM)
    rows = [count * BLK for _, count in spans]
    out_shape = [jax.ShapeDtypeStruct((n, cols), BF16) for cols in (width, inner, inner) for n in rows]
    out_shape.append(jax.ShapeDtypeStruct((width, inner), BF16))
    out_shape.append(jax.ShapeDtypeStruct((tokens // BLK, HEADS, HEAD, HEAD), BF16))
    out_shape += [jax.ShapeDtypeStruct((HEADS // cores, HEAD, HEAD), BF16)] * cores
    outs = list(
        pl.pallas_call(
            functools.partial(key_value_kernel, spans),
            in_specs=[hbm, hbm],
            out_specs=[vmem] * len(out_shape),
            out_shape=out_shape,
            scratch_shapes=[
                pltpu.VMEM((2, width, inner), BF16),
                pltpu.SemaphoreType.DMA((len(spans) + 3,)),
            ],
            compiler_params=params(KEY_VALUE_KIB),
            name="key_value",
        )(voxels, w_qkv)
    )
    n = len(spans)
    return outs[:n], outs[n : 2 * n], outs[2 * n : 3 * n], outs[3 * n], outs[3 * n + 1], outs[3 * n + 2 :]


def local_kernel(first, count, x_ref, wq_ref, k_ref, v_ref, before_ref, q_ref, part_ref):
    causal = lax.broadcasted_iota(jnp.int32, (BLK, BLK), 0) >= lax.broadcasted_iota(
        jnp.int32, (BLK, BLK), 1
    )
    q = dot(x_ref[...], wq_ref[...]).astype(BF16)
    q_ref[...] = q
    for b in range(count):
        rows = slice(b * BLK, (b + 1) * BLK)
        for h in range(HEADS):
            cols = head_cols(h)
            scores = dot_nt(q[rows, cols], k_ref[rows, cols])
            scores = jnp.where(causal, scores, 0.0).astype(BF16)
            part_ref[rows, cols] = dot(scores, v_ref[rows, cols]) + dot(
                q[rows, cols], before_ref[first + b, h]
            )


def local_attention(x, w_q, k, v, before, first, count):
    rows, width = x.shape
    inner = HEADS * HEAD
    vmem = pl.BlockSpec(memory_space=pltpu.VMEM)
    return pl.pallas_call(
        functools.partial(local_kernel, first, count),
        in_specs=[vmem] * 5,
        out_specs=[vmem] * 2,
        out_shape=[
            jax.ShapeDtypeStruct((rows, inner), BF16),
            jax.ShapeDtypeStruct((rows, inner), F32),
        ],
        compiler_params=params(),
        cost_estimate=pl.CostEstimate(
            flops=2 * rows * inner * (width + 2 * BLK + HEAD),
            bytes_accessed=rows * inner * 12,
            transcendentals=0,
        ),
        name="local_attention",
    )(x, w_q, k, v, before)


def direct_kernel(*refs):
    count = len(refs) // 2 - 1
    xs, (wo_ref, wf_ref), outs = refs[:count], refs[count : count + 2], refs[count + 2 :]
    for x, out in zip(xs, outs):
        out[...] = dot(x[...], wf_ref[...])
    outs[-1][...] = dot(wo_ref[...], wf_ref[...]).astype(BF16)


def direct_features(xs, w_out, w_feature):
    channels = w_feature.shape[1]
    vmem = pl.BlockSpec(memory_space=pltpu.VMEM)
    rows = sum(x.shape[0] for x in xs)
    return pl.pallas_call(
        direct_kernel,
        in_specs=[vmem] * (len(xs) + 2),
        out_specs=[vmem] * (len(xs) + 1),
        out_shape=[jax.ShapeDtypeStruct((x.shape[0], channels), F32) for x in xs]
        + [jax.ShapeDtypeStruct(w_feature.shape, BF16)],
        compiler_params=params(),
        cost_estimate=pl.CostEstimate(
            flops=2 * (rows + w_out.shape[0]) * w_out.shape[1] * channels,
            bytes_accessed=rows * channels * 8,
            transcendentals=0,
        ),
        name="direct_features",
    )(*xs, w_out, w_feature)


def gather_kernel(*refs):
    ins, (running_ref, packed_ref) = refs[:-2], refs[-2:]
    running = sum(ref[...].astype(F32) for ref in ins)
    running_ref[...] = running
    packed_ref[...] = running.astype(BF16)


def earlier_sum(bits, others):
    digit = (lax.axis_index("wide") >> bits[0]) & ((1 << len(bits)) - 1)
    return sum(
        ((digit ^ (k + 1)) < digit).astype(F32) * other for k, other in enumerate(others)
    )


def scan_kernel(bits, count, running_ref, before_ref, *refs):
    others = [ref[...].astype(F32) for ref in refs[:count]]
    new_before, packed, *new_running = refs[count:]
    running = running_ref[...] + sum(others)
    packed[...] = running.astype(BF16)
    for ref in new_running:
        ref[...] = running
    new_before[...] = before_ref[...] + earlier_sum(bits, others)


def spread_kernel(cores, bits, count, before_ref, *refs):
    others = [ref[...].astype(F32) for ref in refs[:count]]
    pieces, outs = refs[count : count + cores], refs[count + cores :]
    place = lax.axis_index("narrow")
    before = before_ref[...] + earlier_sum(bits, others)
    for k, out in enumerate(outs):
        receiver = (place + k) % cores
        value = before
        for j, piece in enumerate(pieces):
            source = (place - j + cores) % cores
            value = value + jnp.where(source < receiver, 1.0, 0.0) * piece[...].astype(F32)
        out[...] = value.astype(BF16)


def small_call(kernel, name, inputs, dtypes, shape):
    vmem = pl.BlockSpec(memory_space=pltpu.VMEM)
    smem = pl.BlockSpec(memory_space=pltpu.SMEM)
    return pl.pallas_call(
        kernel,
        in_specs=[smem if array.dtype == jnp.int32 else vmem for array in inputs],
        out_specs=[vmem] * len(dtypes),
        out_shape=[jax.ShapeDtypeStruct(shape, dtype) for dtype in dtypes],
        compiler_params=params(4 * 1024),
        name=name,
    )(*inputs)


def ones_blocks(width):
    rows, cols = (lax.broadcasted_iota(jnp.int32, (width, width), axis) for axis in range(2))
    return jnp.where(rows // HEAD == cols // HEAD, 1.0, 0.0).astype(BF16)


def block_state(state_ref, scratch):
    scratch[...] = jnp.zeros_like(scratch)
    for j in range(state_ref.shape[0]):
        scratch[head_cols(j), head_cols(j)] = state_ref[j]
    return scratch[...]


def norm_share(q, part, state, ones):
    attended = part + dot(q, state)
    squares = dot((attended * attended).astype(BF16), ones)
    return (attended * lax.rsqrt(squares * (1 / HEAD) + EPS)).astype(BF16)


def share_columns(cores, before):
    width = HEADS // cores * HEAD
    owner = (lax.axis_index("narrow") - before + cores) % cores
    return pl.ds(pl.multiple_of(owner * width, width), width)


def own_share_kernel(cores, state_ref, w_ref, *refs):
    pieces = len(refs) // 4
    qs, parts, direct, outs = (refs[i * pieces : (i + 1) * pieces] for i in range(4))
    scratch = refs[-1]
    cols = share_columns(cores, 0)
    state, ones = block_state(state_ref, scratch), ones_blocks(scratch.shape[0])
    for q, part, start, out in zip(qs, parts, direct, outs):
        normed = norm_share(q[:, cols], part[:, cols], state, ones)
        out[...] = start[...] + dot(normed, w_ref[cols, :])


def own_share(cores, state, weights, qs, parts, direct):
    width = HEADS // cores * HEAD
    vmem = pl.BlockSpec(memory_space=pltpu.VMEM)
    rows = sum(q.shape[0] for q in qs)
    return pl.pallas_call(
        functools.partial(own_share_kernel, cores),
        in_specs=[vmem] * (2 + 3 * len(qs)),
        out_specs=[vmem] * len(qs),
        out_shape=[jax.ShapeDtypeStruct(start.shape, F32) for start in direct],
        scratch_shapes=[pltpu.VMEM((width, width), BF16)],
        compiler_params=params(),
        cost_estimate=pl.CostEstimate(
            flops=6 * rows * width * width, bytes_accessed=rows * width * 8, transcendentals=0
        ),
        name="own_share",
    )(state, weights, *qs, *parts, *direct)


def list_rows(brick_ref, most, slots, fill):
    for i in range(slots.shape[0]):
        slots[i] = -1
    for b in range(fill.shape[0]):
        fill[b] = 0
    for r in range(brick_ref.shape[0]):
        brick = brick_ref[r] ^ lax.axis_index("wide")
        used = fill[brick]
        slots[brick * most + used] = r
        fill[brick] = used + 1


def cell_numbers(middle):
    number = lax.broadcasted_iota(jnp.int32, (BX * BY // 2, 1), 0)
    if middle:
        return number + 2 * BY
    return number + jnp.where(number < 2 * BY, 0, BX * BY // 2)


def cell_sums(brick, numbers, most, slots, cell_ref, features_ref):
    onehots, rows = [], []
    for j in range(most):
        row = slots[brick * most + j]
        at = jnp.maximum(row, 0)
        match = (numbers == cell_ref[at]) & (row >= 0)
        onehots.append(jnp.where(match, 1.0, 0.0).astype(BF16))
        rows.append(features_ref[pl.ds(pl.multiple_of(at * ROW, ROW), ROW), :])
    return dot(jnp.concatenate(onehots, axis=1), jnp.concatenate(rows, axis=0)).astype(BF16)


def pool_into(outs, brick_ref, cell_ref, features_ref, slots, fill):
    most = slots.shape[0] // fill.shape[0]
    list_rows(brick_ref, most, slots, fill)
    for bricks, middle, out in outs:
        numbers = cell_numbers(middle)
        for n, brick in enumerate(bricks):
            out[n] = cell_sums(brick, numbers, most, slots, cell_ref, features_ref)


def features_kernel(bricks, spans, cores, brick_ref, *refs):
    pieces = len(spans)
    refs = list(refs)
    take = lambda n: [refs.pop(0) for _ in range(n)]
    q_refs, part_refs, own_refs = (take(pieces) for _ in range(3))
    state_refs = take(cores - 1)
    w_ref, cell_ref, features_ref, out = take(4)
    scratch, slots, fill = refs
    shares = [share_columns(cores, k) for k in range(cores)]
    ones = ones_blocks(scratch.shape[1])
    states = [block_state(ref, scratch.at[k]) for k, ref in enumerate(state_refs)]
    for n, (first, count) in enumerate(spans):
        features = own_refs[n][...]
        for state, cols in zip(states, shares[1:]):
            normed = norm_share(q_refs[n][:, cols], part_refs[n][:, cols], state, ones)
            features += dot(normed, w_ref[cols, :])
        features_ref[first * BLK : (first + count) * BLK] = features.astype(BF16)
    pool_into([(bricks, False, out)], brick_ref, cell_ref, features_ref, slots, fill)


def list_scratch(count, most):
    return [pltpu.SMEM((count * most,), jnp.int32), pltpu.SMEM((count,), jnp.int32)]


def sums_shape(count, channels):
    return jax.ShapeDtypeStruct((count, BX * BY // 2, channels), BF16)


def voxel_features(
    spans, bricks, qs, parts, own, states, weights, cell_rows, chosen, count, most
):
    tokens, channels = sum(q.shape[0] for q in qs), weights.shape[1]
    cores = len(states) + 1
    width = HEADS // cores * HEAD
    vmem = pl.BlockSpec(memory_space=pltpu.VMEM)
    smem = pl.BlockSpec(memory_space=pltpu.SMEM)
    return pl.pallas_call(
        functools.partial(features_kernel, chosen, spans, cores),
        in_specs=[smem] + [vmem] * (3 * len(spans) + cores + 1),
        out_specs=[vmem] * 2,
        out_shape=[
            jax.ShapeDtypeStruct((tokens, channels), BF16),
            sums_shape(len(chosen), channels),
        ],
        scratch_shapes=[pltpu.VMEM((max(1, cores - 1), width, width), BF16)]
        + list_scratch(count, most),
        compiler_params=params(),
        name="voxel_features",
    )(bricks, *qs, *parts, *own, *states, weights, cell_rows)


def pool_kernel(chosen, brick_ref, cell_ref, features_ref, *refs):
    outs, (slots, fill) = refs[:-2], refs[-2:]
    pool_into(
        [(bricks, middle, out) for (bricks, middle), out in zip(chosen, outs)],
        brick_ref,
        cell_ref,
        features_ref,
        slots,
        fill,
    )


def pool(bricks, cell_rows, features, chosen, count, most):
    tokens, channels = features.shape
    vmem = pl.BlockSpec(memory_space=pltpu.VMEM)
    smem = pl.BlockSpec(memory_space=pltpu.SMEM)
    return pl.pallas_call(
        functools.partial(pool_kernel, chosen),
        in_specs=[smem, vmem, vmem],
        out_specs=[vmem] * len(chosen),
        out_shape=[sums_shape(len(which), channels) for which, _ in chosen],
        scratch_shapes=list_scratch(count, most),
        compiler_params=params(),
        cost_estimate=pl.CostEstimate(
            flops=sum(len(which) for which, _ in chosen) * most * ROW * BX * BY * channels,
            bytes_accessed=tokens * channels * 2,
            transcendentals=0,
        ),
        name="pool",
    )(bricks, cell_rows, features)


def field_kernel(lines_ref, sides_ref, w1_ref, w2_ref, out_ref, field):
    lines = BX + 4
    wide, narrow = lax.axis_index("wide"), lax.axis_index("narrow")
    first_line, last_line = wide == 0, wide == lax.axis_size("wide") - 1
    first_column, last_column = narrow == 0, narrow == lax.axis_size("narrow") - 1
    for r in range(lines):
        field[r * LINE : r * LINE + GAP] = sides_ref[r]
        field[r * LINE + GAP : (r + 1) * LINE] = lines_ref[r]
    field[lines * LINE :] = sides_ref[lines]

    def convolve(w_ref, start, count):
        lhs = jnp.concatenate(
            [field[start + dy * LINE : start + dy * LINE + count] for dy in (-1, 0, 1)], axis=1
        )
        left, middle, right = [
            dot(lhs, jnp.concatenate([w_ref[dy, dx] for dy in range(3)], axis=0))
            for dx in range(3)
        ]
        return pltpu.roll(left, 1, 0) + middle + pltpu.roll(right, count - 1, 0)

    count = (BX + 2) * LINE + GAP
    inner = jax.nn.gelu(convolve(w1_ref, LINE, count), approximate=True)
    at = lax.broadcasted_iota(jnp.int32, (count, 1), 0)
    outside = first_line & (at <= LINE) | last_line & (at > (BX + 1) * LINE)
    for r in range(BX + 2):
        outside |= first_column & (at == r * LINE + GAP - 1)
        outside |= last_column & (at == (r + 1) * LINE)
    field[LINE : LINE + count] = jnp.where(outside, 0.0, inner).astype(BF16)
    flow = convolve(w2_ref, 2 * LINE, BX * LINE + GAP)
    for r in range(BX):
        out_ref[r] = flow[r * LINE + GAP : (r + 1) * LINE]


def field_flow(lines, left, right, conv_first, conv_second):
    count, _, channels = lines.shape
    vmem = pl.BlockSpec(memory_space=pltpu.VMEM)
    sides = jnp.pad(right, ((1, 0), (0, GAP - 2), (0, 0))) + jnp.pad(
        left, ((0, 1), (GAP - 2, 0), (0, 0))
    )
    return pl.pallas_call(
        field_kernel,
        in_specs=[vmem] * 4,
        out_specs=vmem,
        out_shape=jax.ShapeDtypeStruct((BX, BY, channels), F32),
        scratch_shapes=[pltpu.VMEM((count * LINE + GAP, channels), BF16)],
        compiler_params=params(16 * 1024),
        name="field_flow",
    )(lines, sides, conv_first, conv_second)


def swap(array, axis, bit):
    count = lax.axis_size(axis)
    return lax.ppermute(array, axis, [(i, i ^ (1 << bit)) for i in range(count)])


def swap_digit(array, axis, bit, by):
    count = lax.axis_size(axis)
    return lax.ppermute(array, axis, [(i, i ^ (by << bit)) for i in range(count)])


def shift(array, axis, by):
    count = lax.axis_size(axis)
    return lax.ppermute(
        array, axis, [(i, i + by) for i in range(count) if 0 <= i + by < count]
    )


def rotate(array, axis, by):
    count = lax.axis_size(axis)
    return lax.ppermute(array, axis, [(i, (i + by) % count) for i in range(count)])


def side_columns(lines):
    if lax.axis_size("narrow") != 2:
        return shift(lines[:, BY - 2 :], "narrow", 1), shift(lines[:, :2], "narrow", -1)
    first = lax.axis_index("narrow") == 0
    other = swap(jnp.where(first, lines[:, BY - 2 :], lines[:, :2]), "narrow", 0)
    nothing = jnp.zeros_like(other)
    return jnp.where(first, nothing, other), jnp.where(first, other, nothing)


def exchange_lines(strip, with_it):
    groups, count, cores = (lax.axis_size(axis) for axis in ("group", "wide", "narrow"))
    place = lax.axis_index("wide")
    got = []
    for start in range(2):
        pairs = []
        for g in range(groups):
            for w in range(count):
                other = w + 1 if w % 2 == start else w - 1
                far = g
                if not 0 <= other < count:
                    other, far = w, g ^ 1 if groups % 2 == 0 else g
                for c in range(cores):
                    pairs.append(((g * count + w) * cores + c, (far * count + other) * cores + c))
        upper = place % 2 == start
        out = jnp.where(upper, strip[2:], strip[:2])
        got.append(lax.ppermute(out, ("group", "wide", "narrow"), pairs))
    got, with_it = lax.optimization_barrier((got, with_it))
    above = jnp.where(place % 2 == 1, got[0], got[1])
    below = jnp.where(place % 2 == 1, got[1], got[0])
    above = jnp.where(place > 0, above, jnp.zeros_like(above))
    below = jnp.where(place < count - 1, below, jnp.zeros_like(below))
    return above, below, with_it


def earlier_state(totals, first_work, works):
    cores, shape = len(totals), totals[0].shape
    works, done = list(works), []

    def beside(work, arrays, exchange):
        held, arrays = work(arrays)
        done.append(held)
        held, arrived = lax.optimization_barrier((held, exchange(arrays)))
        done[-1] = held
        return arrived

    others = beside(
        first_work,
        totals[1:],
        lambda arrays: [rotate(array, "narrow", k + 1) for k, array in enumerate(arrays)],
    )
    pieces = [totals[0]] + others
    running, packed = small_call(gather_kernel, "gather", pieces, [F32, BF16], shape)
    before = jnp.zeros(shape, F32)
    count = lax.axis_size("wide").bit_length() - 1
    levels = [list(range(bit, min(bit + 2, count))) for bit in range(0, count, 2)]
    for level, bits in enumerate(levels):
        exchange = lambda packed: [
            swap_digit(packed, "wide", bits[0], k) for k in range(1, 1 << len(bits))
        ]
        others = beside(works.pop(0), packed, exchange) if works else exchange(packed)
        if level == len(levels) - 1:
            break
        before, packed, *more = small_call(
            functools.partial(scan_kernel, bits, len(others)),
            "scan",
            [running, before] + others,
            [F32, BF16] + [F32] * (level < len(levels) - 2),
            shape,
        )
        running = more[0] if more else None
    outs = small_call(
        functools.partial(spread_kernel, cores, bits, len(others)),
        "spread",
        [before] + others + pieces,
        [BF16] * cores,
        shape,
    )
    states = [outs[0]] + [rotate(outs[k], "narrow", k) for k in range(1, cores)]
    while works:
        done.append(works.pop(0)(outs[0])[0])
    return states, done


def split_order(order):
    half = 1 << (len(order) - 1)
    place = lambda slot: sum(
        ((slot >> (len(order) - 1 - i)) & 1) << bit for i, bit in enumerate(order)
    )
    return [place(slot) for slot in range(half)], [place(slot) for slot in range(half, 2 * half)]


def reduce_level(stays, goes, bit, with_it=None):
    arrived = [swap(array, "wide", bit) for array in reversed(goes)][::-1]
    if with_it is not None:
        arrived, with_it = lax.optimization_barrier((arrived, with_it))
    sums = [
        (here.astype(F32) + more.astype(F32)).astype(BF16) for here, more in zip(stays, arrived)
    ]
    return sums, with_it


def next_level(sums):
    if len(sums) == 1:
        half = sums[0].shape[0] // 2
        return [sums[0][:half]], [sums[0][half:]]
    return sums[:1], sums[1:]


def reduce_both(outer, middle, orders):
    levels = len(orders[0])
    outer_sums, _ = reduce_level(*outer, orders[0][0])
    stays, (later, first) = middle
    later, outer_sums[-1] = lax.optimization_barrier((later, outer_sums[-1]))
    middle = stays, [later, first]
    outer = next_level(outer_sums)
    for level in range(1, levels):
        middle_sums, _ = reduce_level(*middle, orders[1][level - 1])
        middle = next_level(middle_sums)
        if level > 1:
            outer_sums, middle = reduce_level(*outer, orders[0][level], middle)
        else:
            outer_sums, _ = reduce_level(*outer, orders[0][level])
        outer = next_level(outer_sums)
    return outer_sums[0][0], reduce_level(*middle, orders[1][-1])[0][0][0]


def per_device(voxels, w_qkv, w_out, w_feature, conv_first, conv_second, row_brick, cell_place):
    tokens = voxels.shape[0]
    channels = w_feature.shape[1]
    wide_count, wide_place = lax.axis_size("wide"), lax.axis_index("wide")
    narrow_count, narrow_place = lax.axis_size("narrow"), lax.axis_index("narrow")

    blocks = tokens // BLK
    cuts = sorted({blocks * i // 2 for i in range(3)})
    spans = [(first, last - first) for first, last in zip(cuts, cuts[1:])]
    xs, ks, vs, w_q, before, totals = key_value(spans, voxels, w_qkv, narrow_count)

    def direct(arrays):
        arrays, x = lax.optimization_barrier((arrays, xs[0]))
        return direct_features([x] + xs[1:], w_out, w_feature), arrays

    def work(n):
        def run(array):
            array, k = lax.optimization_barrier((array, ks[n]))
            return local_attention(xs[n], w_q, k, vs[n], before, *spans[n]), array

        return run

    states, done = earlier_state(totals, direct, [work(n) for n in range(len(spans))])
    own, weights = done[0][:-1], done[0][-1]
    qs, parts = ([piece[i] for piece in done[1:]] for i in range(2))
    own = own_share(narrow_count, states[0], weights, qs, parts, own)

    bits = list(range(wide_count.bit_length() - 1))
    orders = [bits, bits[1::-1] + bits[2:]]
    halves = lambda places: (places[: len(places) // 2], places[len(places) // 2 :])
    stay, go = zip(*(map(halves, split_order(order)) for order in orders))
    cell_rows = cell_place.reshape(-1, 1, ROW)
    most = max(2, 2 * (tokens // ROW) // wide_count)
    bricks = row_brick[:, 0]
    features, outer_first = voxel_features(
        spans, bricks, qs, parts, own, states[1:], weights, cell_rows, go[0][1], wide_count, most
    )
    pooled = lambda *chosen: pool(bricks, cell_rows, features, chosen, wide_count, most)
    middle_first, outer_later, middle_later, *sums = pooled(
        (go[1][1], True),
        (go[0][0], False),
        (go[1][0], True),
        *((stay[middle][n], middle == 1) for middle in range(2) for n in range(2)),
    )
    outer, middle = reduce_both(
        (sums[:2], [outer_later, outer_first]), (sums[2:], [middle_later, middle_first]), orders
    )
    outer, middle = (part.reshape(-1, BY, channels) for part in (outer, middle))
    above, below, middle = exchange_lines(outer, middle)
    lines = jnp.concatenate([above, outer[:2], middle, outer[2:], below], axis=0)
    left, right = side_columns(lines)
    return field_flow(lines, left, right, conv_first, conv_second)


def solution(mesh):
    placed = (
        P(("group", "wide", "narrow"), None),
        P(),
        P(),
        P(),
        P(),
        P(),
        P(("group", "wide", "narrow"), None),
        P(("group", "wide", "narrow")),
    )
    return jax.shard_map(
        per_device,
        mesh=mesh,
        in_specs=placed,
        out_specs=P(("group", "wide"), "narrow", None),
        check_vma=False,
    )
```

```python
import functools

import jax
import jax.numpy as jnp
from jax import lax
from jax.experimental import pallas as pl
from jax.experimental.pallas import tpu as pltpu
from jax.sharding import PartitionSpec as P

HEADS = 4
HEAD = 128
ROW = 128
BLK = 256
BX = 8
BY = 32
EPS = 1e-06
GAP = 16
LINE = GAP + BY

F32 = jnp.float32
BF16 = jnp.bfloat16


def dot(a, b):
    return jnp.dot(a, b, preferred_element_type=F32)


def dot_t(a, b):
    return lax.dot_general(a, b, (((0,), (0,)), ((), ())), preferred_element_type=F32)


def dot_nt(a, b):
    return lax.dot_general(a, b, (((1,), (1,)), ((), ())), preferred_element_type=F32)


KEY_VALUE_KIB = 46592


def params(kib=24 * 1024):
    return pltpu.CompilerParams(vmem_limit_bytes=kib << 10)


def head_cols(h):
    return slice(h * HEAD, (h + 1) * HEAD)


def key_value_kernel(spans, x_ref, w_ref, *refs):
    refs = list(refs)
    take = lambda n: [refs.pop(0) for _ in range(n)]
    xs, ks, vs = take(len(spans)), take(len(spans)), take(len(spans))
    wq, before_ref = take(2)
    totals, (w, sems) = refs[:-2], refs[-2:]
    inner = HEADS * HEAD

    def columns(part, target):
        return pltpu.make_async_copy(
            w_ref.at[:, pl.ds(part * inner, inner)], target, sems.at[len(spans) + part]
        )

    loads = [
        pltpu.make_async_copy(x_ref.at[pl.ds(first * BLK, count * BLK)], x, sems.at[n])
        for n, ((first, count), x) in enumerate(zip(spans, xs))
    ]
    w_loads = [columns(0, wq), columns(1, w.at[0]), columns(2, w.at[1])]
    w_loads[1].start()
    loads[0].start()
    w_loads[2].start()
    for load in loads[1:]:
        load.start()
    w_loads[0].start()
    running = [jnp.zeros((HEAD, HEAD), F32) for _ in range(HEADS)]
    for n, ((first, count), x, k_ref, v_ref) in enumerate(zip(spans, xs, ks, vs)):
        if n == 0:
            w_loads[1].wait()
        loads[n].wait()
        k = dot(x[...], w[0]).astype(BF16)
        k_ref[...] = k
        if n == 0:
            w_loads[2].wait()
        v = dot(x[...], w[1]).astype(BF16)
        v_ref[...] = v
        for b in range(count):
            block = slice(b * BLK, (b + 1) * BLK)
            for h in range(HEADS):
                before_ref[first + b, h] = running[h].astype(BF16)
            for pair in range(HEADS // 2):
                cols = slice(pair * 2 * HEAD, (pair + 1) * 2 * HEAD)
                outer = dot_t(k[block, cols], v[block, cols])
                running[2 * pair] += outer[:HEAD, :HEAD]
                running[2 * pair + 1] += outer[HEAD:, HEAD:]
    share = HEADS // len(totals)
    for h in range(HEADS):
        for k, total_ref in enumerate(totals):

            @pl.when((lax.axis_index("narrow") + k) % len(totals) == h // share)
            def _(total_ref=total_ref, h=h):
                total_ref[h % share] = running[h].astype(BF16)

    w_loads[0].wait()


def key_value(spans, voxels, w_qkv, cores):
    tokens, width = voxels.shape
    inner = HEADS * HEAD
    hbm = pl.BlockSpec(memory_space=pl.ANY)
    vmem = pl.BlockSpec(memory_space=pltpu.VMEM)
    rows = [count * BLK for _, count in spans]
    out_shape = [jax.ShapeDtypeStruct((n, cols), BF16) for cols in (width, inner, inner) for n in rows]
    out_shape.append(jax.ShapeDtypeStruct((width, inner), BF16))
    out_shape.append(jax.ShapeDtypeStruct((tokens // BLK, HEADS, HEAD, HEAD), BF16))
    out_shape += [jax.ShapeDtypeStruct((HEADS // cores, HEAD, HEAD), BF16)] * cores
    outs = list(
        pl.pallas_call(
            functools.partial(key_value_kernel, spans),
            in_specs=[hbm, hbm],
            out_specs=[vmem] * len(out_shape),
            out_shape=out_shape,
            scratch_shapes=[
                pltpu.VMEM((2, width, inner), BF16),
                pltpu.SemaphoreType.DMA((len(spans) + 3,)),
            ],
            compiler_params=params(KEY_VALUE_KIB),
            name="key_value",
        )(voxels, w_qkv)
    )
    n = len(spans)
    return outs[:n], outs[n : 2 * n], outs[2 * n : 3 * n], outs[3 * n], outs[3 * n + 1], outs[3 * n + 2 :]


def local_kernel(first, count, x_ref, wq_ref, k_ref, v_ref, before_ref, q_ref, part_ref):
    causal = lax.broadcasted_iota(jnp.int32, (BLK, BLK), 0) >= lax.broadcasted_iota(
        jnp.int32, (BLK, BLK), 1
    )
    q = dot(x_ref[...], wq_ref[...]).astype(BF16)
    q_ref[...] = q
    for b in range(count):
        rows = slice(b * BLK, (b + 1) * BLK)
        for h in range(HEADS):
            cols = head_cols(h)
            scores = dot_nt(q[rows, cols], k_ref[rows, cols])
            scores = jnp.where(causal, scores, 0.0).astype(BF16)
            part_ref[rows, cols] = dot(scores, v_ref[rows, cols]) + dot(
                q[rows, cols], before_ref[first + b, h]
            )


def local_attention(x, w_q, k, v, before, first, count):
    rows, width = x.shape
    inner = HEADS * HEAD
    vmem = pl.BlockSpec(memory_space=pltpu.VMEM)
    return pl.pallas_call(
        functools.partial(local_kernel, first, count),
        in_specs=[vmem] * 5,
        out_specs=[vmem] * 2,
        out_shape=[
            jax.ShapeDtypeStruct((rows, inner), BF16),
            jax.ShapeDtypeStruct((rows, inner), F32),
        ],
        compiler_params=params(),
        cost_estimate=pl.CostEstimate(
            flops=2 * rows * inner * (width + 2 * BLK + HEAD),
            bytes_accessed=rows * inner * 12,
            transcendentals=0,
        ),
        name="local_attention",
    )(x, w_q, k, v, before)


def direct_kernel(*refs):
    count = len(refs) // 2 - 1
    xs, (wo_ref, wf_ref), outs = refs[:count], refs[count : count + 2], refs[count + 2 :]
    for x, out in zip(xs, outs):
        out[...] = dot(x[...], wf_ref[...])
    outs[-1][...] = dot(wo_ref[...], wf_ref[...]).astype(BF16)


def direct_features(xs, w_out, w_feature):
    channels = w_feature.shape[1]
    vmem = pl.BlockSpec(memory_space=pltpu.VMEM)
    rows = sum(x.shape[0] for x in xs)
    return pl.pallas_call(
        direct_kernel,
        in_specs=[vmem] * (len(xs) + 2),
        out_specs=[vmem] * (len(xs) + 1),
        out_shape=[jax.ShapeDtypeStruct((x.shape[0], channels), F32) for x in xs]
        + [jax.ShapeDtypeStruct(w_feature.shape, BF16)],
        compiler_params=params(),
        cost_estimate=pl.CostEstimate(
            flops=2 * (rows + w_out.shape[0]) * w_out.shape[1] * channels,
            bytes_accessed=rows * channels * 8,
            transcendentals=0,
        ),
        name="direct_features",
    )(*xs, w_out, w_feature)


def gather_kernel(*refs):
    ins, (running_ref, packed_ref) = refs[:-2], refs[-2:]
    running = sum(ref[...].astype(F32) for ref in ins)
    running_ref[...] = running
    packed_ref[...] = running.astype(BF16)


def earlier_sum(bits, others):
    digit = (lax.axis_index("wide") >> bits[0]) & ((1 << len(bits)) - 1)
    return sum(
        ((digit ^ (k + 1)) < digit).astype(F32) * other for k, other in enumerate(others)
    )


def scan_kernel(bits, count, running_ref, before_ref, *refs):
    others = [ref[...].astype(F32) for ref in refs[:count]]
    new_before, packed, *new_running = refs[count:]
    running = running_ref[...] + sum(others)
    packed[...] = running.astype(BF16)
    for ref in new_running:
        ref[...] = running
    new_before[...] = before_ref[...] + earlier_sum(bits, others)


def spread_kernel(cores, bits, count, before_ref, *refs):
    others = [ref[...].astype(F32) for ref in refs[:count]]
    pieces, outs = refs[count : count + cores], refs[count + cores :]
    place = lax.axis_index("narrow")
    before = before_ref[...] + earlier_sum(bits, others)
    for k, out in enumerate(outs):
        receiver = (place + k) % cores
        value = before
        for j, piece in enumerate(pieces):
            source = (place - j + cores) % cores
            value = value + jnp.where(source < receiver, 1.0, 0.0) * piece[...].astype(F32)
        out[...] = value.astype(BF16)


def small_call(kernel, name, inputs, dtypes, shape):
    vmem = pl.BlockSpec(memory_space=pltpu.VMEM)
    smem = pl.BlockSpec(memory_space=pltpu.SMEM)
    return pl.pallas_call(
        kernel,
        in_specs=[smem if array.dtype == jnp.int32 else vmem for array in inputs],
        out_specs=[vmem] * len(dtypes),
        out_shape=[jax.ShapeDtypeStruct(shape, dtype) for dtype in dtypes],
        compiler_params=params(4 * 1024),
        name=name,
    )(*inputs)


def ones_blocks(width):
    rows, cols = (lax.broadcasted_iota(jnp.int32, (width, width), axis) for axis in range(2))
    return jnp.where(rows // HEAD == cols // HEAD, 1.0, 0.0).astype(BF16)


def block_state(state_ref, scratch):
    scratch[...] = jnp.zeros_like(scratch)
    for j in range(state_ref.shape[0]):
        scratch[head_cols(j), head_cols(j)] = state_ref[j]
    return scratch[...]


def norm_share(q, part, state, ones):
    attended = part + dot(q, state)
    squares = dot((attended * attended).astype(BF16), ones)
    return (attended * lax.rsqrt(squares * (1 / HEAD) + EPS)).astype(BF16)


def share_columns(cores, before):
    width = HEADS // cores * HEAD
    owner = (lax.axis_index("narrow") - before + cores) % cores
    return pl.ds(pl.multiple_of(owner * width, width), width)


def own_share_kernel(cores, state_ref, w_ref, *refs):
    pieces = len(refs) // 4
    qs, parts, direct, outs = (refs[i * pieces : (i + 1) * pieces] for i in range(4))
    scratch = refs[-1]
    cols = share_columns(cores, 0)
    state, ones = block_state(state_ref, scratch), ones_blocks(scratch.shape[0])
    for q, part, start, out in zip(qs, parts, direct, outs):
        normed = norm_share(q[:, cols], part[:, cols], state, ones)
        out[...] = start[...] + dot(normed, w_ref[cols, :])


def own_share(cores, state, weights, qs, parts, direct):
    width = HEADS // cores * HEAD
    vmem = pl.BlockSpec(memory_space=pltpu.VMEM)
    rows = sum(q.shape[0] for q in qs)
    return pl.pallas_call(
        functools.partial(own_share_kernel, cores),
        in_specs=[vmem] * (2 + 3 * len(qs)),
        out_specs=[vmem] * len(qs),
        out_shape=[jax.ShapeDtypeStruct(start.shape, F32) for start in direct],
        scratch_shapes=[pltpu.VMEM((width, width), BF16)],
        compiler_params=params(),
        cost_estimate=pl.CostEstimate(
            flops=6 * rows * width * width, bytes_accessed=rows * width * 8, transcendentals=0
        ),
        name="own_share",
    )(state, weights, *qs, *parts, *direct)


def list_rows(brick_ref, most, slots, fill):
    for i in range(slots.shape[0]):
        slots[i] = -1
    for b in range(fill.shape[0]):
        fill[b] = 0
    for r in range(brick_ref.shape[0]):
        brick = brick_ref[r] ^ lax.axis_index("wide")
        used = fill[brick]
        slots[brick * most + used] = r
        fill[brick] = used + 1


def cell_numbers(middle):
    number = lax.broadcasted_iota(jnp.int32, (BX * BY // 2, 1), 0)
    if middle:
        return number + 2 * BY
    return number + jnp.where(number < 2 * BY, 0, BX * BY // 2)


def cell_sums(brick, numbers, most, slots, cell_ref, features_ref):
    onehots, rows = [], []
    for j in range(most):
        row = slots[brick * most + j]
        at = jnp.maximum(row, 0)
        match = (numbers == cell_ref[at]) & (row >= 0)
        onehots.append(jnp.where(match, 1.0, 0.0).astype(BF16))
        rows.append(features_ref[pl.ds(pl.multiple_of(at * ROW, ROW), ROW), :])
    return dot(jnp.concatenate(onehots, axis=1), jnp.concatenate(rows, axis=0)).astype(BF16)


def pool_into(outs, brick_ref, cell_ref, features_ref, slots, fill):
    most = slots.shape[0] // fill.shape[0]
    list_rows(brick_ref, most, slots, fill)
    for bricks, middle, out in outs:
        numbers = cell_numbers(middle)
        for n, brick in enumerate(bricks):
            out[n] = cell_sums(brick, numbers, most, slots, cell_ref, features_ref)


def features_kernel(bricks, spans, cores, brick_ref, *refs):
    pieces = len(spans)
    refs = list(refs)
    take = lambda n: [refs.pop(0) for _ in range(n)]
    q_refs, part_refs, own_refs = (take(pieces) for _ in range(3))
    state_refs = take(cores - 1)
    w_ref, cell_ref, features_ref, out = take(4)
    scratch, slots, fill = refs
    shares = [share_columns(cores, k) for k in range(cores)]
    ones = ones_blocks(scratch.shape[1])
    states = [block_state(ref, scratch.at[k]) for k, ref in enumerate(state_refs)]
    for n, (first, count) in enumerate(spans):
        features = own_refs[n][...]
        for state, cols in zip(states, shares[1:]):
            normed = norm_share(q_refs[n][:, cols], part_refs[n][:, cols], state, ones)
            features += dot(normed, w_ref[cols, :])
        features_ref[first * BLK : (first + count) * BLK] = features.astype(BF16)
    pool_into([(bricks, False, out)], brick_ref, cell_ref, features_ref, slots, fill)


def list_scratch(count, most):
    return [pltpu.SMEM((count * most,), jnp.int32), pltpu.SMEM((count,), jnp.int32)]


def sums_shape(count, channels):
    return jax.ShapeDtypeStruct((count, BX * BY // 2, channels), BF16)


def voxel_features(
    spans, bricks, qs, parts, own, states, weights, cell_rows, chosen, count, most
):
    tokens, channels = sum(q.shape[0] for q in qs), weights.shape[1]
    cores = len(states) + 1
    width = HEADS // cores * HEAD
    vmem = pl.BlockSpec(memory_space=pltpu.VMEM)
    smem = pl.BlockSpec(memory_space=pltpu.SMEM)
    return pl.pallas_call(
        functools.partial(features_kernel, chosen, spans, cores),
        in_specs=[smem] + [vmem] * (3 * len(spans) + cores + 1),
        out_specs=[vmem] * 2,
        out_shape=[
            jax.ShapeDtypeStruct((tokens, channels), BF16),
            sums_shape(len(chosen), channels),
        ],
        scratch_shapes=[pltpu.VMEM((max(1, cores - 1), width, width), BF16)]
        + list_scratch(count, most),
        compiler_params=params(),
        name="voxel_features",
    )(bricks, *qs, *parts, *own, *states, weights, cell_rows)


def pool_kernel(chosen, brick_ref, cell_ref, features_ref, *refs):
    outs, (slots, fill) = refs[:-2], refs[-2:]
    pool_into(
        [(bricks, middle, out) for (bricks, middle), out in zip(chosen, outs)],
        brick_ref,
        cell_ref,
        features_ref,
        slots,
        fill,
    )


def pool(bricks, cell_rows, features, chosen, count, most):
    tokens, channels = features.shape
    vmem = pl.BlockSpec(memory_space=pltpu.VMEM)
    smem = pl.BlockSpec(memory_space=pltpu.SMEM)
    return pl.pallas_call(
        functools.partial(pool_kernel, chosen),
        in_specs=[smem, vmem, vmem],
        out_specs=[vmem] * len(chosen),
        out_shape=[sums_shape(len(which), channels) for which, _ in chosen],
        scratch_shapes=list_scratch(count, most),
        compiler_params=params(),
        cost_estimate=pl.CostEstimate(
            flops=sum(len(which) for which, _ in chosen) * most * ROW * BX * BY * channels,
            bytes_accessed=tokens * channels * 2,
            transcendentals=0,
        ),
        name="pool",
    )(bricks, cell_rows, features)


def convolve(field, w_ref, start, count):
    lhs = jnp.concatenate(
        [field[start + dy * LINE : start + dy * LINE + count] for dy in (-1, 0, 1)], axis=1
    )
    left, middle, right = weighted(lhs, w_ref)
    return pltpu.roll(left, 1, 0) + middle + pltpu.roll(right, count - 1, 0)


def weighted(lhs, w_ref):
    return [
        dot(lhs, jnp.concatenate([w_ref[dy, dx] for dy in range(3)], axis=0)) for dx in range(3)
    ]


def own_columns_kernel(lines_ref, w_ref, out_ref, field):
    lines = lines_ref.shape[0]
    for r in range(lines):
        field[r * LINE : r * LINE + GAP] = jnp.zeros((GAP, field.shape[1]), BF16)
        field[r * LINE + GAP : (r + 1) * LINE] = lines_ref[r]
    field[lines * LINE :] = jnp.zeros((GAP, field.shape[1]), BF16)
    out_ref[...] = convolve(field, w_ref, LINE, out_ref.shape[0])


def own_columns(lines, conv_first):
    count, _, channels = lines.shape
    vmem = pl.BlockSpec(memory_space=pltpu.VMEM)
    shown = (count - 2) * LINE + GAP
    return pl.pallas_call(
        own_columns_kernel,
        in_specs=[vmem] * 2,
        out_specs=vmem,
        out_shape=jax.ShapeDtypeStruct((shown, channels), F32),
        scratch_shapes=[pltpu.VMEM((count * LINE + GAP, channels), BF16)],
        compiler_params=params(16 * 1024),
        cost_estimate=pl.CostEstimate(
            flops=18 * shown * channels * channels,
            bytes_accessed=shown * channels * 8,
            transcendentals=0,
        ),
        name="own_columns",
    )(lines, conv_first)


def field_kernel(first_ref, sides_ref, w1_ref, w2_ref, out_ref, first, field):
    count, channels = first.shape
    wide, narrow = lax.axis_index("wide"), lax.axis_index("narrow")
    first_line, last_line = wide == 0, wide == lax.axis_size("wide") - 1
    first_column, last_column = narrow == 0, narrow == lax.axis_size("narrow") - 1
    gaps = sides_ref.shape[0] - 2
    sides = sides_ref[...].reshape((gaps + 2) * GAP, channels)
    lhs = jnp.concatenate([sides[dy * GAP : (dy + gaps) * GAP] for dy in range(3)], axis=1)
    none = jnp.zeros((8, channels), F32)
    left, middle, right = [
        jnp.concatenate(
            [part for g in range(gaps) for part in (none, given[g * GAP : (g + 1) * GAP], none)],
            axis=0,
        )
        for given in weighted(lhs, w1_ref)
    ]
    span = GAP + 16
    added = pltpu.roll(left, 1, 0) + middle + pltpu.roll(right, gaps * span - 1, 0)
    first[...] = first_ref[...]
    for g in range(gaps):
        start, stop = max(g * LINE - 8, 0), min(g * LINE + GAP + 8, count)
        at = g * span + 8 - g * LINE
        first[start:stop] += added[start + at : stop + at]
    inner = jax.nn.gelu(first[...], approximate=True)
    at = lax.broadcasted_iota(jnp.int32, (count, 1), 0)
    outside = first_line & (at <= LINE) | last_line & (at > (BX + 1) * LINE)
    for r in range(BX + 2):
        outside |= first_column & (at == r * LINE + GAP - 1)
        outside |= last_column & (at == (r + 1) * LINE)
    field[...] = jnp.where(outside, 0.0, inner).astype(BF16)
    flow = convolve(field, w2_ref, LINE, BX * LINE + GAP)
    for r in range(BX):
        out_ref[r] = flow[r * LINE + GAP : (r + 1) * LINE]


def field_flow(first, left, right, conv_first, conv_second):
    count, channels = first.shape
    vmem = pl.BlockSpec(memory_space=pltpu.VMEM)
    sides = jnp.pad(right, ((1, 0), (0, GAP - 2), (0, 0))) + jnp.pad(
        left, ((0, 1), (GAP - 2, 0), (0, 0))
    )
    return pl.pallas_call(
        field_kernel,
        in_specs=[vmem] * 4,
        out_specs=vmem,
        out_shape=jax.ShapeDtypeStruct((BX, BY, channels), F32),
        scratch_shapes=[pltpu.VMEM((count, channels), F32), pltpu.VMEM((count, channels), BF16)],
        compiler_params=params(16 * 1024),
        name="field_flow",
    )(first, sides, conv_first, conv_second)


def swap(array, axis, bit):
    count = lax.axis_size(axis)
    return lax.ppermute(array, axis, [(i, i ^ (1 << bit)) for i in range(count)])


def swap_digit(array, axis, bit, by):
    count = lax.axis_size(axis)
    return lax.ppermute(array, axis, [(i, i ^ (by << bit)) for i in range(count)])


def shift(array, axis, by):
    count = lax.axis_size(axis)
    return lax.ppermute(
        array, axis, [(i, i + by) for i in range(count) if 0 <= i + by < count]
    )


def rotate(array, axis, by):
    count = lax.axis_size(axis)
    return lax.ppermute(array, axis, [(i, (i + by) % count) for i in range(count)])


def side_columns(lines):
    if lax.axis_size("narrow") != 2:
        return shift(lines[:, BY - 2 :], "narrow", 1), shift(lines[:, :2], "narrow", -1)
    first = lax.axis_index("narrow") == 0
    other = swap(jnp.where(first, lines[:, BY - 2 :], lines[:, :2]), "narrow", 0)
    nothing = jnp.zeros_like(other)
    return jnp.where(first, nothing, other), jnp.where(first, other, nothing)


def exchange_lines(strip, with_it):
    groups, count, cores = (lax.axis_size(axis) for axis in ("group", "wide", "narrow"))
    place = lax.axis_index("wide")
    got = []
    for start in range(2):
        pairs = []
        for g in range(groups):
            for w in range(count):
                other = w + 1 if w % 2 == start else w - 1
                far = g
                if not 0 <= other < count:
                    other, far = w, g ^ 1 if groups % 2 == 0 else g
                for c in range(cores):
                    pairs.append(((g * count + w) * cores + c, (far * count + other) * cores + c))
        upper = place % 2 == start
        out = jnp.where(upper, strip[2:], strip[:2])
        got.append(lax.ppermute(out, ("group", "wide", "narrow"), pairs))
    got, with_it = lax.optimization_barrier((got, with_it))
    above = jnp.where(place % 2 == 1, got[0], got[1])
    below = jnp.where(place % 2 == 1, got[1], got[0])
    above = jnp.where(place > 0, above, jnp.zeros_like(above))
    below = jnp.where(place < count - 1, below, jnp.zeros_like(below))
    return above, below, with_it


def earlier_state(totals, first_work, works):
    cores, shape = len(totals), totals[0].shape
    works, done = list(works), []

    def beside(work, arrays, exchange):
        held, arrays = work(arrays)
        done.append(held)
        held, arrived = lax.optimization_barrier((held, exchange(arrays)))
        done[-1] = held
        return arrived

    others = beside(
        first_work,
        totals[1:],
        lambda arrays: [rotate(array, "narrow", k + 1) for k, array in enumerate(arrays)],
    )
    pieces = [totals[0]] + others
    running, packed = small_call(gather_kernel, "gather", pieces, [F32, BF16], shape)
    before = jnp.zeros(shape, F32)
    count = lax.axis_size("wide").bit_length() - 1
    levels = [list(range(bit, min(bit + 2, count))) for bit in range(0, count, 2)]
    for level, bits in enumerate(levels):
        exchange = lambda packed: [
            swap_digit(packed, "wide", bits[0], k) for k in range(1, 1 << len(bits))
        ]
        others = beside(works.pop(0), packed, exchange) if works else exchange(packed)
        if level == len(levels) - 1:
            break
        before, packed, *more = small_call(
            functools.partial(scan_kernel, bits, len(others)),
            "scan",
            [running, before] + others,
            [F32, BF16] + [F32] * (level < len(levels) - 2),
            shape,
        )
        running = more[0] if more else None
    outs = small_call(
        functools.partial(spread_kernel, cores, bits, len(others)),
        "spread",
        [before] + others + pieces,
        [BF16] * cores,
        shape,
    )
    states = [outs[0]] + [rotate(outs[k], "narrow", k) for k in range(1, cores)]
    while works:
        done.append(works.pop(0)(outs[0])[0])
    return states, done


def split_order(order):
    half = 1 << (len(order) - 1)
    place = lambda slot: sum(
        ((slot >> (len(order) - 1 - i)) & 1) << bit for i, bit in enumerate(order)
    )
    return [place(slot) for slot in range(half)], [place(slot) for slot in range(half, 2 * half)]


def reduce_level(stays, goes, bit, with_it=None):
    arrived = [swap(array, "wide", bit) for array in reversed(goes)][::-1]
    if with_it is not None:
        arrived, with_it = lax.optimization_barrier((arrived, with_it))
    sums = [
        (here.astype(F32) + more.astype(F32)).astype(BF16) for here, more in zip(stays, arrived)
    ]
    return sums, with_it


def next_level(sums):
    if len(sums) == 1:
        half = sums[0].shape[0] // 2
        return [sums[0][:half]], [sums[0][half:]]
    return sums[:1], sums[1:]


def reduce_both(outer, middle, orders):
    levels = len(orders[0])
    outer_sums, _ = reduce_level(*outer, orders[0][0])
    stays, (later, first) = middle
    later, outer_sums[-1] = lax.optimization_barrier((later, outer_sums[-1]))
    middle = stays, [later, first]
    outer = next_level(outer_sums)
    for level in range(1, levels):
        middle_sums, _ = reduce_level(*middle, orders[1][level - 1])
        middle = next_level(middle_sums)
        if level > 1:
            outer_sums, middle = reduce_level(*outer, orders[0][level], middle)
        else:
            outer_sums, _ = reduce_level(*outer, orders[0][level])
        outer = next_level(outer_sums)
    return outer_sums[0][0], reduce_level(*middle, orders[1][-1])[0][0][0]


def per_device(voxels, w_qkv, w_out, w_feature, conv_first, conv_second, row_brick, cell_place):
    tokens = voxels.shape[0]
    channels = w_feature.shape[1]
    wide_count, wide_place = lax.axis_size("wide"), lax.axis_index("wide")
    narrow_count, narrow_place = lax.axis_size("narrow"), lax.axis_index("narrow")

    blocks = tokens // BLK
    cuts = sorted({blocks * i // 2 for i in range(3)})
    spans = [(first, last - first) for first, last in zip(cuts, cuts[1:])]
    xs, ks, vs, w_q, before, totals = key_value(spans, voxels, w_qkv, narrow_count)

    def direct(arrays):
        arrays, x = lax.optimization_barrier((arrays, xs[0]))
        return direct_features([x] + xs[1:], w_out, w_feature), arrays

    def work(n):
        def run(array):
            array, k = lax.optimization_barrier((array, ks[n]))
            return local_attention(xs[n], w_q, k, vs[n], before, *spans[n]), array

        return run

    states, done = earlier_state(totals, direct, [work(n) for n in range(len(spans))])
    own, weights = done[0][:-1], done[0][-1]
    qs, parts = ([piece[i] for piece in done[1:]] for i in range(2))
    own = own_share(narrow_count, states[0], weights, qs, parts, own)

    bits = list(range(wide_count.bit_length() - 1))
    orders = [bits, bits[1::-1] + bits[2:]]
    halves = lambda places: (places[: len(places) // 2], places[len(places) // 2 :])
    stay, go = zip(*(map(halves, split_order(order)) for order in orders))
    cell_rows = cell_place.reshape(-1, 1, ROW)
    most = max(2, 2 * (tokens // ROW) // wide_count)
    bricks = row_brick[:, 0]
    features, outer_first = voxel_features(
        spans, bricks, qs, parts, own, states[1:], weights, cell_rows, go[0][1], wide_count, most
    )
    pooled = lambda *chosen: pool(bricks, cell_rows, features, chosen, wide_count, most)
    middle_first, outer_later, middle_later, *sums = pooled(
        (go[1][1], True),
        (go[0][0], False),
        (go[1][0], True),
        *((stay[middle][n], middle == 1) for middle in range(2) for n in range(2)),
    )
    outer, middle = reduce_both(
        (sums[:2], [outer_later, outer_first]), (sums[2:], [middle_later, middle_first]), orders
    )
    outer, middle = (part.reshape(-1, BY, channels) for part in (outer, middle))
    above, below, middle = exchange_lines(outer, middle)
    lines = jnp.concatenate([above, outer[:2], middle, outer[2:], below], axis=0)
    left, right = side_columns(lines)
    return field_flow(own_columns(lines, conv_first), left, right, conv_first, conv_second)


def solution(mesh):
    placed = (
        P(("group", "wide", "narrow"), None),
        P(),
        P(),
        P(),
        P(),
        P(),
        P(("group", "wide", "narrow"), None),
        P(("group", "wide", "narrow")),
    )
    return jax.shard_map(
        per_device,
        mesh=mesh,
        in_specs=placed,
        out_specs=P(("group", "wide"), "narrow", None),
        check_vma=False,
    )
```

```python
import functools

import jax
import jax.numpy as jnp
from jax import lax
from jax.experimental import pallas as pl
from jax.experimental.pallas import tpu as pltpu
from jax.sharding import PartitionSpec as P

HEADS = 4
HEAD = 128
ROW = 128
BLK = 256
BX = 8
BY = 32
EPS = 1e-06
GAP = 16
LINE = GAP + BY

F32 = jnp.float32
BF16 = jnp.bfloat16


def dot(a, b):
    return jnp.dot(a, b, preferred_element_type=F32)


def dot_t(a, b):
    return lax.dot_general(a, b, (((0,), (0,)), ((), ())), preferred_element_type=F32)


def dot_nt(a, b):
    return lax.dot_general(a, b, (((1,), (1,)), ((), ())), preferred_element_type=F32)


TOTALS_KIB = 50688


def params(kib=24 * 1024):
    return pltpu.CompilerParams(vmem_limit_bytes=kib << 10)


def head_cols(h):
    return slice(h * HEAD, (h + 1) * HEAD)


def in_two(array):
    high = array.astype(BF16)
    return high, (array - high.astype(F32)).astype(BF16)


def totals_kernel(spans, x_ref, w_ref, *refs):
    refs = list(refs)
    take = lambda n: [refs.pop(0) for _ in range(n)]
    xs, ws = take(len(spans)), take(3)
    totals, sems = refs[:-1], refs[-1]
    inner = HEADS * HEAD
    loads = [
        pltpu.make_async_copy(x_ref.at[pl.ds(first * BLK, count * BLK)], x, sems.at[n])
        for n, ((first, count), x) in enumerate(zip(spans, xs))
    ]
    w_loads = [
        pltpu.make_async_copy(
            w_ref.at[:, pl.ds(part * inner, inner)], w, sems.at[len(spans) + part]
        )
        for part, w in enumerate(ws)
    ]
    for load in loads + w_loads[::-1]:
        load.start()
    gram = 0.0
    for x, load in zip(xs, loads):
        load.wait()
        gram = gram + dot_t(x[...], x[...])
    w_loads[2].wait()
    weighed = sum(dot(part, ws[2][...]) for part in in_two(gram)).astype(BF16)
    w_loads[1].wait()
    cores, share = len(totals), HEADS // len(totals)
    for n in range(cores):
        cols = slice(n * share * HEAD, (n + 1) * share * HEAD)
        outer = dot_t(ws[1][:, cols], weighed[:, cols])
        for k, total_ref in enumerate(totals):

            @pl.when((lax.axis_index("narrow") + k) % cores == n)
            def _(total_ref=total_ref, outer=outer):
                for j in range(share):
                    total_ref[j] = outer[head_cols(j), head_cols(j)].astype(BF16)

    w_loads[0].wait()


def device_totals(spans, voxels, w_qkv, cores):
    width = voxels.shape[1]
    inner = HEADS * HEAD
    hbm = pl.BlockSpec(memory_space=pl.ANY)
    vmem = pl.BlockSpec(memory_space=pltpu.VMEM)
    out_shape = [jax.ShapeDtypeStruct((count * BLK, width), BF16) for _, count in spans]
    out_shape += [jax.ShapeDtypeStruct((width, inner), BF16)] * 3
    out_shape += [jax.ShapeDtypeStruct((HEADS // cores, HEAD, HEAD), BF16)] * cores
    outs = list(
        pl.pallas_call(
            functools.partial(totals_kernel, spans),
            in_specs=[hbm, hbm],
            out_specs=[vmem] * len(out_shape),
            out_shape=out_shape,
            scratch_shapes=[pltpu.SemaphoreType.DMA((len(spans) + 3,))],
            compiler_params=params(TOTALS_KIB),
            name="device_totals",
        )(voxels, w_qkv)
    )
    n = len(spans)
    return outs[:n], outs[n : n + 3], outs[n + 3 :]


PAIR = 2 * HEAD


def local_kernel(count, starts, ends, x_ref, wq_ref, wk_ref, wv_ref, *refs):
    refs = list(refs)
    before_ref = None if starts else refs.pop(0)
    q_ref, part_ref = refs[:2]
    k, v = refs[-2:]
    causal = lax.broadcasted_iota(jnp.int32, (BLK, BLK), 0) >= lax.broadcasted_iota(
        jnp.int32, (BLK, BLK), 1
    )
    same_head = ones_blocks(PAIR) > 0
    q = dot(x_ref[...], wq_ref[...]).astype(BF16)
    q_ref[...] = q
    k[...] = dot(x_ref[...], wk_ref[...]).astype(BF16)
    v[...] = dot(x_ref[...], wv_ref[...]).astype(BF16)
    for pair in range(HEADS // 2):
        both = slice(pair * PAIR, (pair + 1) * PAIR)
        state = None if starts else before_ref[pair]
        for b in range(count):
            rows = slice(b * BLK, (b + 1) * BLK)
            if state is not None:
                carried = dot(q[rows, both], jnp.where(same_head, state, 0.0).astype(BF16))
            for h in range(2):
                cols = head_cols(2 * pair + h)
                scores = dot_nt(q[rows, cols], k[rows, cols])
                scores = jnp.where(causal, scores, 0.0).astype(BF16)
                attended = dot(scores, v[rows, cols])
                if state is not None:
                    attended += carried[:, head_cols(h)]
                part_ref[rows, cols] = attended
            if not (ends and b == count - 1):
                outer = dot_t(k[rows, both], v[rows, both])
                state = outer if state is None else state + outer
        if not ends:
            refs[2][pair] = state


def local_attention(x, ws, before, ends):
    rows, width = x.shape
    inner = HEADS * HEAD
    vmem = pl.BlockSpec(memory_space=pltpu.VMEM)
    inputs = [x, *ws] + ([] if before is None else [before])
    out_shape = [
        jax.ShapeDtypeStruct((rows, inner), BF16),
        jax.ShapeDtypeStruct((rows, inner), F32),
    ]
    if not ends:
        out_shape.append(jax.ShapeDtypeStruct((HEADS // 2, PAIR, PAIR), F32))
    return pl.pallas_call(
        functools.partial(local_kernel, rows // BLK, before is None, ends),
        in_specs=[vmem] * len(inputs),
        out_specs=[vmem] * len(out_shape),
        out_shape=out_shape,
        scratch_shapes=[pltpu.VMEM((rows, inner), BF16)] * 2,
        compiler_params=params(),
        cost_estimate=pl.CostEstimate(
            flops=2 * rows * inner * (3 * width + 2 * BLK + 2 * HEAD),
            bytes_accessed=rows * inner * 12,
            transcendentals=0,
        ),
        name="local_attention",
    )(*inputs)


def direct_kernel(*refs):
    count = len(refs) // 2 - 1
    xs, (wo_ref, wf_ref), outs = refs[:count], refs[count : count + 2], refs[count + 2 :]
    for x, out in zip(xs, outs):
        out[...] = dot(x[...], wf_ref[...])
    outs[-1][...] = dot(wo_ref[...], wf_ref[...]).astype(BF16)


def direct_features(xs, w_out, w_feature):
    channels = w_feature.shape[1]
    vmem = pl.BlockSpec(memory_space=pltpu.VMEM)
    rows = sum(x.shape[0] for x in xs)
    return pl.pallas_call(
        direct_kernel,
        in_specs=[vmem] * (len(xs) + 2),
        out_specs=[vmem] * (len(xs) + 1),
        out_shape=[jax.ShapeDtypeStruct((x.shape[0], channels), F32) for x in xs]
        + [jax.ShapeDtypeStruct(w_feature.shape, BF16)],
        compiler_params=params(),
        cost_estimate=pl.CostEstimate(
            flops=2 * (rows + w_out.shape[0]) * w_out.shape[1] * channels,
            bytes_accessed=rows * channels * 8,
            transcendentals=0,
        ),
        name="direct_features",
    )(*xs, w_out, w_feature)


def gather_kernel(*refs):
    ins, (running_ref, packed_ref) = refs[:-2], refs[-2:]
    running = sum(ref[...].astype(F32) for ref in ins)
    running_ref[...] = running
    packed_ref[...] = running.astype(BF16)


def earlier_sum(bits, others):
    digit = (lax.axis_index("wide") >> bits[0]) & ((1 << len(bits)) - 1)
    return sum(
        ((digit ^ (k + 1)) < digit).astype(F32) * other for k, other in enumerate(others)
    )


def scan_kernel(bits, count, running_ref, before_ref, *refs):
    others = [ref[...].astype(F32) for ref in refs[:count]]
    new_before, packed, *new_running = refs[count:]
    running = running_ref[...] + sum(others)
    packed[...] = running.astype(BF16)
    for ref in new_running:
        ref[...] = running
    new_before[...] = before_ref[...] + earlier_sum(bits, others)


def spread_kernel(cores, bits, count, before_ref, *refs):
    others = [ref[...].astype(F32) for ref in refs[:count]]
    pieces, outs = refs[count : count + cores], refs[count + cores :]
    place = lax.axis_index("narrow")
    before = before_ref[...] + earlier_sum(bits, others)
    for k, out in enumerate(outs):
        receiver = (place + k) % cores
        value = before
        for j, piece in enumerate(pieces):
            source = (place - j + cores) % cores
            value = value + jnp.where(source < receiver, 1.0, 0.0) * piece[...].astype(F32)
        out[...] = value.astype(BF16)


def small_call(kernel, name, inputs, dtypes, shape):
    vmem = pl.BlockSpec(memory_space=pltpu.VMEM)
    smem = pl.BlockSpec(memory_space=pltpu.SMEM)
    return pl.pallas_call(
        kernel,
        in_specs=[smem if array.dtype == jnp.int32 else vmem for array in inputs],
        out_specs=[vmem] * len(dtypes),
        out_shape=[jax.ShapeDtypeStruct(shape, dtype) for dtype in dtypes],
        compiler_params=params(4 * 1024),
        name=name,
    )(*inputs)


def ones_blocks(width):
    rows, cols = (lax.broadcasted_iota(jnp.int32, (width, width), axis) for axis in range(2))
    return jnp.where(rows // HEAD == cols // HEAD, 1.0, 0.0).astype(BF16)


def block_state(state_ref, scratch):
    scratch[...] = jnp.zeros_like(scratch)
    for j in range(state_ref.shape[0]):
        scratch[head_cols(j), head_cols(j)] = state_ref[j]
    return scratch[...]


def norm_share(q, part, state, ones):
    attended = part + dot(q, state)
    squares = dot((attended * attended).astype(BF16), ones)
    return (attended * lax.rsqrt(squares * (1 / HEAD) + EPS)).astype(BF16)


def share_columns(cores, before):
    width = HEADS // cores * HEAD
    owner = (lax.axis_index("narrow") - before + cores) % cores
    return pl.ds(pl.multiple_of(owner * width, width), width)


def own_share_kernel(cores, state_ref, w_ref, *refs):
    pieces = len(refs) // 4
    qs, parts, direct, outs = (refs[i * pieces : (i + 1) * pieces] for i in range(4))
    scratch = refs[-1]
    cols = share_columns(cores, 0)
    state, ones = block_state(state_ref, scratch), ones_blocks(scratch.shape[0])
    for q, part, start, out in zip(qs, parts, direct, outs):
        normed = norm_share(q[:, cols], part[:, cols], state, ones)
        out[...] = start[...] + dot(normed, w_ref[cols, :])


def own_share(cores, state, weights, qs, parts, direct):
    width = HEADS // cores * HEAD
    vmem = pl.BlockSpec(memory_space=pltpu.VMEM)
    rows = sum(q.shape[0] for q in qs)
    return pl.pallas_call(
        functools.partial(own_share_kernel, cores),
        in_specs=[vmem] * (2 + 3 * len(qs)),
        out_specs=[vmem] * len(qs),
        out_shape=[jax.ShapeDtypeStruct(start.shape, F32) for start in direct],
        scratch_shapes=[pltpu.VMEM((width, width), BF16)],
        compiler_params=params(),
        cost_estimate=pl.CostEstimate(
            flops=6 * rows * width * width, bytes_accessed=rows * width * 8, transcendentals=0
        ),
        name="own_share",
    )(state, weights, *qs, *parts, *direct)


def list_rows(brick_ref, most, slots, fill):
    for i in range(slots.shape[0]):
        slots[i] = -1
    for b in range(fill.shape[0]):
        fill[b] = 0
    for r in range(brick_ref.shape[0]):
        brick = brick_ref[r] ^ lax.axis_index("wide")
        used = fill[brick]
        slots[brick * most + used] = r
        fill[brick] = used + 1


def cell_numbers(middle):
    number = lax.broadcasted_iota(jnp.int32, (BX * BY // 2, 1), 0)
    if middle:
        return number + 2 * BY
    return number + jnp.where(number < 2 * BY, 0, BX * BY // 2)


def cell_sums(brick, numbers, most, slots, cell_ref, features_ref):
    onehots, rows = [], []
    for j in range(most):
        row = slots[brick * most + j]
        at = jnp.maximum(row, 0)
        match = (numbers == cell_ref[at]) & (row >= 0)
        onehots.append(jnp.where(match, 1.0, 0.0).astype(BF16))
        rows.append(features_ref[pl.ds(pl.multiple_of(at * ROW, ROW), ROW), :])
    return dot(jnp.concatenate(onehots, axis=1), jnp.concatenate(rows, axis=0)).astype(BF16)


def pool_into(outs, brick_ref, cell_ref, features_ref, slots, fill):
    most = slots.shape[0] // fill.shape[0]
    list_rows(brick_ref, most, slots, fill)
    for bricks, middle, out in outs:
        numbers = cell_numbers(middle)
        for n, brick in enumerate(bricks):
            out[n] = cell_sums(brick, numbers, most, slots, cell_ref, features_ref)


def features_kernel(bricks, spans, cores, brick_ref, *refs):
    pieces = len(spans)
    refs = list(refs)
    take = lambda n: [refs.pop(0) for _ in range(n)]
    q_refs, part_refs, own_refs = (take(pieces) for _ in range(3))
    state_refs = take(cores - 1)
    w_ref, cell_ref, features_ref, out = take(4)
    scratch, slots, fill = refs
    shares = [share_columns(cores, k) for k in range(cores)]
    ones = ones_blocks(scratch.shape[1])
    states = [block_state(ref, scratch.at[k]) for k, ref in enumerate(state_refs)]
    for n, (first, count) in enumerate(spans):
        features = own_refs[n][...]
        for state, cols in zip(states, shares[1:]):
            normed = norm_share(q_refs[n][:, cols], part_refs[n][:, cols], state, ones)
            features += dot(normed, w_ref[cols, :])
        features_ref[first * BLK : (first + count) * BLK] = features.astype(BF16)
    pool_into([(bricks, False, out)], brick_ref, cell_ref, features_ref, slots, fill)


def list_scratch(count, most):
    return [pltpu.SMEM((count * most,), jnp.int32), pltpu.SMEM((count,), jnp.int32)]


def sums_shape(count, channels):
    return jax.ShapeDtypeStruct((count, BX * BY // 2, channels), BF16)


def voxel_features(
    spans, bricks, qs, parts, own, states, weights, cell_rows, chosen, count, most
):
    tokens, channels = sum(q.shape[0] for q in qs), weights.shape[1]
    cores = len(states) + 1
    width = HEADS // cores * HEAD
    vmem = pl.BlockSpec(memory_space=pltpu.VMEM)
    smem = pl.BlockSpec(memory_space=pltpu.SMEM)
    return pl.pallas_call(
        functools.partial(features_kernel, chosen, spans, cores),
        in_specs=[smem] + [vmem] * (3 * len(spans) + cores + 1),
        out_specs=[vmem] * 2,
        out_shape=[
            jax.ShapeDtypeStruct((tokens, channels), BF16),
            sums_shape(len(chosen), channels),
        ],
        scratch_shapes=[pltpu.VMEM((max(1, cores - 1), width, width), BF16)]
        + list_scratch(count, most),
        compiler_params=params(),
        name="voxel_features",
    )(bricks, *qs, *parts, *own, *states, weights, cell_rows)


def pool_kernel(chosen, brick_ref, cell_ref, features_ref, *refs):
    outs, (slots, fill) = refs[:-2], refs[-2:]
    pool_into(
        [(bricks, middle, out) for (bricks, middle), out in zip(chosen, outs)],
        brick_ref,
        cell_ref,
        features_ref,
        slots,
        fill,
    )


def pool(bricks, cell_rows, features, chosen, count, most):
    tokens, channels = features.shape
    vmem = pl.BlockSpec(memory_space=pltpu.VMEM)
    smem = pl.BlockSpec(memory_space=pltpu.SMEM)
    return pl.pallas_call(
        functools.partial(pool_kernel, chosen),
        in_specs=[smem, vmem, vmem],
        out_specs=[vmem] * len(chosen),
        out_shape=[sums_shape(len(which), channels) for which, _ in chosen],
        scratch_shapes=list_scratch(count, most),
        compiler_params=params(),
        cost_estimate=pl.CostEstimate(
            flops=sum(len(which) for which, _ in chosen) * most * ROW * BX * BY * channels,
            bytes_accessed=tokens * channels * 2,
            transcendentals=0,
        ),
        name="pool",
    )(bricks, cell_rows, features)


def convolve(field, w_ref, start, count):
    lhs = jnp.concatenate(
        [field[start + dy * LINE : start + dy * LINE + count] for dy in (-1, 0, 1)], axis=1
    )
    left, middle, right = weighted(lhs, w_ref)
    return pltpu.roll(left, 1, 0) + middle + pltpu.roll(right, count - 1, 0)


def weighted(lhs, w_ref):
    return [
        dot(lhs, jnp.concatenate([w_ref[dy, dx] for dy in range(3)], axis=0)) for dx in range(3)
    ]


def own_columns_kernel(lines_ref, w_ref, out_ref, field):
    lines = lines_ref.shape[0]
    for r in range(lines):
        field[r * LINE : r * LINE + GAP] = jnp.zeros((GAP, field.shape[1]), BF16)
        field[r * LINE + GAP : (r + 1) * LINE] = lines_ref[r]
    field[lines * LINE :] = jnp.zeros((GAP, field.shape[1]), BF16)
    out_ref[...] = convolve(field, w_ref, LINE, out_ref.shape[0])


def own_columns(lines, conv_first):
    count, _, channels = lines.shape
    vmem = pl.BlockSpec(memory_space=pltpu.VMEM)
    shown = (count - 2) * LINE + GAP
    return pl.pallas_call(
        own_columns_kernel,
        in_specs=[vmem] * 2,
        out_specs=vmem,
        out_shape=jax.ShapeDtypeStruct((shown, channels), F32),
        scratch_shapes=[pltpu.VMEM((count * LINE + GAP, channels), BF16)],
        compiler_params=params(16 * 1024),
        cost_estimate=pl.CostEstimate(
            flops=18 * shown * channels * channels,
            bytes_accessed=shown * channels * 8,
            transcendentals=0,
        ),
        name="own_columns",
    )(lines, conv_first)


def field_kernel(first_ref, sides_ref, w1_ref, w2_ref, out_ref, first, field):
    count, channels = first.shape
    wide, narrow = lax.axis_index("wide"), lax.axis_index("narrow")
    first_line, last_line = wide == 0, wide == lax.axis_size("wide") - 1
    first_column, last_column = narrow == 0, narrow == lax.axis_size("narrow") - 1
    gaps = sides_ref.shape[0] - 2
    sides = sides_ref[...].reshape((gaps + 2) * GAP, channels)
    lhs = jnp.concatenate([sides[dy * GAP : (dy + gaps) * GAP] for dy in range(3)], axis=1)
    none = jnp.zeros((8, channels), F32)
    left, middle, right = [
        jnp.concatenate(
            [part for g in range(gaps) for part in (none, given[g * GAP : (g + 1) * GAP], none)],
            axis=0,
        )
        for given in weighted(lhs, w1_ref)
    ]
    span = GAP + 16
    added = pltpu.roll(left, 1, 0) + middle + pltpu.roll(right, gaps * span - 1, 0)
    first[...] = first_ref[...]
    for g in range(gaps):
        start, stop = max(g * LINE - 8, 0), min(g * LINE + GAP + 8, count)
        at = g * span + 8 - g * LINE
        first[start:stop] += added[start + at : stop + at]
    inner = jax.nn.gelu(first[...], approximate=True)
    at = lax.broadcasted_iota(jnp.int32, (count, 1), 0)
    outside = first_line & (at <= LINE) | last_line & (at > (BX + 1) * LINE)
    for r in range(BX + 2):
        outside |= first_column & (at == r * LINE + GAP - 1)
        outside |= last_column & (at == (r + 1) * LINE)
    field[...] = jnp.where(outside, 0.0, inner).astype(BF16)
    flow = convolve(field, w2_ref, LINE, BX * LINE + GAP)
    for r in range(BX):
        out_ref[r] = flow[r * LINE + GAP : (r + 1) * LINE]


def field_flow(first, left, right, conv_first, conv_second):
    count, channels = first.shape
    vmem = pl.BlockSpec(memory_space=pltpu.VMEM)
    sides = jnp.pad(right, ((1, 0), (0, GAP - 2), (0, 0))) + jnp.pad(
        left, ((0, 1), (GAP - 2, 0), (0, 0))
    )
    return pl.pallas_call(
        field_kernel,
        in_specs=[vmem] * 4,
        out_specs=vmem,
        out_shape=jax.ShapeDtypeStruct((BX, BY, channels), F32),
        scratch_shapes=[pltpu.VMEM((count, channels), F32), pltpu.VMEM((count, channels), BF16)],
        compiler_params=params(16 * 1024),
        name="field_flow",
    )(first, sides, conv_first, conv_second)


def swap(array, axis, bit):
    count = lax.axis_size(axis)
    return lax.ppermute(array, axis, [(i, i ^ (1 << bit)) for i in range(count)])


def swap_digit(array, axis, bit, by):
    count = lax.axis_size(axis)
    return lax.ppermute(array, axis, [(i, i ^ (by << bit)) for i in range(count)])


def shift(array, axis, by):
    count = lax.axis_size(axis)
    return lax.ppermute(
        array, axis, [(i, i + by) for i in range(count) if 0 <= i + by < count]
    )


def rotate(array, axis, by):
    count = lax.axis_size(axis)
    return lax.ppermute(array, axis, [(i, (i + by) % count) for i in range(count)])


def side_columns(lines):
    if lax.axis_size("narrow") != 2:
        return shift(lines[:, BY - 2 :], "narrow", 1), shift(lines[:, :2], "narrow", -1)
    first = lax.axis_index("narrow") == 0
    other = swap(jnp.where(first, lines[:, BY - 2 :], lines[:, :2]), "narrow", 0)
    nothing = jnp.zeros_like(other)
    return jnp.where(first, nothing, other), jnp.where(first, other, nothing)


def exchange_lines(strip, with_it):
    groups, count, cores = (lax.axis_size(axis) for axis in ("group", "wide", "narrow"))
    place = lax.axis_index("wide")
    got = []
    for start in range(2):
        pairs = []
        for g in range(groups):
            for w in range(count):
                other = w + 1 if w % 2 == start else w - 1
                far = g
                if not 0 <= other < count:
                    other, far = w, g ^ 1 if groups % 2 == 0 else g
                for c in range(cores):
                    pairs.append(((g * count + w) * cores + c, (far * count + other) * cores + c))
        upper = place % 2 == start
        out = jnp.where(upper, strip[2:], strip[:2])
        got.append(lax.ppermute(out, ("group", "wide", "narrow"), pairs))
    got, with_it = lax.optimization_barrier((got, with_it))
    above = jnp.where(place % 2 == 1, got[0], got[1])
    below = jnp.where(place % 2 == 1, got[1], got[0])
    above = jnp.where(place > 0, above, jnp.zeros_like(above))
    below = jnp.where(place < count - 1, below, jnp.zeros_like(below))
    return above, below, with_it


def earlier_state(totals, first_work, works):
    cores, shape = len(totals), totals[0].shape
    works, done = list(works), []

    def beside(work, arrays, exchange):
        held, arrays = work(arrays)
        done.append(held)
        held, arrived = lax.optimization_barrier((held, exchange(arrays)))
        done[-1] = held
        return arrived

    others = beside(
        first_work,
        totals[1:],
        lambda arrays: [rotate(array, "narrow", k + 1) for k, array in enumerate(arrays)],
    )
    pieces = [totals[0]] + others
    running, packed = small_call(gather_kernel, "gather", pieces, [F32, BF16], shape)
    before = jnp.zeros(shape, F32)
    count = lax.axis_size("wide").bit_length() - 1
    levels = [list(range(bit, min(bit + 2, count))) for bit in range(0, count, 2)]
    for level, bits in enumerate(levels):
        exchange = lambda packed: [
            swap_digit(packed, "wide", bits[0], k) for k in range(1, 1 << len(bits))
        ]
        others = beside(works.pop(0), packed, exchange) if works else exchange(packed)
        if level == len(levels) - 1:
            break
        before, packed, *more = small_call(
            functools.partial(scan_kernel, bits, len(others)),
            "scan",
            [running, before] + others,
            [F32, BF16] + [F32] * (level < len(levels) - 2),
            shape,
        )
        running = more[0] if more else None
    outs = small_call(
        functools.partial(spread_kernel, cores, bits, len(others)),
        "spread",
        [before] + others + pieces,
        [BF16] * cores,
        shape,
    )
    states = [outs[0]] + [rotate(outs[k], "narrow", k) for k in range(1, cores)]
    while works:
        done.append(works.pop(0)(outs[0])[0])
    return states, done


def split_order(order):
    half = 1 << (len(order) - 1)
    place = lambda slot: sum(
        ((slot >> (len(order) - 1 - i)) & 1) << bit for i, bit in enumerate(order)
    )
    return [place(slot) for slot in range(half)], [place(slot) for slot in range(half, 2 * half)]


def reduce_level(stays, goes, bit, with_it=None):
    arrived = [swap(array, "wide", bit) for array in reversed(goes)][::-1]
    if with_it is not None:
        arrived, with_it = lax.optimization_barrier((arrived, with_it))
    sums = [
        (here.astype(F32) + more.astype(F32)).astype(BF16) for here, more in zip(stays, arrived)
    ]
    return sums, with_it


def next_level(sums):
    if len(sums) == 1:
        half = sums[0].shape[0] // 2
        return [sums[0][:half]], [sums[0][half:]]
    return sums[:1], sums[1:]


def reduce_both(outer, middle, orders):
    levels = len(orders[0])
    outer_sums, _ = reduce_level(*outer, orders[0][0])
    stays, (later, first) = middle
    later, outer_sums[-1] = lax.optimization_barrier((later, outer_sums[-1]))
    middle = stays, [later, first]
    outer = next_level(outer_sums)
    for level in range(1, levels):
        middle_sums, _ = reduce_level(*middle, orders[1][level - 1])
        middle = next_level(middle_sums)
        if level > 1:
            outer_sums, middle = reduce_level(*outer, orders[0][level], middle)
        else:
            outer_sums, _ = reduce_level(*outer, orders[0][level])
        outer = next_level(outer_sums)
    return outer_sums[0][0], reduce_level(*middle, orders[1][-1])[0][0][0]


def per_device(voxels, w_qkv, w_out, w_feature, conv_first, conv_second, row_brick, cell_place):
    tokens = voxels.shape[0]
    channels = w_feature.shape[1]
    wide_count, wide_place = lax.axis_size("wide"), lax.axis_index("wide")
    narrow_count, narrow_place = lax.axis_size("narrow"), lax.axis_index("narrow")

    blocks = tokens // BLK
    cuts = sorted({blocks * i // 2 for i in range(3)})
    spans = [(first, last - first) for first, last in zip(cuts, cuts[1:])]
    xs, ws, totals = device_totals(spans, voxels, w_qkv, narrow_count)

    def direct(arrays):
        arrays, x = lax.optimization_barrier((arrays, xs[0]))
        return direct_features([x] + xs[1:], w_out, w_feature), arrays

    after = [None]

    def work(n):
        def run(array):
            array, x = lax.optimization_barrier((array, xs[n]))
            piece = local_attention(x, ws, after[-1], n == len(spans) - 1)
            after.append(piece[-1])
            return piece, array

        return run

    states, done = earlier_state(totals, direct, [work(n) for n in range(len(spans))])
    own, weights = done[0][:-1], done[0][-1]
    qs, parts = ([piece[i] for piece in done[1:]] for i in range(2))
    own = own_share(narrow_count, states[0], weights, qs, parts, own)

    bits = list(range(wide_count.bit_length() - 1))
    orders = [bits, bits[1::-1] + bits[2:]]
    halves = lambda places: (places[: len(places) // 2], places[len(places) // 2 :])
    stay, go = zip(*(map(halves, split_order(order)) for order in orders))
    cell_rows = cell_place.reshape(-1, 1, ROW)
    most = max(2, 2 * (tokens // ROW) // wide_count)
    bricks = row_brick[:, 0]
    features, outer_first = voxel_features(
        spans, bricks, qs, parts, own, states[1:], weights, cell_rows, go[0][1], wide_count, most
    )
    pooled = lambda *chosen: pool(bricks, cell_rows, features, chosen, wide_count, most)
    middle_first, outer_later, middle_later, *sums = pooled(
        (go[1][1], True),
        (go[0][0], False),
        (go[1][0], True),
        *((stay[middle][n], middle == 1) for middle in range(2) for n in range(2)),
    )
    outer, middle = reduce_both(
        (sums[:2], [outer_later, outer_first]), (sums[2:], [middle_later, middle_first]), orders
    )
    outer, middle = (part.reshape(-1, BY, channels) for part in (outer, middle))
    above, below, middle = exchange_lines(outer, middle)
    lines = jnp.concatenate([above, outer[:2], middle, outer[2:], below], axis=0)
    left, right = side_columns(lines)
    return field_flow(own_columns(lines, conv_first), left, right, conv_first, conv_second)


def solution(mesh):
    placed = (
        P(("group", "wide", "narrow"), None),
        P(),
        P(),
        P(),
        P(),
        P(),
        P(("group", "wide", "narrow"), None),
        P(("group", "wide", "narrow")),
    )
    return jax.shard_map(
        per_device,
        mesh=mesh,
        in_specs=placed,
        out_specs=P(("group", "wide"), "narrow", None),
        check_vma=False,
    )
```

```python
import functools

import jax
import jax.numpy as jnp
from jax import lax
from jax.experimental import pallas as pl
from jax.experimental.pallas import tpu as pltpu
from jax.sharding import PartitionSpec as P

HEADS = 4
HEAD = 128
ROW = 128
BLK = 256
BX = 8
BY = 32
EPS = 1e-06
GAP = 16
LINE = GAP + BY

F32 = jnp.float32
BF16 = jnp.bfloat16


def dot(a, b):
    return jnp.dot(a, b, preferred_element_type=F32)


def dot_t(a, b):
    return lax.dot_general(a, b, (((0,), (0,)), ((), ())), preferred_element_type=F32)


def dot_nt(a, b):
    return lax.dot_general(a, b, (((1,), (1,)), ((), ())), preferred_element_type=F32)


TOTALS_KIB = 50688


def params(kib=24 * 1024):
    return pltpu.CompilerParams(vmem_limit_bytes=kib << 10)


def head_cols(h):
    return slice(h * HEAD, (h + 1) * HEAD)


def in_two(array):
    high = array.astype(BF16)
    return high, (array - high.astype(F32)).astype(BF16)


def totals_kernel(spans, x_ref, w_ref, *refs):
    refs = list(refs)
    take = lambda n: [refs.pop(0) for _ in range(n)]
    xs, ws = take(len(spans)), take(3)
    totals, sems = refs[:-1], refs[-1]
    inner = HEADS * HEAD
    loads = [
        pltpu.make_async_copy(x_ref.at[pl.ds(first * BLK, count * BLK)], x, sems.at[n])
        for n, ((first, count), x) in enumerate(zip(spans, xs))
    ]
    w_loads = [
        pltpu.make_async_copy(
            w_ref.at[:, pl.ds(part * inner, inner)], w, sems.at[len(spans) + part]
        )
        for part, w in enumerate(ws)
    ]
    for load in loads + w_loads[::-1]:
        load.start()
    gram = 0.0
    for x, load in zip(xs, loads):
        load.wait()
        gram = gram + dot_t(x[...], x[...])
    w_loads[2].wait()
    weighed = sum(dot(part, ws[2][...]) for part in in_two(gram)).astype(BF16)
    w_loads[1].wait()
    cores, share = len(totals), HEADS // len(totals)
    for n in range(cores):
        cols = slice(n * share * HEAD, (n + 1) * share * HEAD)
        outer = dot_t(ws[1][:, cols], weighed[:, cols])
        for k, total_ref in enumerate(totals):

            @pl.when((lax.axis_index("narrow") + k) % cores == n)
            def _(total_ref=total_ref, outer=outer):
                for j in range(share):
                    total_ref[j] = outer[head_cols(j), head_cols(j)].astype(BF16)

    w_loads[0].wait()


def device_totals(spans, voxels, w_qkv, cores):
    width = voxels.shape[1]
    inner = HEADS * HEAD
    hbm = pl.BlockSpec(memory_space=pl.ANY)
    vmem = pl.BlockSpec(memory_space=pltpu.VMEM)
    out_shape = [jax.ShapeDtypeStruct((count * BLK, width), BF16) for _, count in spans]
    out_shape += [jax.ShapeDtypeStruct((width, inner), BF16)] * 3
    out_shape += [jax.ShapeDtypeStruct((HEADS // cores, HEAD, HEAD), BF16)] * cores
    outs = list(
        pl.pallas_call(
            functools.partial(totals_kernel, spans),
            in_specs=[hbm, hbm],
            out_specs=[vmem] * len(out_shape),
            out_shape=out_shape,
            scratch_shapes=[pltpu.SemaphoreType.DMA((len(spans) + 3,))],
            compiler_params=params(TOTALS_KIB),
            name="device_totals",
        )(voxels, w_qkv)
    )
    n = len(spans)
    return outs[:n], outs[n : n + 3], outs[n + 3 :]


PAIR = 2 * HEAD


def local_kernel(count, starts, ends, x_ref, wq_ref, wk_ref, wv_ref, *refs):
    refs = list(refs)
    before_ref = None if starts else refs.pop(0)
    q_ref, part_ref = refs[:2]
    k, v = refs[-2:]
    causal = lax.broadcasted_iota(jnp.int32, (BLK, BLK), 0) >= lax.broadcasted_iota(
        jnp.int32, (BLK, BLK), 1
    )
    same_head = ones_blocks(PAIR) > 0
    q = dot(x_ref[...], wq_ref[...]).astype(BF16)
    q_ref[...] = q
    k[...] = dot(x_ref[...], wk_ref[...]).astype(BF16)
    v[...] = dot(x_ref[...], wv_ref[...]).astype(BF16)
    pairs = [slice(pair * PAIR, (pair + 1) * PAIR) for pair in range(HEADS // 2)]
    states = None if starts else [before_ref[pair] for pair in range(HEADS // 2)]
    for b in range(count):
        rows = slice(b * BLK, (b + 1) * BLK)
        scores = [dot_nt(q[rows, head_cols(h)], k[rows, head_cols(h)]) for h in range(HEADS)]
        if states is not None:
            carried = [
                dot(q[rows, both], jnp.where(same_head, state, 0.0).astype(BF16))
                for both, state in zip(pairs, states)
            ]
        scores = [jnp.where(causal, score, 0.0).astype(BF16) for score in scores]
        attended = [dot(score, v[rows, head_cols(h)]) for h, score in enumerate(scores)]
        for h in range(HEADS):
            if states is not None:
                attended[h] += carried[h // 2][:, head_cols(h % 2)]
            part_ref[rows, head_cols(h)] = attended[h]
        if not (ends and b == count - 1):
            outer = [dot_t(k[rows, both], v[rows, both]) for both in pairs]
            states = outer if states is None else [x + y for x, y in zip(states, outer)]
    if not ends:
        for pair, state in enumerate(states):
            refs[2][pair] = state


def local_attention(x, ws, before, ends):
    rows, width = x.shape
    inner = HEADS * HEAD
    vmem = pl.BlockSpec(memory_space=pltpu.VMEM)
    inputs = [x, *ws] + ([] if before is None else [before])
    out_shape = [
        jax.ShapeDtypeStruct((rows, inner), BF16),
        jax.ShapeDtypeStruct((rows, inner), F32),
    ]
    if not ends:
        out_shape.append(jax.ShapeDtypeStruct((HEADS // 2, PAIR, PAIR), F32))
    return pl.pallas_call(
        functools.partial(local_kernel, rows // BLK, before is None, ends),
        in_specs=[vmem] * len(inputs),
        out_specs=[vmem] * len(out_shape),
        out_shape=out_shape,
        scratch_shapes=[pltpu.VMEM((rows, inner), BF16)] * 2,
        compiler_params=params(),
        cost_estimate=pl.CostEstimate(
            flops=2 * rows * inner * (3 * width + 2 * BLK + 2 * HEAD),
            bytes_accessed=rows * inner * 12,
            transcendentals=0,
        ),
        name="local_attention",
    )(*inputs)


def direct_kernel(*refs):
    count = len(refs) // 2 - 1
    xs, (wo_ref, wf_ref), outs = refs[:count], refs[count : count + 2], refs[count + 2 :]
    for x, out in zip(xs, outs):
        out[...] = dot(x[...], wf_ref[...])
    outs[-1][...] = dot(wo_ref[...], wf_ref[...]).astype(BF16)


def direct_features(xs, w_out, w_feature):
    channels = w_feature.shape[1]
    vmem = pl.BlockSpec(memory_space=pltpu.VMEM)
    rows = sum(x.shape[0] for x in xs)
    return pl.pallas_call(
        direct_kernel,
        in_specs=[vmem] * (len(xs) + 2),
        out_specs=[vmem] * (len(xs) + 1),
        out_shape=[jax.ShapeDtypeStruct((x.shape[0], channels), F32) for x in xs]
        + [jax.ShapeDtypeStruct(w_feature.shape, BF16)],
        compiler_params=params(),
        cost_estimate=pl.CostEstimate(
            flops=2 * (rows + w_out.shape[0]) * w_out.shape[1] * channels,
            bytes_accessed=rows * channels * 8,
            transcendentals=0,
        ),
        name="direct_features",
    )(*xs, w_out, w_feature)


def gather_kernel(*refs):
    ins, (running_ref, packed_ref) = refs[:-2], refs[-2:]
    running = sum(ref[...].astype(F32) for ref in ins)
    running_ref[...] = running
    packed_ref[...] = running.astype(BF16)


def earlier_sum(bits, others):
    digit = (lax.axis_index("wide") >> bits[0]) & ((1 << len(bits)) - 1)
    return sum(
        ((digit ^ (k + 1)) < digit).astype(F32) * other for k, other in enumerate(others)
    )


def scan_kernel(bits, count, running_ref, before_ref, *refs):
    others = [ref[...].astype(F32) for ref in refs[:count]]
    new_before, packed, *new_running = refs[count:]
    running = running_ref[...] + sum(others)
    packed[...] = running.astype(BF16)
    for ref in new_running:
        ref[...] = running
    new_before[...] = before_ref[...] + earlier_sum(bits, others)


def spread_kernel(cores, bits, count, before_ref, *refs):
    others = [ref[...].astype(F32) for ref in refs[:count]]
    pieces, outs = refs[count : count + cores], refs[count + cores :]
    place = lax.axis_index("narrow")
    before = before_ref[...] + earlier_sum(bits, others)
    for k, out in enumerate(outs):
        receiver = (place + k) % cores
        value = before
        for j, piece in enumerate(pieces):
            source = (place - j + cores) % cores
            value = value + jnp.where(source < receiver, 1.0, 0.0) * piece[...].astype(F32)
        out[...] = value.astype(BF16)


def small_call(kernel, name, inputs, dtypes, shape):
    vmem = pl.BlockSpec(memory_space=pltpu.VMEM)
    smem = pl.BlockSpec(memory_space=pltpu.SMEM)
    return pl.pallas_call(
        kernel,
        in_specs=[smem if array.dtype == jnp.int32 else vmem for array in inputs],
        out_specs=[vmem] * len(dtypes),
        out_shape=[jax.ShapeDtypeStruct(shape, dtype) for dtype in dtypes],
        compiler_params=params(4 * 1024),
        name=name,
    )(*inputs)


def ones_blocks(width):
    rows, cols = (lax.broadcasted_iota(jnp.int32, (width, width), axis) for axis in range(2))
    return jnp.where(rows // HEAD == cols // HEAD, 1.0, 0.0).astype(BF16)


def block_state(state_ref, scratch):
    scratch[...] = jnp.zeros_like(scratch)
    for j in range(state_ref.shape[0]):
        scratch[head_cols(j), head_cols(j)] = state_ref[j]
    return scratch[...]


def norm_share(q, part, state, ones):
    attended = part + dot(q, state)
    squares = dot((attended * attended).astype(BF16), ones)
    return (attended * lax.rsqrt(squares * (1 / HEAD) + EPS)).astype(BF16)


def share_columns(cores, before):
    width = HEADS // cores * HEAD
    owner = (lax.axis_index("narrow") - before + cores) % cores
    return pl.ds(pl.multiple_of(owner * width, width), width)


def own_share_kernel(cores, state_ref, w_ref, *refs):
    pieces = len(refs) // 4
    qs, parts, direct, outs = (refs[i * pieces : (i + 1) * pieces] for i in range(4))
    scratch = refs[-1]
    cols = share_columns(cores, 0)
    state, ones = block_state(state_ref, scratch), ones_blocks(scratch.shape[0])
    for q, part, start, out in zip(qs, parts, direct, outs):
        normed = norm_share(q[:, cols], part[:, cols], state, ones)
        out[...] = start[...] + dot(normed, w_ref[cols, :])


def own_share(cores, state, weights, qs, parts, direct):
    width = HEADS // cores * HEAD
    vmem = pl.BlockSpec(memory_space=pltpu.VMEM)
    rows = sum(q.shape[0] for q in qs)
    return pl.pallas_call(
        functools.partial(own_share_kernel, cores),
        in_specs=[vmem] * (2 + 3 * len(qs)),
        out_specs=[vmem] * len(qs),
        out_shape=[jax.ShapeDtypeStruct(start.shape, F32) for start in direct],
        scratch_shapes=[pltpu.VMEM((width, width), BF16)],
        compiler_params=params(),
        cost_estimate=pl.CostEstimate(
            flops=6 * rows * width * width, bytes_accessed=rows * width * 8, transcendentals=0
        ),
        name="own_share",
    )(state, weights, *qs, *parts, *direct)


def list_rows(brick_ref, most, slots, fill):
    for i in range(slots.shape[0]):
        slots[i] = -1
    for b in range(fill.shape[0]):
        fill[b] = 0
    for r in range(brick_ref.shape[0]):
        brick = brick_ref[r] ^ lax.axis_index("wide")
        used = fill[brick]
        slots[brick * most + used] = r
        fill[brick] = used + 1


def cell_numbers(middle):
    number = lax.broadcasted_iota(jnp.int32, (BX * BY // 2, 1), 0)
    if middle:
        return number + 2 * BY
    return number + jnp.where(number < 2 * BY, 0, BX * BY // 2)


def cell_sums(brick, numbers, most, slots, cell_ref, features_ref):
    onehots, rows = [], []
    for j in range(most):
        row = slots[brick * most + j]
        at = jnp.maximum(row, 0)
        match = (numbers == cell_ref[at]) & (row >= 0)
        onehots.append(jnp.where(match, 1.0, 0.0).astype(BF16))
        rows.append(features_ref[pl.ds(pl.multiple_of(at * ROW, ROW), ROW), :])
    return dot(jnp.concatenate(onehots, axis=1), jnp.concatenate(rows, axis=0)).astype(BF16)


def pool_into(outs, brick_ref, cell_ref, features_ref, slots, fill):
    most = slots.shape[0] // fill.shape[0]
    list_rows(brick_ref, most, slots, fill)
    for bricks, middle, out in outs:
        numbers = cell_numbers(middle)
        for n, brick in enumerate(bricks):
            out[n] = cell_sums(brick, numbers, most, slots, cell_ref, features_ref)


def features_kernel(bricks, spans, cores, brick_ref, *refs):
    pieces = len(spans)
    refs = list(refs)
    take = lambda n: [refs.pop(0) for _ in range(n)]
    q_refs, part_refs, own_refs = (take(pieces) for _ in range(3))
    state_refs = take(cores - 1)
    w_ref, cell_ref, features_ref, out = take(4)
    scratch, slots, fill = refs
    shares = [share_columns(cores, k) for k in range(cores)]
    ones = ones_blocks(scratch.shape[1])
    states = [block_state(ref, scratch.at[k]) for k, ref in enumerate(state_refs)]
    for n, (first, count) in enumerate(spans):
        features = own_refs[n][...]
        for state, cols in zip(states, shares[1:]):
            normed = norm_share(q_refs[n][:, cols], part_refs[n][:, cols], state, ones)
            features += dot(normed, w_ref[cols, :])
        features_ref[first * BLK : (first + count) * BLK] = features.astype(BF16)
    pool_into([(bricks, False, out)], brick_ref, cell_ref, features_ref, slots, fill)


def list_scratch(count, most):
    return [pltpu.SMEM((count * most,), jnp.int32), pltpu.SMEM((count,), jnp.int32)]


def sums_shape(count, channels):
    return jax.ShapeDtypeStruct((count, BX * BY // 2, channels), BF16)


def voxel_features(
    spans, bricks, qs, parts, own, states, weights, cell_rows, chosen, count, most
):
    tokens, channels = sum(q.shape[0] for q in qs), weights.shape[1]
    cores = len(states) + 1
    width = HEADS // cores * HEAD
    vmem = pl.BlockSpec(memory_space=pltpu.VMEM)
    smem = pl.BlockSpec(memory_space=pltpu.SMEM)
    return pl.pallas_call(
        functools.partial(features_kernel, chosen, spans, cores),
        in_specs=[smem] + [vmem] * (3 * len(spans) + cores + 1),
        out_specs=[vmem] * 2,
        out_shape=[
            jax.ShapeDtypeStruct((tokens, channels), BF16),
            sums_shape(len(chosen), channels),
        ],
        scratch_shapes=[pltpu.VMEM((max(1, cores - 1), width, width), BF16)]
        + list_scratch(count, most),
        compiler_params=params(),
        name="voxel_features",
    )(bricks, *qs, *parts, *own, *states, weights, cell_rows)


def pool_kernel(chosen, brick_ref, cell_ref, features_ref, *refs):
    outs, (slots, fill) = refs[:-2], refs[-2:]
    pool_into(
        [(bricks, middle, out) for (bricks, middle), out in zip(chosen, outs)],
        brick_ref,
        cell_ref,
        features_ref,
        slots,
        fill,
    )


def pool(bricks, cell_rows, features, chosen, count, most):
    tokens, channels = features.shape
    vmem = pl.BlockSpec(memory_space=pltpu.VMEM)
    smem = pl.BlockSpec(memory_space=pltpu.SMEM)
    return pl.pallas_call(
        functools.partial(pool_kernel, chosen),
        in_specs=[smem, vmem, vmem],
        out_specs=[vmem] * len(chosen),
        out_shape=[sums_shape(len(which), channels) for which, _ in chosen],
        scratch_shapes=list_scratch(count, most),
        compiler_params=params(),
        cost_estimate=pl.CostEstimate(
            flops=sum(len(which) for which, _ in chosen) * most * ROW * BX * BY * channels,
            bytes_accessed=tokens * channels * 2,
            transcendentals=0,
        ),
        name="pool",
    )(bricks, cell_rows, features)


def convolve(field, w_ref, start, count):
    lhs = jnp.concatenate(
        [field[start + dy * LINE : start + dy * LINE + count] for dy in (-1, 0, 1)], axis=1
    )
    left, middle, right = weighted(lhs, w_ref)
    return pltpu.roll(left, 1, 0) + middle + pltpu.roll(right, count - 1, 0)


def weighted(lhs, w_ref):
    return [
        dot(lhs, jnp.concatenate([w_ref[dy, dx] for dy in range(3)], axis=0)) for dx in range(3)
    ]


def own_columns_kernel(lines_ref, w_ref, out_ref, field):
    lines = lines_ref.shape[0]
    for r in range(lines):
        field[r * LINE : r * LINE + GAP] = jnp.zeros((GAP, field.shape[1]), BF16)
        field[r * LINE + GAP : (r + 1) * LINE] = lines_ref[r]
    field[lines * LINE :] = jnp.zeros((GAP, field.shape[1]), BF16)
    out_ref[...] = convolve(field, w_ref, LINE, out_ref.shape[0])


def own_columns(lines, conv_first):
    count, _, channels = lines.shape
    vmem = pl.BlockSpec(memory_space=pltpu.VMEM)
    shown = (count - 2) * LINE + GAP
    return pl.pallas_call(
        own_columns_kernel,
        in_specs=[vmem] * 2,
        out_specs=vmem,
        out_shape=jax.ShapeDtypeStruct((shown, channels), F32),
        scratch_shapes=[pltpu.VMEM((count * LINE + GAP, channels), BF16)],
        compiler_params=params(16 * 1024),
        cost_estimate=pl.CostEstimate(
            flops=18 * shown * channels * channels,
            bytes_accessed=shown * channels * 8,
            transcendentals=0,
        ),
        name="own_columns",
    )(lines, conv_first)


def field_kernel(first_ref, sides_ref, w1_ref, w2_ref, out_ref, first, field):
    count, channels = first.shape
    wide, narrow = lax.axis_index("wide"), lax.axis_index("narrow")
    first_line, last_line = wide == 0, wide == lax.axis_size("wide") - 1
    first_column, last_column = narrow == 0, narrow == lax.axis_size("narrow") - 1
    gaps = sides_ref.shape[0] - 2
    sides = sides_ref[...].reshape((gaps + 2) * GAP, channels)
    lhs = jnp.concatenate([sides[dy * GAP : (dy + gaps) * GAP] for dy in range(3)], axis=1)
    none = jnp.zeros((8, channels), F32)
    left, middle, right = [
        jnp.concatenate(
            [part for g in range(gaps) for part in (none, given[g * GAP : (g + 1) * GAP], none)],
            axis=0,
        )
        for given in weighted(lhs, w1_ref)
    ]
    span = GAP + 16
    added = pltpu.roll(left, 1, 0) + middle + pltpu.roll(right, gaps * span - 1, 0)
    first[...] = first_ref[...]
    for g in range(gaps):
        start, stop = max(g * LINE - 8, 0), min(g * LINE + GAP + 8, count)
        at = g * span + 8 - g * LINE
        first[start:stop] += added[start + at : stop + at]
    inner = jax.nn.gelu(first[...], approximate=True)
    at = lax.broadcasted_iota(jnp.int32, (count, 1), 0)
    outside = first_line & (at <= LINE) | last_line & (at > (BX + 1) * LINE)
    for r in range(BX + 2):
        outside |= first_column & (at == r * LINE + GAP - 1)
        outside |= last_column & (at == (r + 1) * LINE)
    field[...] = jnp.where(outside, 0.0, inner).astype(BF16)
    flow = convolve(field, w2_ref, LINE, BX * LINE + GAP)
    for r in range(BX):
        out_ref[r] = flow[r * LINE + GAP : (r + 1) * LINE]


def field_flow(first, left, right, conv_first, conv_second):
    count, channels = first.shape
    vmem = pl.BlockSpec(memory_space=pltpu.VMEM)
    sides = jnp.pad(right, ((1, 0), (0, GAP - 2), (0, 0))) + jnp.pad(
        left, ((0, 1), (GAP - 2, 0), (0, 0))
    )
    return pl.pallas_call(
        field_kernel,
        in_specs=[vmem] * 4,
        out_specs=vmem,
        out_shape=jax.ShapeDtypeStruct((BX, BY, channels), F32),
        scratch_shapes=[pltpu.VMEM((count, channels), F32), pltpu.VMEM((count, channels), BF16)],
        compiler_params=params(16 * 1024),
        name="field_flow",
    )(first, sides, conv_first, conv_second)


def swap(array, axis, bit):
    count = lax.axis_size(axis)
    return lax.ppermute(array, axis, [(i, i ^ (1 << bit)) for i in range(count)])


def swap_digit(array, axis, bit, by):
    count = lax.axis_size(axis)
    return lax.ppermute(array, axis, [(i, i ^ (by << bit)) for i in range(count)])


def shift(array, axis, by):
    count = lax.axis_size(axis)
    return lax.ppermute(
        array, axis, [(i, i + by) for i in range(count) if 0 <= i + by < count]
    )


def rotate(array, axis, by):
    count = lax.axis_size(axis)
    return lax.ppermute(array, axis, [(i, (i + by) % count) for i in range(count)])


def side_columns(lines):
    if lax.axis_size("narrow") != 2:
        return shift(lines[:, BY - 2 :], "narrow", 1), shift(lines[:, :2], "narrow", -1)
    first = lax.axis_index("narrow") == 0
    other = swap(jnp.where(first, lines[:, BY - 2 :], lines[:, :2]), "narrow", 0)
    nothing = jnp.zeros_like(other)
    return jnp.where(first, nothing, other), jnp.where(first, other, nothing)


def exchange_lines(strip, with_it):
    groups, count, cores = (lax.axis_size(axis) for axis in ("group", "wide", "narrow"))
    place = lax.axis_index("wide")
    got = []
    for start in range(2):
        pairs = []
        for g in range(groups):
            for w in range(count):
                other = w + 1 if w % 2 == start else w - 1
                far = g
                if not 0 <= other < count:
                    other, far = w, g ^ 1 if groups % 2 == 0 else g
                for c in range(cores):
                    pairs.append(((g * count + w) * cores + c, (far * count + other) * cores + c))
        upper = place % 2 == start
        out = jnp.where(upper, strip[2:], strip[:2])
        got.append(lax.ppermute(out, ("group", "wide", "narrow"), pairs))
    got, with_it = lax.optimization_barrier((got, with_it))
    above = jnp.where(place % 2 == 1, got[0], got[1])
    below = jnp.where(place % 2 == 1, got[1], got[0])
    above = jnp.where(place > 0, above, jnp.zeros_like(above))
    below = jnp.where(place < count - 1, below, jnp.zeros_like(below))
    return above, below, with_it


def earlier_state(totals, first_work, works):
    cores, shape = len(totals), totals[0].shape
    works, done = list(works), []

    def beside(work, arrays, exchange):
        held, arrays = work(arrays)
        done.append(held)
        held, arrived = lax.optimization_barrier((held, exchange(arrays)))
        done[-1] = held
        return arrived

    others = beside(
        first_work,
        totals[1:],
        lambda arrays: [rotate(array, "narrow", k + 1) for k, array in enumerate(arrays)],
    )
    pieces = [totals[0]] + others
    running, packed = small_call(gather_kernel, "gather", pieces, [F32, BF16], shape)
    before = jnp.zeros(shape, F32)
    count = lax.axis_size("wide").bit_length() - 1
    levels = [list(range(bit, min(bit + 2, count))) for bit in range(0, count, 2)]
    for level, bits in enumerate(levels):
        exchange = lambda packed: [
            swap_digit(packed, "wide", bits[0], k) for k in range(1, 1 << len(bits))
        ]
        others = beside(works.pop(0), packed, exchange) if works else exchange(packed)
        if level == len(levels) - 1:
            break
        before, packed, *more = small_call(
            functools.partial(scan_kernel, bits, len(others)),
            "scan",
            [running, before] + others,
            [F32, BF16] + [F32] * (level < len(levels) - 2),
            shape,
        )
        running = more[0] if more else None
    outs = small_call(
        functools.partial(spread_kernel, cores, bits, len(others)),
        "spread",
        [before] + others + pieces,
        [BF16] * cores,
        shape,
    )
    states = [outs[0]] + [rotate(outs[k], "narrow", k) for k in range(1, cores)]
    while works:
        done.append(works.pop(0)(outs[0])[0])
    return states, done


def split_order(order):
    half = 1 << (len(order) - 1)
    place = lambda slot: sum(
        ((slot >> (len(order) - 1 - i)) & 1) << bit for i, bit in enumerate(order)
    )
    return [place(slot) for slot in range(half)], [place(slot) for slot in range(half, 2 * half)]


def reduce_level(stays, goes, bit, with_it=None):
    arrived = [swap(array, "wide", bit) for array in reversed(goes)][::-1]
    if with_it is not None:
        arrived, with_it = lax.optimization_barrier((arrived, with_it))
    sums = [
        (here.astype(F32) + more.astype(F32)).astype(BF16) for here, more in zip(stays, arrived)
    ]
    return sums, with_it


def next_level(sums):
    if len(sums) == 1:
        half = sums[0].shape[0] // 2
        return [sums[0][:half]], [sums[0][half:]]
    return sums[:1], sums[1:]


def reduce_both(outer, middle, orders):
    levels = len(orders[0])
    outer_sums, _ = reduce_level(*outer, orders[0][0])
    stays, (later, first) = middle
    later, outer_sums[-1] = lax.optimization_barrier((later, outer_sums[-1]))
    middle = stays, [later, first]
    outer = next_level(outer_sums)
    for level in range(1, levels):
        middle_sums, _ = reduce_level(*middle, orders[1][level - 1])
        middle = next_level(middle_sums)
        if level > 1:
            outer_sums, middle = reduce_level(*outer, orders[0][level], middle)
        else:
            outer_sums, _ = reduce_level(*outer, orders[0][level])
        outer = next_level(outer_sums)
    return outer_sums[0][0], reduce_level(*middle, orders[1][-1])[0][0][0]


def per_device(voxels, w_qkv, w_out, w_feature, conv_first, conv_second, row_brick, cell_place):
    tokens = voxels.shape[0]
    channels = w_feature.shape[1]
    wide_count, wide_place = lax.axis_size("wide"), lax.axis_index("wide")
    narrow_count, narrow_place = lax.axis_size("narrow"), lax.axis_index("narrow")

    blocks = tokens // BLK
    cuts = sorted({blocks * i // 2 for i in range(3)})
    spans = [(first, last - first) for first, last in zip(cuts, cuts[1:])]
    xs, ws, totals = device_totals(spans, voxels, w_qkv, narrow_count)

    def direct(arrays):
        arrays, x = lax.optimization_barrier((arrays, xs[0]))
        return direct_features([x] + xs[1:], w_out, w_feature), arrays

    after = [None]

    def work(n):
        def run(array):
            array, x = lax.optimization_barrier((array, xs[n]))
            piece = local_attention(x, ws, after[-1], n == len(spans) - 1)
            after.append(piece[-1])
            return piece, array

        return run

    states, done = earlier_state(totals, direct, [work(n) for n in range(len(spans))])
    own, weights = done[0][:-1], done[0][-1]
    qs, parts = ([piece[i] for piece in done[1:]] for i in range(2))
    own = own_share(narrow_count, states[0], weights, qs, parts, own)

    bits = list(range(wide_count.bit_length() - 1))
    orders = [bits, bits[1::-1] + bits[2:]]
    halves = lambda places: (places[: len(places) // 2], places[len(places) // 2 :])
    stay, go = zip(*(map(halves, split_order(order)) for order in orders))
    cell_rows = cell_place.reshape(-1, 1, ROW)
    most = max(2, 2 * (tokens // ROW) // wide_count)
    bricks = row_brick[:, 0]
    features, outer_first = voxel_features(
        spans, bricks, qs, parts, own, states[1:], weights, cell_rows, go[0][1], wide_count, most
    )
    pooled = lambda *chosen: pool(bricks, cell_rows, features, chosen, wide_count, most)
    middle_first, outer_later, middle_later, *sums = pooled(
        (go[1][1], True),
        (go[0][0], False),
        (go[1][0], True),
        *((stay[middle][n], middle == 1) for middle in range(2) for n in range(2)),
    )
    outer, middle = reduce_both(
        (sums[:2], [outer_later, outer_first]), (sums[2:], [middle_later, middle_first]), orders
    )
    outer, middle = (part.reshape(-1, BY, channels) for part in (outer, middle))
    above, below, middle = exchange_lines(outer, middle)
    lines = jnp.concatenate([above, outer[:2], middle, outer[2:], below], axis=0)
    left, right = side_columns(lines)
    return field_flow(own_columns(lines, conv_first), left, right, conv_first, conv_second)


def solution(mesh):
    placed = (
        P(("group", "wide", "narrow"), None),
        P(),
        P(),
        P(),
        P(),
        P(),
        P(("group", "wide", "narrow"), None),
        P(("group", "wide", "narrow")),
    )
    return jax.shard_map(
        per_device,
        mesh=mesh,
        in_specs=placed,
        out_specs=P(("group", "wide"), "narrow", None),
        check_vma=False,
    )
```

```python
import functools

import jax
import jax.numpy as jnp
from jax import lax
from jax.experimental import pallas as pl
from jax.experimental.pallas import tpu as pltpu
from jax.sharding import PartitionSpec as P

HEADS = 4
HEAD = 128
ROW = 128
BLK = 256
BX = 8
BY = 32
EPS = 1e-06
GAP = 16
LINE = GAP + BY

F32 = jnp.float32
BF16 = jnp.bfloat16


def dot(a, b):
    return jnp.dot(a, b, preferred_element_type=F32)


def dot_t(a, b):
    return lax.dot_general(a, b, (((0,), (0,)), ((), ())), preferred_element_type=F32)


def dot_nt(a, b):
    return lax.dot_general(a, b, (((1,), (1,)), ((), ())), preferred_element_type=F32)


TOTALS_KIB = 50688


def params(kib=24 * 1024):
    return pltpu.CompilerParams(vmem_limit_bytes=kib << 10)


def head_cols(h):
    return slice(h * HEAD, (h + 1) * HEAD)


def in_two(array):
    high = array.astype(BF16)
    return high, (array - high.astype(F32)).astype(BF16)


def totals_kernel(spans, x_ref, w_ref, *refs):
    refs = list(refs)
    take = lambda n: [refs.pop(0) for _ in range(n)]
    xs, ws = take(len(spans)), take(3)
    totals, sems = refs[:-1], refs[-1]
    inner = HEADS * HEAD
    loads = [
        pltpu.make_async_copy(x_ref.at[pl.ds(first * BLK, count * BLK)], x, sems.at[n])
        for n, ((first, count), x) in enumerate(zip(spans, xs))
    ]
    w_loads = [
        pltpu.make_async_copy(
            w_ref.at[:, pl.ds(part * inner, inner)], w, sems.at[len(spans) + part]
        )
        for part, w in enumerate(ws)
    ]
    for load in loads + w_loads[::-1]:
        load.start()
    gram = 0.0
    for x, load in zip(xs, loads):
        load.wait()
        gram = gram + dot_t(x[...], x[...])
    w_loads[2].wait()
    weighed = sum(dot(part, ws[2][...]) for part in in_two(gram)).astype(BF16)
    w_loads[1].wait()
    cores, share = len(totals), HEADS // len(totals)
    for n in range(cores):
        cols = slice(n * share * HEAD, (n + 1) * share * HEAD)
        outer = dot_t(ws[1][:, cols], weighed[:, cols])
        for k, total_ref in enumerate(totals):

            @pl.when((lax.axis_index("narrow") + k) % cores == n)
            def _(total_ref=total_ref, outer=outer):
                for j in range(share):
                    total_ref[j] = outer[head_cols(j), head_cols(j)].astype(BF16)

    w_loads[0].wait()


def device_totals(spans, voxels, w_qkv, cores):
    width = voxels.shape[1]
    inner = HEADS * HEAD
    hbm = pl.BlockSpec(memory_space=pl.ANY)
    vmem = pl.BlockSpec(memory_space=pltpu.VMEM)
    out_shape = [jax.ShapeDtypeStruct((count * BLK, width), BF16) for _, count in spans]
    out_shape += [jax.ShapeDtypeStruct((width, inner), BF16)] * 3
    out_shape += [jax.ShapeDtypeStruct((HEADS // cores, HEAD, HEAD), BF16)] * cores
    outs = list(
        pl.pallas_call(
            functools.partial(totals_kernel, spans),
            in_specs=[hbm, hbm],
            out_specs=[vmem] * len(out_shape),
            out_shape=out_shape,
            scratch_shapes=[pltpu.SemaphoreType.DMA((len(spans) + 3,))],
            compiler_params=params(TOTALS_KIB),
            name="device_totals",
        )(voxels, w_qkv)
    )
    n = len(spans)
    return outs[:n], outs[n : n + 3], outs[n + 3 :]


PAIR = 2 * HEAD


def local_kernel(count, starts, ends, x_ref, wq_ref, wk_ref, wv_ref, *refs):
    refs = list(refs)
    before_ref = None if starts else refs.pop(0)
    q_ref, part_ref = refs[:2]
    k, v = refs[-2:]
    causal = lax.broadcasted_iota(jnp.int32, (BLK, BLK), 0) >= lax.broadcasted_iota(
        jnp.int32, (BLK, BLK), 1
    )
    same_head = ones_blocks(PAIR) > 0
    q = dot(x_ref[...], wq_ref[...]).astype(BF16)
    q_ref[...] = q
    k[...] = dot(x_ref[...], wk_ref[...]).astype(BF16)
    v[...] = dot(x_ref[...], wv_ref[...]).astype(BF16)
    pairs = [slice(pair * PAIR, (pair + 1) * PAIR) for pair in range(HEADS // 2)]
    states = None if starts else [before_ref[pair] for pair in range(HEADS // 2)]
    for b in range(count):
        rows = slice(b * BLK, (b + 1) * BLK)
        scores = [dot_nt(q[rows, head_cols(h)], k[rows, head_cols(h)]) for h in range(HEADS)]
        if states is not None:
            carried = [
                dot(q[rows, both], jnp.where(same_head, state, 0.0).astype(BF16))
                for both, state in zip(pairs, states)
            ]
        scores = [jnp.where(causal, score, 0.0).astype(BF16) for score in scores]
        attended = [dot(score, v[rows, head_cols(h)]) for h, score in enumerate(scores)]
        for h in range(HEADS):
            if states is not None:
                attended[h] += carried[h // 2][:, head_cols(h % 2)]
            part_ref[rows, head_cols(h)] = attended[h].astype(BF16)
        if not (ends and b == count - 1):
            outer = [dot_t(k[rows, both], v[rows, both]) for both in pairs]
            states = outer if states is None else [x + y for x, y in zip(states, outer)]
    if not ends:
        for pair, state in enumerate(states):
            refs[2][pair] = state


def local_attention(x, ws, before, ends):
    rows, width = x.shape
    inner = HEADS * HEAD
    vmem = pl.BlockSpec(memory_space=pltpu.VMEM)
    inputs = [x, *ws] + ([] if before is None else [before])
    out_shape = [jax.ShapeDtypeStruct((rows, inner), BF16)] * 2
    if not ends:
        out_shape.append(jax.ShapeDtypeStruct((HEADS // 2, PAIR, PAIR), F32))
    return pl.pallas_call(
        functools.partial(local_kernel, rows // BLK, before is None, ends),
        in_specs=[vmem] * len(inputs),
        out_specs=[vmem] * len(out_shape),
        out_shape=out_shape,
        scratch_shapes=[pltpu.VMEM((rows, inner), BF16)] * 2,
        compiler_params=params(),
        cost_estimate=pl.CostEstimate(
            flops=2 * rows * inner * (3 * width + 2 * BLK + 2 * HEAD),
            bytes_accessed=rows * inner * 10,
            transcendentals=0,
        ),
        name="local_attention",
    )(*inputs)


def direct_kernel(*refs):
    count = len(refs) // 2 - 1
    xs, (wo_ref, wf_ref), outs = refs[:count], refs[count : count + 2], refs[count + 2 :]
    for x, out in zip(xs, outs):
        out[...] = dot(x[...], wf_ref[...])
    outs[-1][...] = dot(wo_ref[...], wf_ref[...]).astype(BF16)


def direct_features(xs, w_out, w_feature):
    channels = w_feature.shape[1]
    vmem = pl.BlockSpec(memory_space=pltpu.VMEM)
    rows = sum(x.shape[0] for x in xs)
    return pl.pallas_call(
        direct_kernel,
        in_specs=[vmem] * (len(xs) + 2),
        out_specs=[vmem] * (len(xs) + 1),
        out_shape=[jax.ShapeDtypeStruct((x.shape[0], channels), F32) for x in xs]
        + [jax.ShapeDtypeStruct(w_feature.shape, BF16)],
        compiler_params=params(),
        cost_estimate=pl.CostEstimate(
            flops=2 * (rows + w_out.shape[0]) * w_out.shape[1] * channels,
            bytes_accessed=rows * channels * 8,
            transcendentals=0,
        ),
        name="direct_features",
    )(*xs, w_out, w_feature)


def gather_kernel(*refs):
    ins, (running_ref, packed_ref) = refs[:-2], refs[-2:]
    running = sum(ref[...].astype(F32) for ref in ins)
    running_ref[...] = running
    packed_ref[...] = running.astype(BF16)


def earlier_sum(bits, others):
    digit = (lax.axis_index("wide") >> bits[0]) & ((1 << len(bits)) - 1)
    return sum(
        ((digit ^ (k + 1)) < digit).astype(F32) * other for k, other in enumerate(others)
    )


def scan_kernel(bits, count, running_ref, before_ref, *refs):
    others = [ref[...].astype(F32) for ref in refs[:count]]
    new_before, packed, *new_running = refs[count:]
    running = running_ref[...] + sum(others)
    packed[...] = running.astype(BF16)
    for ref in new_running:
        ref[...] = running
    new_before[...] = before_ref[...] + earlier_sum(bits, others)


def spread_kernel(cores, bits, count, before_ref, *refs):
    others = [ref[...].astype(F32) for ref in refs[:count]]
    pieces, outs = refs[count : count + cores], refs[count + cores :]
    place = lax.axis_index("narrow")
    before = before_ref[...] + earlier_sum(bits, others)
    for k, out in enumerate(outs):
        receiver = (place + k) % cores
        value = before
        for j, piece in enumerate(pieces):
            source = (place - j + cores) % cores
            value = value + jnp.where(source < receiver, 1.0, 0.0) * piece[...].astype(F32)
        out[...] = value.astype(BF16)


def small_call(kernel, name, inputs, dtypes, shape):
    vmem = pl.BlockSpec(memory_space=pltpu.VMEM)
    smem = pl.BlockSpec(memory_space=pltpu.SMEM)
    return pl.pallas_call(
        kernel,
        in_specs=[smem if array.dtype == jnp.int32 else vmem for array in inputs],
        out_specs=[vmem] * len(dtypes),
        out_shape=[jax.ShapeDtypeStruct(shape, dtype) for dtype in dtypes],
        compiler_params=params(4 * 1024),
        name=name,
    )(*inputs)


def ones_blocks(width):
    rows, cols = (lax.broadcasted_iota(jnp.int32, (width, width), axis) for axis in range(2))
    return jnp.where(rows // HEAD == cols // HEAD, 1.0, 0.0).astype(BF16)


def block_state(state_ref, scratch):
    scratch[...] = jnp.zeros_like(scratch)
    for j in range(state_ref.shape[0]):
        scratch[head_cols(j), head_cols(j)] = state_ref[j]
    return scratch[...]


def norm_share(q, part, state, ones):
    attended = part.astype(F32) + dot(q, state)
    squares = dot((attended * attended).astype(BF16), ones)
    return (attended * lax.rsqrt(squares * (1 / HEAD) + EPS)).astype(BF16)


def share_columns(cores, before):
    width = HEADS // cores * HEAD
    owner = (lax.axis_index("narrow") - before + cores) % cores
    return pl.ds(pl.multiple_of(owner * width, width), width)


def own_share_kernel(cores, state_ref, w_ref, *refs):
    pieces = len(refs) // 4
    qs, parts, direct, outs = (refs[i * pieces : (i + 1) * pieces] for i in range(4))
    scratch = refs[-1]
    cols = share_columns(cores, 0)
    state, ones = block_state(state_ref, scratch), ones_blocks(scratch.shape[0])
    for q, part, start, out in zip(qs, parts, direct, outs):
        normed = norm_share(q[:, cols], part[:, cols], state, ones)
        out[...] = start[...] + dot(normed, w_ref[cols, :])


def own_share(cores, state, weights, qs, parts, direct):
    width = HEADS // cores * HEAD
    vmem = pl.BlockSpec(memory_space=pltpu.VMEM)
    rows = sum(q.shape[0] for q in qs)
    return pl.pallas_call(
        functools.partial(own_share_kernel, cores),
        in_specs=[vmem] * (2 + 3 * len(qs)),
        out_specs=[vmem] * len(qs),
        out_shape=[jax.ShapeDtypeStruct(start.shape, F32) for start in direct],
        scratch_shapes=[pltpu.VMEM((width, width), BF16)],
        compiler_params=params(),
        cost_estimate=pl.CostEstimate(
            flops=6 * rows * width * width, bytes_accessed=rows * width * 8, transcendentals=0
        ),
        name="own_share",
    )(state, weights, *qs, *parts, *direct)


def list_rows(brick_ref, most, slots, fill):
    for i in range(slots.shape[0]):
        slots[i] = -1
    for b in range(fill.shape[0]):
        fill[b] = 0
    for r in range(brick_ref.shape[0]):
        brick = brick_ref[r] ^ lax.axis_index("wide")
        used = fill[brick]
        slots[brick * most + used] = r
        fill[brick] = used + 1


def cell_numbers(middle):
    number = lax.broadcasted_iota(jnp.int32, (BX * BY // 2, 1), 0)
    if middle:
        return number + 2 * BY
    return number + jnp.where(number < 2 * BY, 0, BX * BY // 2)


def cell_sums(brick, numbers, most, slots, cell_ref, features_ref):
    onehots, rows = [], []
    for j in range(most):
        row = slots[brick * most + j]
        at = jnp.maximum(row, 0)
        match = (numbers == cell_ref[at]) & (row >= 0)
        onehots.append(jnp.where(match, 1.0, 0.0).astype(BF16))
        rows.append(features_ref[pl.ds(pl.multiple_of(at * ROW, ROW), ROW), :])
    return dot(jnp.concatenate(onehots, axis=1), jnp.concatenate(rows, axis=0)).astype(BF16)


def pool_into(outs, brick_ref, cell_ref, features_ref, slots, fill):
    most = slots.shape[0] // fill.shape[0]
    list_rows(brick_ref, most, slots, fill)
    for bricks, middle, out in outs:
        numbers = cell_numbers(middle)
        for n, brick in enumerate(bricks):
            out[n] = cell_sums(brick, numbers, most, slots, cell_ref, features_ref)


def features_kernel(bricks, spans, cores, brick_ref, *refs):
    pieces = len(spans)
    refs = list(refs)
    take = lambda n: [refs.pop(0) for _ in range(n)]
    q_refs, part_refs, own_refs = (take(pieces) for _ in range(3))
    state_refs = take(cores - 1)
    w_ref, cell_ref, features_ref, out = take(4)
    scratch, slots, fill = refs
    shares = [share_columns(cores, k) for k in range(cores)]
    ones = ones_blocks(scratch.shape[1])
    states = [block_state(ref, scratch.at[k]) for k, ref in enumerate(state_refs)]
    for n, (first, count) in enumerate(spans):
        features = own_refs[n][...]
        for state, cols in zip(states, shares[1:]):
            normed = norm_share(q_refs[n][:, cols], part_refs[n][:, cols], state, ones)
            features += dot(normed, w_ref[cols, :])
        features_ref[first * BLK : (first + count) * BLK] = features.astype(BF16)
    pool_into([(bricks, False, out)], brick_ref, cell_ref, features_ref, slots, fill)


def list_scratch(count, most):
    return [pltpu.SMEM((count * most,), jnp.int32), pltpu.SMEM((count,), jnp.int32)]


def sums_shape(count, channels):
    return jax.ShapeDtypeStruct((count, BX * BY // 2, channels), BF16)


def voxel_features(
    spans, bricks, qs, parts, own, states, weights, cell_rows, chosen, count, most
):
    tokens, channels = sum(q.shape[0] for q in qs), weights.shape[1]
    cores = len(states) + 1
    width = HEADS // cores * HEAD
    vmem = pl.BlockSpec(memory_space=pltpu.VMEM)
    smem = pl.BlockSpec(memory_space=pltpu.SMEM)
    return pl.pallas_call(
        functools.partial(features_kernel, chosen, spans, cores),
        in_specs=[smem] + [vmem] * (3 * len(spans) + cores + 1),
        out_specs=[vmem] * 2,
        out_shape=[
            jax.ShapeDtypeStruct((tokens, channels), BF16),
            sums_shape(len(chosen), channels),
        ],
        scratch_shapes=[pltpu.VMEM((max(1, cores - 1), width, width), BF16)]
        + list_scratch(count, most),
        compiler_params=params(),
        name="voxel_features",
    )(bricks, *qs, *parts, *own, *states, weights, cell_rows)


def pool_kernel(chosen, brick_ref, cell_ref, features_ref, *refs):
    outs, (slots, fill) = refs[:-2], refs[-2:]
    pool_into(
        [(bricks, middle, out) for (bricks, middle), out in zip(chosen, outs)],
        brick_ref,
        cell_ref,
        features_ref,
        slots,
        fill,
    )


def pool(bricks, cell_rows, features, chosen, count, most):
    tokens, channels = features.shape
    vmem = pl.BlockSpec(memory_space=pltpu.VMEM)
    smem = pl.BlockSpec(memory_space=pltpu.SMEM)
    return pl.pallas_call(
        functools.partial(pool_kernel, chosen),
        in_specs=[smem, vmem, vmem],
        out_specs=[vmem] * len(chosen),
        out_shape=[sums_shape(len(which), channels) for which, _ in chosen],
        scratch_shapes=list_scratch(count, most),
        compiler_params=params(),
        cost_estimate=pl.CostEstimate(
            flops=sum(len(which) for which, _ in chosen) * most * ROW * BX * BY * channels,
            bytes_accessed=tokens * channels * 2,
            transcendentals=0,
        ),
        name="pool",
    )(bricks, cell_rows, features)


def convolve(field, w_ref, start, count):
    lhs = jnp.concatenate(
        [field[start + dy * LINE : start + dy * LINE + count] for dy in (-1, 0, 1)], axis=1
    )
    left, middle, right = weighted(lhs, w_ref)
    return pltpu.roll(left, 1, 0) + middle + pltpu.roll(right, count - 1, 0)


def weighted(lhs, w_ref):
    return [
        dot(lhs, jnp.concatenate([w_ref[dy, dx] for dy in range(3)], axis=0)) for dx in range(3)
    ]


def own_columns_kernel(lines_ref, w_ref, out_ref, field):
    lines = lines_ref.shape[0]
    for r in range(lines):
        field[r * LINE : r * LINE + GAP] = jnp.zeros((GAP, field.shape[1]), BF16)
        field[r * LINE + GAP : (r + 1) * LINE] = lines_ref[r]
    field[lines * LINE :] = jnp.zeros((GAP, field.shape[1]), BF16)
    out_ref[...] = convolve(field, w_ref, LINE, out_ref.shape[0])


def own_columns(lines, conv_first):
    count, _, channels = lines.shape
    vmem = pl.BlockSpec(memory_space=pltpu.VMEM)
    shown = (count - 2) * LINE + GAP
    return pl.pallas_call(
        own_columns_kernel,
        in_specs=[vmem] * 2,
        out_specs=vmem,
        out_shape=jax.ShapeDtypeStruct((shown, channels), F32),
        scratch_shapes=[pltpu.VMEM((count * LINE + GAP, channels), BF16)],
        compiler_params=params(16 * 1024),
        cost_estimate=pl.CostEstimate(
            flops=18 * shown * channels * channels,
            bytes_accessed=shown * channels * 8,
            transcendentals=0,
        ),
        name="own_columns",
    )(lines, conv_first)


def field_kernel(first_ref, sides_ref, w1_ref, w2_ref, out_ref, first, field):
    count, channels = first.shape
    wide, narrow = lax.axis_index("wide"), lax.axis_index("narrow")
    first_line, last_line = wide == 0, wide == lax.axis_size("wide") - 1
    first_column, last_column = narrow == 0, narrow == lax.axis_size("narrow") - 1
    gaps = sides_ref.shape[0] - 2
    sides = sides_ref[...].reshape((gaps + 2) * GAP, channels)
    lhs = jnp.concatenate([sides[dy * GAP : (dy + gaps) * GAP] for dy in range(3)], axis=1)
    none = jnp.zeros((8, channels), F32)
    left, middle, right = [
        jnp.concatenate(
            [part for g in range(gaps) for part in (none, given[g * GAP : (g + 1) * GAP], none)],
            axis=0,
        )
        for given in weighted(lhs, w1_ref)
    ]
    span = GAP + 16
    added = pltpu.roll(left, 1, 0) + middle + pltpu.roll(right, gaps * span - 1, 0)
    first[...] = first_ref[...]
    for g in range(gaps):
        start, stop = max(g * LINE - 8, 0), min(g * LINE + GAP + 8, count)
        at = g * span + 8 - g * LINE
        first[start:stop] += added[start + at : stop + at]
    inner = jax.nn.gelu(first[...], approximate=True)
    at = lax.broadcasted_iota(jnp.int32, (count, 1), 0)
    outside = first_line & (at <= LINE) | last_line & (at > (BX + 1) * LINE)
    for r in range(BX + 2):
        outside |= first_column & (at == r * LINE + GAP - 1)
        outside |= last_column & (at == (r + 1) * LINE)
    field[...] = jnp.where(outside, 0.0, inner).astype(BF16)
    flow = convolve(field, w2_ref, LINE, BX * LINE + GAP)
    for r in range(BX):
        out_ref[r] = flow[r * LINE + GAP : (r + 1) * LINE]


def field_flow(first, left, right, conv_first, conv_second):
    count, channels = first.shape
    vmem = pl.BlockSpec(memory_space=pltpu.VMEM)
    sides = jnp.pad(right, ((1, 0), (0, GAP - 2), (0, 0))) + jnp.pad(
        left, ((0, 1), (GAP - 2, 0), (0, 0))
    )
    return pl.pallas_call(
        field_kernel,
        in_specs=[vmem] * 4,
        out_specs=vmem,
        out_shape=jax.ShapeDtypeStruct((BX, BY, channels), F32),
        scratch_shapes=[pltpu.VMEM((count, channels), F32), pltpu.VMEM((count, channels), BF16)],
        compiler_params=params(16 * 1024),
        name="field_flow",
    )(first, sides, conv_first, conv_second)


def swap(array, axis, bit):
    count = lax.axis_size(axis)
    return lax.ppermute(array, axis, [(i, i ^ (1 << bit)) for i in range(count)])


def swap_digit(array, axis, bit, by):
    count = lax.axis_size(axis)
    return lax.ppermute(array, axis, [(i, i ^ (by << bit)) for i in range(count)])


def shift(array, axis, by):
    count = lax.axis_size(axis)
    return lax.ppermute(
        array, axis, [(i, i + by) for i in range(count) if 0 <= i + by < count]
    )


def rotate(array, axis, by):
    count = lax.axis_size(axis)
    return lax.ppermute(array, axis, [(i, (i + by) % count) for i in range(count)])


def side_columns(lines):
    if lax.axis_size("narrow") != 2:
        return shift(lines[:, BY - 2 :], "narrow", 1), shift(lines[:, :2], "narrow", -1)
    first = lax.axis_index("narrow") == 0
    other = swap(jnp.where(first, lines[:, BY - 2 :], lines[:, :2]), "narrow", 0)
    nothing = jnp.zeros_like(other)
    return jnp.where(first, nothing, other), jnp.where(first, other, nothing)


def exchange_lines(strip, with_it):
    groups, count, cores = (lax.axis_size(axis) for axis in ("group", "wide", "narrow"))
    place = lax.axis_index("wide")
    got = []
    for start in range(2):
        pairs = []
        for g in range(groups):
            for w in range(count):
                other = w + 1 if w % 2 == start else w - 1
                far = g
                if not 0 <= other < count:
                    other, far = w, g ^ 1 if groups % 2 == 0 else g
                for c in range(cores):
                    pairs.append(((g * count + w) * cores + c, (far * count + other) * cores + c))
        upper = place % 2 == start
        out = jnp.where(upper, strip[2:], strip[:2])
        got.append(lax.ppermute(out, ("group", "wide", "narrow"), pairs))
    got, with_it = lax.optimization_barrier((got, with_it))
    above = jnp.where(place % 2 == 1, got[0], got[1])
    below = jnp.where(place % 2 == 1, got[1], got[0])
    above = jnp.where(place > 0, above, jnp.zeros_like(above))
    below = jnp.where(place < count - 1, below, jnp.zeros_like(below))
    return above, below, with_it


def earlier_state(totals, first_work, works):
    cores, shape = len(totals), totals[0].shape
    works, done = list(works), []

    def beside(work, arrays, exchange):
        held, arrays = work(arrays)
        done.append(held)
        held, arrived = lax.optimization_barrier((held, exchange(arrays)))
        done[-1] = held
        return arrived

    others = beside(
        first_work,
        totals[1:],
        lambda arrays: [rotate(array, "narrow", k + 1) for k, array in enumerate(arrays)],
    )
    pieces = [totals[0]] + others
    running, packed = small_call(gather_kernel, "gather", pieces, [F32, BF16], shape)
    before = jnp.zeros(shape, F32)
    count = lax.axis_size("wide").bit_length() - 1
    levels = [list(range(bit, min(bit + 2, count))) for bit in range(0, count, 2)]
    for level, bits in enumerate(levels):
        exchange = lambda packed: [
            swap_digit(packed, "wide", bits[0], k) for k in range(1, 1 << len(bits))
        ]
        others = beside(works.pop(0), packed, exchange) if works else exchange(packed)
        if level == len(levels) - 1:
            break
        before, packed, *more = small_call(
            functools.partial(scan_kernel, bits, len(others)),
            "scan",
            [running, before] + others,
            [F32, BF16] + [F32] * (level < len(levels) - 2),
            shape,
        )
        running = more[0] if more else None
    outs = small_call(
        functools.partial(spread_kernel, cores, bits, len(others)),
        "spread",
        [before] + others + pieces,
        [BF16] * cores,
        shape,
    )
    states = [outs[0]] + [rotate(outs[k], "narrow", k) for k in range(1, cores)]
    while works:
        done.append(works.pop(0)(outs[0])[0])
    return states, done


def split_order(order):
    half = 1 << (len(order) - 1)
    place = lambda slot: sum(
        ((slot >> (len(order) - 1 - i)) & 1) << bit for i, bit in enumerate(order)
    )
    return [place(slot) for slot in range(half)], [place(slot) for slot in range(half, 2 * half)]


def reduce_level(stays, goes, bit, with_it=None):
    arrived = [swap(array, "wide", bit) for array in reversed(goes)][::-1]
    if with_it is not None:
        arrived, with_it = lax.optimization_barrier((arrived, with_it))
    sums = [
        (here.astype(F32) + more.astype(F32)).astype(BF16) for here, more in zip(stays, arrived)
    ]
    return sums, with_it


def next_level(sums):
    if len(sums) == 1:
        half = sums[0].shape[0] // 2
        return [sums[0][:half]], [sums[0][half:]]
    return sums[:1], sums[1:]


def reduce_both(outer, middle, orders):
    levels = len(orders[0])
    outer_sums, _ = reduce_level(*outer, orders[0][0])
    stays, (later, first) = middle
    later, outer_sums[-1] = lax.optimization_barrier((later, outer_sums[-1]))
    middle = stays, [later, first]
    outer = next_level(outer_sums)
    for level in range(1, levels):
        middle_sums, _ = reduce_level(*middle, orders[1][level - 1])
        middle = next_level(middle_sums)
        if level > 1:
            outer_sums, middle = reduce_level(*outer, orders[0][level], middle)
        else:
            outer_sums, _ = reduce_level(*outer, orders[0][level])
        outer = next_level(outer_sums)
    return outer_sums[0][0], reduce_level(*middle, orders[1][-1])[0][0][0]


def per_device(voxels, w_qkv, w_out, w_feature, conv_first, conv_second, row_brick, cell_place):
    tokens = voxels.shape[0]
    channels = w_feature.shape[1]
    wide_count, wide_place = lax.axis_size("wide"), lax.axis_index("wide")
    narrow_count, narrow_place = lax.axis_size("narrow"), lax.axis_index("narrow")

    blocks = tokens // BLK
    cuts = sorted({blocks * i // 2 for i in range(3)})
    spans = [(first, last - first) for first, last in zip(cuts, cuts[1:])]
    xs, ws, totals = device_totals(spans, voxels, w_qkv, narrow_count)

    def direct(arrays):
        arrays, x = lax.optimization_barrier((arrays, xs[0]))
        return direct_features([x] + xs[1:], w_out, w_feature), arrays

    after = [None]

    def work(n):
        def run(array):
            array, x = lax.optimization_barrier((array, xs[n]))
            piece = local_attention(x, ws, after[-1], n == len(spans) - 1)
            after.append(piece[-1])
            return piece, array

        return run

    states, done = earlier_state(totals, direct, [work(n) for n in range(len(spans))])
    own, weights = done[0][:-1], done[0][-1]
    qs, parts = ([piece[i] for piece in done[1:]] for i in range(2))
    own = own_share(narrow_count, states[0], weights, qs, parts, own)

    bits = list(range(wide_count.bit_length() - 1))
    orders = [bits, bits[1::-1] + bits[2:]]
    halves = lambda places: (places[: len(places) // 2], places[len(places) // 2 :])
    stay, go = zip(*(map(halves, split_order(order)) for order in orders))
    cell_rows = cell_place.reshape(-1, 1, ROW)
    most = max(2, 2 * (tokens // ROW) // wide_count)
    bricks = row_brick[:, 0]
    features, outer_first = voxel_features(
        spans, bricks, qs, parts, own, states[1:], weights, cell_rows, go[0][1], wide_count, most
    )
    pooled = lambda *chosen: pool(bricks, cell_rows, features, chosen, wide_count, most)
    middle_first, outer_later, middle_later, *sums = pooled(
        (go[1][1], True),
        (go[0][0], False),
        (go[1][0], True),
        *((stay[middle][n], middle == 1) for middle in range(2) for n in range(2)),
    )
    outer, middle = reduce_both(
        (sums[:2], [outer_later, outer_first]), (sums[2:], [middle_later, middle_first]), orders
    )
    outer, middle = (part.reshape(-1, BY, channels) for part in (outer, middle))
    above, below, middle = exchange_lines(outer, middle)
    lines = jnp.concatenate([above, outer[:2], middle, outer[2:], below], axis=0)
    left, right = side_columns(lines)
    return field_flow(own_columns(lines, conv_first), left, right, conv_first, conv_second)


def solution(mesh):
    placed = (
        P(("group", "wide", "narrow"), None),
        P(),
        P(),
        P(),
        P(),
        P(),
        P(("group", "wide", "narrow"), None),
        P(("group", "wide", "narrow")),
    )
    return jax.shard_map(
        per_device,
        mesh=mesh,
        in_specs=placed,
        out_specs=P(("group", "wide"), "narrow", None),
        check_vma=False,
    )
```

```python
import functools

import jax
import jax.numpy as jnp
from jax import lax
from jax.experimental import pallas as pl
from jax.experimental.pallas import tpu as pltpu
from jax.sharding import PartitionSpec as P

HEADS = 4
HEAD = 128
ROW = 128
BLK = 256
BX = 8
BY = 32
EPS = 1e-06
GAP = 16
LINE = GAP + BY

F32 = jnp.float32
BF16 = jnp.bfloat16


def dot(a, b):
    return jnp.dot(a, b, preferred_element_type=F32)


def dot_t(a, b):
    return lax.dot_general(a, b, (((0,), (0,)), ((), ())), preferred_element_type=F32)


def dot_nt(a, b):
    return lax.dot_general(a, b, (((1,), (1,)), ((), ())), preferred_element_type=F32)


TOTALS_KIB = 50688


def params(kib=24 * 1024):
    return pltpu.CompilerParams(vmem_limit_bytes=kib << 10)


def head_cols(h):
    return slice(h * HEAD, (h + 1) * HEAD)


def in_two(array):
    high = array.astype(BF16)
    return high, (array - high.astype(F32)).astype(BF16)


def totals_kernel(spans, x_ref, w_ref, *refs):
    refs = list(refs)
    take = lambda n: [refs.pop(0) for _ in range(n)]
    xs, ws = take(len(spans)), take(3)
    totals, sems = refs[:-1], refs[-1]
    inner = HEADS * HEAD
    loads = [
        pltpu.make_async_copy(x_ref.at[pl.ds(first * BLK, count * BLK)], x, sems.at[n])
        for n, ((first, count), x) in enumerate(zip(spans, xs))
    ]
    w_loads = [
        pltpu.make_async_copy(
            w_ref.at[:, pl.ds(part * inner, inner)], w, sems.at[len(spans) + part]
        )
        for part, w in enumerate(ws)
    ]
    for load in loads + w_loads[::-1]:
        load.start()
    gram = 0.0
    for x, load in zip(xs, loads):
        load.wait()
        gram = gram + dot_t(x[...], x[...])
    w_loads[2].wait()
    weighed = sum(dot(part, ws[2][...]) for part in in_two(gram)).astype(BF16)
    w_loads[1].wait()
    cores, share = len(totals), HEADS // len(totals)
    for n in range(cores):
        cols = slice(n * share * HEAD, (n + 1) * share * HEAD)
        outer = dot_t(ws[1][:, cols], weighed[:, cols])
        for k, total_ref in enumerate(totals):

            @pl.when((lax.axis_index("narrow") + k) % cores == n)
            def _(total_ref=total_ref, outer=outer):
                for j in range(share):
                    total_ref[j] = outer[head_cols(j), head_cols(j)].astype(BF16)

    w_loads[0].wait()


def device_totals(spans, voxels, w_qkv, cores):
    width = voxels.shape[1]
    inner = HEADS * HEAD
    hbm = pl.BlockSpec(memory_space=pl.ANY)
    vmem = pl.BlockSpec(memory_space=pltpu.VMEM)
    out_shape = [jax.ShapeDtypeStruct((count * BLK, width), BF16) for _, count in spans]
    out_shape += [jax.ShapeDtypeStruct((width, inner), BF16)] * 3
    out_shape += [jax.ShapeDtypeStruct((HEADS // cores, HEAD, HEAD), BF16)] * cores
    outs = list(
        pl.pallas_call(
            functools.partial(totals_kernel, spans),
            in_specs=[hbm, hbm],
            out_specs=[vmem] * len(out_shape),
            out_shape=out_shape,
            scratch_shapes=[pltpu.SemaphoreType.DMA((len(spans) + 3,))],
            compiler_params=params(TOTALS_KIB),
            name="device_totals",
        )(voxels, w_qkv)
    )
    n = len(spans)
    return outs[:n], outs[n : n + 3], outs[n + 3 :]


PAIR = 2 * HEAD


def local_kernel(count, starts, ends, x_ref, wq_ref, wk_ref, wv_ref, *refs):
    refs = list(refs)
    before_ref = None if starts else refs.pop(0)
    q_ref, part_ref = refs[:2]
    k, v = refs[-2:]
    causal = lax.broadcasted_iota(jnp.int32, (BLK, BLK), 0) >= lax.broadcasted_iota(
        jnp.int32, (BLK, BLK), 1
    )
    same_head = ones_blocks(PAIR) > 0
    q = dot(x_ref[...], wq_ref[...]).astype(BF16)
    q_ref[...] = q
    k[...] = dot(x_ref[...], wk_ref[...]).astype(BF16)
    v[...] = dot(x_ref[...], wv_ref[...]).astype(BF16)
    pairs = [slice(pair * PAIR, (pair + 1) * PAIR) for pair in range(HEADS // 2)]
    states = None if starts else [before_ref[pair] for pair in range(HEADS // 2)]
    for b in range(count):
        rows = slice(b * BLK, (b + 1) * BLK)
        scores = [dot_nt(q[rows, head_cols(h)], k[rows, head_cols(h)]) for h in range(HEADS)]
        if states is not None:
            carried = [
                dot(q[rows, both], jnp.where(same_head, state, 0.0).astype(BF16))
                for both, state in zip(pairs, states)
            ]
        scores = [jnp.where(causal, score, 0.0).astype(BF16) for score in scores]
        attended = [dot(score, v[rows, head_cols(h)]) for h, score in enumerate(scores)]
        for h in range(HEADS):
            if states is not None:
                attended[h] += carried[h // 2][:, head_cols(h % 2)]
            part_ref[rows, head_cols(h)] = attended[h]
        if not (ends and b == count - 1):
            outer = [dot_t(k[rows, both], v[rows, both]) for both in pairs]
            states = outer if states is None else [x + y for x, y in zip(states, outer)]
    if not ends:
        for pair, state in enumerate(states):
            refs[2][pair] = state


def local_attention(x, ws, before, ends):
    rows, width = x.shape
    inner = HEADS * HEAD
    vmem = pl.BlockSpec(memory_space=pltpu.VMEM)
    inputs = [x, *ws] + ([] if before is None else [before])
    out_shape = [
        jax.ShapeDtypeStruct((rows, inner), BF16),
        jax.ShapeDtypeStruct((rows, inner), F32),
    ]
    if not ends:
        out_shape.append(jax.ShapeDtypeStruct((HEADS // 2, PAIR, PAIR), F32))
    return pl.pallas_call(
        functools.partial(local_kernel, rows // BLK, before is None, ends),
        in_specs=[vmem] * len(inputs),
        out_specs=[vmem] * len(out_shape),
        out_shape=out_shape,
        scratch_shapes=[pltpu.VMEM((rows, inner), BF16)] * 2,
        compiler_params=params(),
        cost_estimate=pl.CostEstimate(
            flops=2 * rows * inner * (3 * width + 2 * BLK + 2 * HEAD),
            bytes_accessed=rows * inner * 12,
            transcendentals=0,
        ),
        name="local_attention",
    )(*inputs)


def direct_kernel(*refs):
    count = len(refs) // 2 - 1
    xs, (wo_ref, wf_ref), outs = refs[:count], refs[count : count + 2], refs[count + 2 :]
    for x, out in zip(xs, outs):
        out[...] = dot(x[...], wf_ref[...])
    outs[-1][...] = dot(wo_ref[...], wf_ref[...]).astype(BF16)


def direct_features(xs, w_out, w_feature):
    channels = w_feature.shape[1]
    vmem = pl.BlockSpec(memory_space=pltpu.VMEM)
    rows = sum(x.shape[0] for x in xs)
    return pl.pallas_call(
        direct_kernel,
        in_specs=[vmem] * (len(xs) + 2),
        out_specs=[vmem] * (len(xs) + 1),
        out_shape=[jax.ShapeDtypeStruct((x.shape[0], channels), F32) for x in xs]
        + [jax.ShapeDtypeStruct(w_feature.shape, BF16)],
        compiler_params=params(),
        cost_estimate=pl.CostEstimate(
            flops=2 * (rows + w_out.shape[0]) * w_out.shape[1] * channels,
            bytes_accessed=rows * channels * 8,
            transcendentals=0,
        ),
        name="direct_features",
    )(*xs, w_out, w_feature)


def gather_kernel(*refs):
    ins, (running_ref, packed_ref) = refs[:-2], refs[-2:]
    running = sum(ref[...].astype(F32) for ref in ins)
    running_ref[...] = running
    packed_ref[...] = running.astype(BF16)


def earlier_sum(bits, others):
    digit = (lax.axis_index("wide") >> bits[0]) & ((1 << len(bits)) - 1)
    return sum(
        ((digit ^ (k + 1)) < digit).astype(F32) * other for k, other in enumerate(others)
    )


def scan_kernel(bits, count, running_ref, before_ref, *refs):
    others = [ref[...].astype(F32) for ref in refs[:count]]
    new_before, packed, *new_running = refs[count:]
    running = running_ref[...] + sum(others)
    packed[...] = running.astype(BF16)
    for ref in new_running:
        ref[...] = running
    new_before[...] = before_ref[...] + earlier_sum(bits, others)


def spread_kernel(cores, bits, count, before_ref, *refs):
    others = [ref[...].astype(F32) for ref in refs[:count]]
    pieces, outs = refs[count : count + cores], refs[count + cores :]
    place = lax.axis_index("narrow")
    before = before_ref[...] + earlier_sum(bits, others)
    for k, out in enumerate(outs):
        receiver = (place + k) % cores
        value = before
        for j, piece in enumerate(pieces):
            source = (place - j + cores) % cores
            value = value + jnp.where(source < receiver, 1.0, 0.0) * piece[...].astype(F32)
        out[...] = value.astype(BF16)


def small_call(kernel, name, inputs, dtypes, shape):
    vmem = pl.BlockSpec(memory_space=pltpu.VMEM)
    smem = pl.BlockSpec(memory_space=pltpu.SMEM)
    return pl.pallas_call(
        kernel,
        in_specs=[smem if array.dtype == jnp.int32 else vmem for array in inputs],
        out_specs=[vmem] * len(dtypes),
        out_shape=[jax.ShapeDtypeStruct(shape, dtype) for dtype in dtypes],
        compiler_params=params(4 * 1024),
        name=name,
    )(*inputs)


def ones_blocks(width):
    rows, cols = (lax.broadcasted_iota(jnp.int32, (width, width), axis) for axis in range(2))
    return jnp.where(rows // HEAD == cols // HEAD, 1.0, 0.0).astype(BF16)


def block_state(state_ref, scratch):
    scratch[...] = jnp.zeros_like(scratch)
    for j in range(state_ref.shape[0]):
        scratch[head_cols(j), head_cols(j)] = state_ref[j]
    return scratch[...]


def norm_share(q, part, state, ones):
    attended = part + dot(q, state)
    squares = dot((attended * attended).astype(BF16), ones)
    return (attended * lax.rsqrt(squares * (1 / HEAD) + EPS)).astype(BF16)


def share_columns(cores, before):
    width = HEADS // cores * HEAD
    owner = (lax.axis_index("narrow") - before + cores) % cores
    return pl.ds(pl.multiple_of(owner * width, width), width)


def own_share_kernel(cores, state_ref, w_ref, *refs):
    pieces = len(refs) // 4
    qs, parts, direct, outs = (refs[i * pieces : (i + 1) * pieces] for i in range(4))
    scratch = refs[-1]
    cols = share_columns(cores, 0)
    state, ones = block_state(state_ref, scratch), ones_blocks(scratch.shape[0])
    for q, part, start, out in zip(qs, parts, direct, outs):
        normed = norm_share(q[:, cols], part[:, cols], state, ones)
        out[...] = start[...] + dot(normed, w_ref[cols, :])


def own_share(cores, state, weights, qs, parts, direct):
    width = HEADS // cores * HEAD
    vmem = pl.BlockSpec(memory_space=pltpu.VMEM)
    rows = sum(q.shape[0] for q in qs)
    return pl.pallas_call(
        functools.partial(own_share_kernel, cores),
        in_specs=[vmem] * (2 + 3 * len(qs)),
        out_specs=[vmem] * len(qs),
        out_shape=[jax.ShapeDtypeStruct(start.shape, F32) for start in direct],
        scratch_shapes=[pltpu.VMEM((width, width), BF16)],
        compiler_params=params(),
        cost_estimate=pl.CostEstimate(
            flops=6 * rows * width * width, bytes_accessed=rows * width * 8, transcendentals=0
        ),
        name="own_share",
    )(state, weights, *qs, *parts, *direct)


def list_rows(brick_ref, most, slots, fill):
    for i in range(slots.shape[0]):
        slots[i] = -1
    for b in range(fill.shape[0]):
        fill[b] = 0
    for r in range(brick_ref.shape[0]):
        brick = brick_ref[r] ^ lax.axis_index("wide")
        used = fill[brick]
        slots[brick * most + used] = r
        fill[brick] = used + 1


def cell_numbers(middle):
    number = lax.broadcasted_iota(jnp.int32, (BX * BY // 2, 1), 0)
    if middle:
        return number + 2 * BY
    return number + jnp.where(number < 2 * BY, 0, BX * BY // 2)


def cell_sums(brick, numbers, most, slots, cell_ref, features_ref):
    onehots, rows = [], []
    for j in range(most):
        row = slots[brick * most + j]
        at = jnp.maximum(row, 0)
        match = (numbers == cell_ref[at]) & (row >= 0)
        onehots.append(jnp.where(match, 1.0, 0.0).astype(BF16))
        rows.append(features_ref[pl.ds(pl.multiple_of(at * ROW, ROW), ROW), :])
    return dot(jnp.concatenate(onehots, axis=1), jnp.concatenate(rows, axis=0)).astype(BF16)


def pool_into(outs, brick_ref, cell_ref, features_ref, slots, fill):
    most = slots.shape[0] // fill.shape[0]
    list_rows(brick_ref, most, slots, fill)
    for bricks, middle, out in outs:
        numbers = cell_numbers(middle)
        for n, brick in enumerate(bricks):
            out[n] = cell_sums(brick, numbers, most, slots, cell_ref, features_ref)


def features_kernel(bricks, spans, cores, brick_ref, *refs):
    pieces = len(spans)
    refs = list(refs)
    take = lambda n: [refs.pop(0) for _ in range(n)]
    q_refs, part_refs, own_refs = (take(pieces) for _ in range(3))
    state_refs = take(cores - 1)
    w_ref, cell_ref, features_ref, out = take(4)
    scratch, slots, fill = refs
    shares = [share_columns(cores, k) for k in range(cores)]
    ones = ones_blocks(scratch.shape[1])
    states = [block_state(ref, scratch.at[k]) for k, ref in enumerate(state_refs)]
    for n, (first, count) in enumerate(spans):
        features = own_refs[n][...]
        for state, cols in zip(states, shares[1:]):
            normed = norm_share(q_refs[n][:, cols], part_refs[n][:, cols], state, ones)
            features += dot(normed, w_ref[cols, :])
        features_ref[first * BLK : (first + count) * BLK] = features.astype(BF16)
    pool_into([(bricks, False, out)], brick_ref, cell_ref, features_ref, slots, fill)


def list_scratch(count, most):
    return [pltpu.SMEM((count * most,), jnp.int32), pltpu.SMEM((count,), jnp.int32)]


def sums_shape(count, channels):
    return jax.ShapeDtypeStruct((count, BX * BY // 2, channels), BF16)


def voxel_features(
    spans, bricks, qs, parts, own, states, weights, cell_rows, chosen, count, most
):
    tokens, channels = sum(q.shape[0] for q in qs), weights.shape[1]
    cores = len(states) + 1
    width = HEADS // cores * HEAD
    vmem = pl.BlockSpec(memory_space=pltpu.VMEM)
    smem = pl.BlockSpec(memory_space=pltpu.SMEM)
    return pl.pallas_call(
        functools.partial(features_kernel, chosen, spans, cores),
        in_specs=[smem] + [vmem] * (3 * len(spans) + cores + 1),
        out_specs=[vmem] * 2,
        out_shape=[
            jax.ShapeDtypeStruct((tokens, channels), BF16),
            sums_shape(len(chosen), channels),
        ],
        scratch_shapes=[pltpu.VMEM((max(1, cores - 1), width, width), BF16)]
        + list_scratch(count, most),
        compiler_params=params(),
        name="voxel_features",
    )(bricks, *qs, *parts, *own, *states, weights, cell_rows)


def pool_kernel(chosen, brick_ref, cell_ref, features_ref, *refs):
    outs, (slots, fill) = refs[:-2], refs[-2:]
    pool_into(
        [(bricks, middle, out) for (bricks, middle), out in zip(chosen, outs)],
        brick_ref,
        cell_ref,
        features_ref,
        slots,
        fill,
    )


def pool(bricks, cell_rows, features, chosen, count, most):
    tokens, channels = features.shape
    vmem = pl.BlockSpec(memory_space=pltpu.VMEM)
    smem = pl.BlockSpec(memory_space=pltpu.SMEM)
    return pl.pallas_call(
        functools.partial(pool_kernel, chosen),
        in_specs=[smem, vmem, vmem],
        out_specs=[vmem] * len(chosen),
        out_shape=[sums_shape(len(which), channels) for which, _ in chosen],
        scratch_shapes=list_scratch(count, most),
        compiler_params=params(),
        cost_estimate=pl.CostEstimate(
            flops=sum(len(which) for which, _ in chosen) * most * ROW * BX * BY * channels,
            bytes_accessed=tokens * channels * 2,
            transcendentals=0,
        ),
        name="pool",
    )(bricks, cell_rows, features)


def convolve(field, w_ref, start, count):
    lhs = jnp.concatenate(
        [field[start + dy * LINE : start + dy * LINE + count] for dy in (-1, 0, 1)], axis=1
    )
    left, middle, right = weighted(lhs, w_ref)
    return pltpu.roll(left, 1, 0) + middle + pltpu.roll(right, count - 1, 0)


def weighted(lhs, w_ref):
    return [
        dot(lhs, jnp.concatenate([w_ref[dy, dx] for dy in range(3)], axis=0)) for dx in range(3)
    ]


def own_columns_kernel(lines_ref, w_ref, out_ref, field):
    lines = lines_ref.shape[0]
    for r in range(lines):
        field[r * LINE : r * LINE + GAP] = jnp.zeros((GAP, field.shape[1]), BF16)
        field[r * LINE + GAP : (r + 1) * LINE] = lines_ref[r]
    field[lines * LINE :] = jnp.zeros((GAP, field.shape[1]), BF16)
    out_ref[...] = convolve(field, w_ref, LINE, out_ref.shape[0])


def own_columns(lines, conv_first):
    count, _, channels = lines.shape
    vmem = pl.BlockSpec(memory_space=pltpu.VMEM)
    shown = (count - 2) * LINE + GAP
    return pl.pallas_call(
        own_columns_kernel,
        in_specs=[vmem] * 2,
        out_specs=vmem,
        out_shape=jax.ShapeDtypeStruct((shown, channels), F32),
        scratch_shapes=[pltpu.VMEM((count * LINE + GAP, channels), BF16)],
        compiler_params=params(16 * 1024),
        cost_estimate=pl.CostEstimate(
            flops=18 * shown * channels * channels,
            bytes_accessed=shown * channels * 8,
            transcendentals=0,
        ),
        name="own_columns",
    )(lines, conv_first)


def field_kernel(first_ref, sides_ref, w1_ref, w2_ref, out_ref, first, field, flow, sems):
    count, channels = first.shape
    wide, narrow = lax.axis_index("wide"), lax.axis_index("narrow")
    first_line, last_line = wide == 0, wide == lax.axis_size("wide") - 1
    first_column, last_column = narrow == 0, narrow == lax.axis_size("narrow") - 1
    gaps = sides_ref.shape[0] - 2
    sides = sides_ref[...].reshape((gaps + 2) * GAP, channels)
    lhs = jnp.concatenate([sides[dy * GAP : (dy + gaps) * GAP] for dy in range(3)], axis=1)
    none = jnp.zeros((8, channels), F32)
    left, middle, right = [
        jnp.concatenate(
            [part for g in range(gaps) for part in (none, given[g * GAP : (g + 1) * GAP], none)],
            axis=0,
        )
        for given in weighted(lhs, w1_ref)
    ]
    span = GAP + 16
    added = pltpu.roll(left, 1, 0) + middle + pltpu.roll(right, gaps * span - 1, 0)
    first[...] = first_ref[...]
    for g in range(gaps):
        start, stop = max(g * LINE - 8, 0), min(g * LINE + GAP + 8, count)
        at = g * span + 8 - g * LINE
        first[start:stop] += added[start + at : stop + at]
    inner = jax.nn.gelu(first[...], approximate=True)
    at = lax.broadcasted_iota(jnp.int32, (count, 1), 0)
    outside = first_line & (at <= LINE) | last_line & (at > (BX + 1) * LINE)
    for r in range(BX + 2):
        outside |= first_column & (at == r * LINE + GAP - 1)
        outside |= last_column & (at == (r + 1) * LINE)
    field[...] = jnp.where(outside, 0.0, inner).astype(BF16)
    half = BX // 2
    copies = []
    for n in range(2):
        given = convolve(field, w2_ref, (1 + n * half) * LINE, half * LINE + GAP)
        for r in range(half):
            flow[n * half + r] = given[r * LINE + GAP : (r + 1) * LINE]
        lines = pl.ds(n * half, half)
        copies.append(pltpu.make_async_copy(flow.at[lines], out_ref.at[lines], sems.at[n]))
        copies[-1].start()
    for copy in copies:
        copy.wait()


def field_flow(first, left, right, conv_first, conv_second):
    count, channels = first.shape
    vmem = pl.BlockSpec(memory_space=pltpu.VMEM)
    sides = jnp.pad(right, ((1, 0), (0, GAP - 2), (0, 0))) + jnp.pad(
        left, ((0, 1), (GAP - 2, 0), (0, 0))
    )
    return pl.pallas_call(
        field_kernel,
        in_specs=[vmem] * 4,
        out_specs=pl.BlockSpec(memory_space=pl.ANY),
        out_shape=jax.ShapeDtypeStruct((BX, BY, channels), F32),
        scratch_shapes=[
            pltpu.VMEM((count, channels), F32),
            pltpu.VMEM((count, channels), BF16),
            pltpu.VMEM((BX, BY, channels), F32),
            pltpu.SemaphoreType.DMA((2,)),
        ],
        compiler_params=params(16 * 1024),
        name="field_flow",
    )(first, sides, conv_first, conv_second)


def swap(array, axis, bit):
    count = lax.axis_size(axis)
    return lax.ppermute(array, axis, [(i, i ^ (1 << bit)) for i in range(count)])


def swap_digit(array, axis, bit, by):
    count = lax.axis_size(axis)
    return lax.ppermute(array, axis, [(i, i ^ (by << bit)) for i in range(count)])


def shift(array, axis, by):
    count = lax.axis_size(axis)
    return lax.ppermute(
        array, axis, [(i, i + by) for i in range(count) if 0 <= i + by < count]
    )


def rotate(array, axis, by):
    count = lax.axis_size(axis)
    return lax.ppermute(array, axis, [(i, (i + by) % count) for i in range(count)])


def side_columns(lines):
    if lax.axis_size("narrow") != 2:
        return shift(lines[:, BY - 2 :], "narrow", 1), shift(lines[:, :2], "narrow", -1)
    first = lax.axis_index("narrow") == 0
    other = swap(jnp.where(first, lines[:, BY - 2 :], lines[:, :2]), "narrow", 0)
    nothing = jnp.zeros_like(other)
    return jnp.where(first, nothing, other), jnp.where(first, other, nothing)


def exchange_lines(strip, with_it):
    groups, count, cores = (lax.axis_size(axis) for axis in ("group", "wide", "narrow"))
    place = lax.axis_index("wide")
    got = []
    for start in range(2):
        pairs = []
        for g in range(groups):
            for w in range(count):
                other = w + 1 if w % 2 == start else w - 1
                far = g
                if not 0 <= other < count:
                    other, far = w, g ^ 1 if groups % 2 == 0 else g
                for c in range(cores):
                    pairs.append(((g * count + w) * cores + c, (far * count + other) * cores + c))
        upper = place % 2 == start
        out = jnp.where(upper, strip[2:], strip[:2])
        got.append(lax.ppermute(out, ("group", "wide", "narrow"), pairs))
    got, with_it = lax.optimization_barrier((got, with_it))
    above = jnp.where(place % 2 == 1, got[0], got[1])
    below = jnp.where(place % 2 == 1, got[1], got[0])
    above = jnp.where(place > 0, above, jnp.zeros_like(above))
    below = jnp.where(place < count - 1, below, jnp.zeros_like(below))
    return above, below, with_it


def earlier_state(totals, first_work, works):
    cores, shape = len(totals), totals[0].shape
    works, done = list(works), []

    def beside(work, arrays, exchange):
        held, arrays = work(arrays)
        done.append(held)
        held, arrived = lax.optimization_barrier((held, exchange(arrays)))
        done[-1] = held
        return arrived

    others = beside(
        first_work,
        totals[1:],
        lambda arrays: [rotate(array, "narrow", k + 1) for k, array in enumerate(arrays)],
    )
    pieces = [totals[0]] + others
    running, packed = small_call(gather_kernel, "gather", pieces, [F32, BF16], shape)
    before = jnp.zeros(shape, F32)
    count = lax.axis_size("wide").bit_length() - 1
    levels = [list(range(bit, min(bit + 2, count))) for bit in range(0, count, 2)]
    for level, bits in enumerate(levels):
        exchange = lambda packed: [
            swap_digit(packed, "wide", bits[0], k) for k in range(1, 1 << len(bits))
        ]
        others = beside(works.pop(0), packed, exchange) if works else exchange(packed)
        if level == len(levels) - 1:
            break
        before, packed, *more = small_call(
            functools.partial(scan_kernel, bits, len(others)),
            "scan",
            [running, before] + others,
            [F32, BF16] + [F32] * (level < len(levels) - 2),
            shape,
        )
        running = more[0] if more else None
    outs = small_call(
        functools.partial(spread_kernel, cores, bits, len(others)),
        "spread",
        [before] + others + pieces,
        [BF16] * cores,
        shape,
    )
    states = [outs[0]] + [rotate(outs[k], "narrow", k) for k in range(1, cores)]
    while works:
        done.append(works.pop(0)(outs[0])[0])
    return states, done


def split_order(order):
    half = 1 << (len(order) - 1)
    place = lambda slot: sum(
        ((slot >> (len(order) - 1 - i)) & 1) << bit for i, bit in enumerate(order)
    )
    return [place(slot) for slot in range(half)], [place(slot) for slot in range(half, 2 * half)]


def reduce_level(stays, goes, bit, with_it=None):
    arrived = [swap(array, "wide", bit) for array in reversed(goes)][::-1]
    if with_it is not None:
        arrived, with_it = lax.optimization_barrier((arrived, with_it))
    sums = [
        (here.astype(F32) + more.astype(F32)).astype(BF16) for here, more in zip(stays, arrived)
    ]
    return sums, with_it


def next_level(sums):
    if len(sums) == 1:
        half = sums[0].shape[0] // 2
        return [sums[0][:half]], [sums[0][half:]]
    return sums[:1], sums[1:]


def reduce_both(outer, middle, orders):
    levels = len(orders[0])
    outer_sums, _ = reduce_level(*outer, orders[0][0])
    stays, (later, first) = middle
    later, outer_sums[-1] = lax.optimization_barrier((later, outer_sums[-1]))
    middle = stays, [later, first]
    outer = next_level(outer_sums)
    for level in range(1, levels):
        middle_sums, _ = reduce_level(*middle, orders[1][level - 1])
        middle = next_level(middle_sums)
        if level > 1:
            outer_sums, middle = reduce_level(*outer, orders[0][level], middle)
        else:
            outer_sums, _ = reduce_level(*outer, orders[0][level])
        outer = next_level(outer_sums)
    return outer_sums[0][0], reduce_level(*middle, orders[1][-1])[0][0][0]


def per_device(voxels, w_qkv, w_out, w_feature, conv_first, conv_second, row_brick, cell_place):
    tokens = voxels.shape[0]
    channels = w_feature.shape[1]
    wide_count, wide_place = lax.axis_size("wide"), lax.axis_index("wide")
    narrow_count, narrow_place = lax.axis_size("narrow"), lax.axis_index("narrow")

    blocks = tokens // BLK
    cuts = sorted({blocks * i // 2 for i in range(3)})
    spans = [(first, last - first) for first, last in zip(cuts, cuts[1:])]
    xs, ws, totals = device_totals(spans, voxels, w_qkv, narrow_count)

    def direct(arrays):
        arrays, x = lax.optimization_barrier((arrays, xs[0]))
        return direct_features([x] + xs[1:], w_out, w_feature), arrays

    after = [None]

    def work(n):
        def run(array):
            array, x = lax.optimization_barrier((array, xs[n]))
            piece = local_attention(x, ws, after[-1], n == len(spans) - 1)
            after.append(piece[-1])
            return piece, array

        return run

    states, done = earlier_state(totals, direct, [work(n) for n in range(len(spans))])
    own, weights = done[0][:-1], done[0][-1]
    qs, parts = ([piece[i] for piece in done[1:]] for i in range(2))
    own = own_share(narrow_count, states[0], weights, qs, parts, own)

    bits = list(range(wide_count.bit_length() - 1))
    orders = [bits, bits[1::-1] + bits[2:]]
    halves = lambda places: (places[: len(places) // 2], places[len(places) // 2 :])
    stay, go = zip(*(map(halves, split_order(order)) for order in orders))
    cell_rows = cell_place.reshape(-1, 1, ROW)
    most = max(2, 2 * (tokens // ROW) // wide_count)
    bricks = row_brick[:, 0]
    features, outer_first = voxel_features(
        spans, bricks, qs, parts, own, states[1:], weights, cell_rows, go[0][1], wide_count, most
    )
    pooled = lambda *chosen: pool(bricks, cell_rows, features, chosen, wide_count, most)
    middle_first, outer_later, middle_later, *sums = pooled(
        (go[1][1], True),
        (go[0][0], False),
        (go[1][0], True),
        *((stay[middle][n], middle == 1) for middle in range(2) for n in range(2)),
    )
    outer, middle = reduce_both(
        (sums[:2], [outer_later, outer_first]), (sums[2:], [middle_later, middle_first]), orders
    )
    outer, middle = (part.reshape(-1, BY, channels) for part in (outer, middle))
    above, below, middle = exchange_lines(outer, middle)
    lines = jnp.concatenate([above, outer[:2], middle, outer[2:], below], axis=0)
    left, right = side_columns(lines)
    return field_flow(own_columns(lines, conv_first), left, right, conv_first, conv_second)


def solution(mesh):
    placed = (
        P(("group", "wide", "narrow"), None),
        P(),
        P(),
        P(),
        P(),
        P(),
        P(("group", "wide", "narrow"), None),
        P(("group", "wide", "narrow")),
    )
    return jax.shard_map(
        per_device,
        mesh=mesh,
        in_specs=placed,
        out_specs=P(("group", "wide"), "narrow", None),
        check_vma=False,
    )
```
